256 devices in a mesh: dp: 64 (over x, y, z_lo, core), pipe: 4 (over z_hi).
Axes of the slice: x: 4, y: 4, z: 8 (z_hi: 4, z_lo: 2; z = z_hi * 2 + z_lo), core: 2. Of those that a mesh axis runs over, the one named last changes fastest.
Arguments:
- saved_inputs: bfloat16 [4, 4, 8192, 5120], P('pipe', None, 'dp'), may hold values from -6 to 6
- cotangent: bfloat16 [4, 8192, 5120], P(None, 'dp'), may hold values from -16 to 16
- adapter_down: bfloat16 [4, 5120, 256], P('pipe', 'dp'), may hold values from -0.078125 to 0.078125
- adapter_up: bfloat16 [4, 256, 5120], P('pipe', None, 'dp'), may hold values from -0.375 to 0.375
- image_rows: int32 [4, 4096], P(None, 'dp'), may hold values from 0 to 127, as said below
Outputs:
- down_grad: float32 [4, 5120, 256], P('pipe', 'dp')
- up_grad: float32 [4, 256, 5120], P('pipe', None, 'dp')
- feature_grads: bfloat16 [3, 4, 4096, 5120], P(None, None, 'dp', 'pipe')
The draws below stay inside these ranges and needn't reach their ends.
Inputs may be any that keep to these rules, and one draw needn't show every extreme that they name: `image_rows`: each block of 64 entries of a row (the image tokens of one micro-batch on one device) holds distinct positions among that device's 128 tokens, ascending.
All inputs are finite; a program needn't handle non-finite values.
Results may differ from the reference program's by a relative error of at most 0.009.
Values may be sent and summed in bfloat16 or wider, within the bound.
No kernel may reach another device: no remote copies, remote signals or barrier semaphores. Data moves between devices by JAX's collectives and lax.ppermute only.
A program may use at most 128 MiB of HBM per device.

```python
import jax
import jax.numpy as jnp
from jax import lax

D = 5120
R = 256
MICRO = 4
LEVELS = 3
TOK_DEV = 128
IMG_DEV = 64
TOKENS = 8192
IMG_TOTAL = 4096
LAYERS = 4


def draw_image_rows(key, part):
    key = jax.random.fold_in(key, 7)
    blocks_dp = TOKENS // TOK_DEV
    raw = jax.random.randint(key, (MICRO, blocks_dp, TOK_DEV), 0, 1 << 20)
    scores = raw * TOK_DEV + jnp.arange(TOK_DEV, dtype=jnp.int32)
    order = jnp.argsort(scores, axis=-1, stable=True).astype(jnp.int32)
    chosen = jnp.sort(order[:, :, :IMG_DEV], axis=-1)
    return chosen.reshape(MICRO, blocks_dp * IMG_DEV).astype(jnp.int32)


def raised(values, own_key, source, target, shards_of, factor):
    def block_of(dim):
        return (jnp.arange(values.shape[dim]) // (values.shape[dim] // shards_of)).reshape((-1,) + (1,) * (values.ndim - 1 - dim))

    one_side = jax.random.permutation(own_key, shards_of)[block_of(target)]
    second = (block_of(target) + shards_of // 2) % shards_of
    return jnp.where((block_of(source) == one_side) | (block_of(source) == second), factor * values, values)


def steps_of(own_key, extent, split, smallest, high):
    level = 1.0
    for position, parts in split:
        steps = jax.random.uniform(jax.random.fold_in(jax.random.fold_in(own_key, 6), position), (parts,), jnp.float32, smallest / len(split), high / len(split))
        level = level * jnp.repeat(jnp.exp(steps), extent[position] // parts).reshape((-1,) + (1,) * (len(extent) - 1 - position))
    return level


def centred(own_key, dims, width, most, split=(), held_as=jnp.bfloat16):
    loudness = steps_of(own_key, dims, split, -0.22, 0.18) if split else 1.0
    entries = jax.random.normal(own_key, dims, jnp.float32) * width * loudness
    return jnp.minimum(jnp.maximum(entries, -most), most).astype(held_as)


def heavy_noise(rng, extent, spread, limit, pieces, heavy, held_as=jnp.bfloat16):
    entries = spread * jax.random.normal(rng, extent, jnp.float32)
    if pieces:
        entries = entries * steps_of(rng, extent, pieces, -0.22, 0.18)
    return jnp.clip(raised(entries, jax.random.fold_in(rng, 3), *heavy), -limit, limit).astype(held_as)


def setup_inputs(seed: int = 0) -> dict:
    key_list = jax.random.split(jax.random.key(seed), 6)
    return {
        "saved_inputs": centred(key_list[0], (LAYERS, MICRO, TOKENS, D), 1.0, 6.0, ((0, 4), (2, 64))),
        "cotangent": heavy_noise(key_list[1], (MICRO, TOKENS, D), 1.0, 16.0, ((1, 64),), (1, 2, 64, 4.0)),
        "adapter_down": centred(key_list[2], (LAYERS, D, R), D ** -0.5, 0.078125, ((0, 4), (1, 64))),
        "adapter_up": centred(key_list[3], (LAYERS, R, D), R ** -0.5, 0.375, ((0, 4), (2, 64))),
        "image_rows": draw_image_rows(jax.random.fold_in(key_list[5], 71), 0),
    }


def silu_slope(pre):
    sigma = jax.nn.sigmoid(pre)
    return sigma * (1.0 + pre * (1.0 - sigma))

def layer_back(hidden_in, grad_out, weights_down, weights_up):
    hidden = hidden_in.astype(jnp.float32)
    inverse_rms = lax.rsqrt(lax.optimization_barrier(jnp.mean(hidden * hidden, axis=-1, keepdims=True)) + 1e-06)
    normed = hidden * inverse_rms
    normed_b = normed.astype(jnp.bfloat16)
    pre = jnp.dot(normed_b, weights_down, preferred_element_type=jnp.float32)
    act = jax.nn.silu(pre).astype(jnp.bfloat16)
    back_act = jnp.dot(grad_out, weights_up.T, preferred_element_type=jnp.float32)
    back_pre = (back_act * silu_slope(pre)).astype(jnp.bfloat16)
    back_norm = jnp.dot(back_pre, weights_down.T, preferred_element_type=jnp.float32)
    along = lax.optimization_barrier(jnp.mean(back_norm * normed, axis=-1, keepdims=True))
    grad_in = grad_out.astype(jnp.float32) + inverse_rms * (back_norm - normed * along)
    down_term = jnp.dot(normed_b.T, back_pre, preferred_element_type=jnp.float32)
    up_term = jnp.dot(act.T, grad_out, preferred_element_type=jnp.float32)
    return (grad_in.astype(jnp.bfloat16), down_term, up_term)

def reference(saved_inputs, cotangent, adapter_down, adapter_up, image_rows):
    blocks = jnp.arange(IMG_TOTAL, dtype=jnp.int32) // IMG_DEV
    positions = (blocks[None, :] * TOK_DEV + image_rows).astype(jnp.int32)
    factor = (MICRO * TOKENS) ** (-0.5)
    gradients = cotangent
    down_list = []
    up_list = []
    feature_list = []
    for layer in range(LAYERS - 1, -1, -1):
        if layer < LEVELS:
            feature_list.insert(0, jnp.stack([gradients[micro_slot][positions[micro_slot]] for micro_slot in range(MICRO)]))
        down_total = jnp.zeros((D, R), jnp.float32)
        up_total = jnp.zeros((R, D), jnp.float32)
        new_grads = []
        for micro_slot in range(MICRO):
            grad_in, down_term, up_term = layer_back(saved_inputs[layer, micro_slot], gradients[micro_slot], adapter_down[layer], adapter_up[layer])
            new_grads.append(grad_in)
            down_total = down_total + down_term
            up_total = up_total + up_term
        gradients = jnp.stack(new_grads)
        down_list.insert(0, down_total * factor)
        up_list.insert(0, up_total * factor)
    return (jnp.stack(down_list), jnp.stack(up_list), jnp.stack(feature_list))
```

```python
import jax
import jax.numpy as jnp
from jax import lax
from jax.sharding import PartitionSpec as P

LEVELS = 3
SIDE = 4
SECTIONS = 4
AXES = ("dp", "pipe")
BF = jnp.bfloat16
F32 = jnp.float32


def route(target):
    pairs = []
    for x in range(SIDE):
        for y in range(SIDE):
            for z in range(2):
                for c in range(2):
                    for s in range(SECTIONS):
                        to = target(x, y, z, c, s)
                        if to is None:
                            continue
                        tx, ty, tz, tc, ts = to
                        source = (((x * SIDE + y) * 2 + z) * 2 + c) * SECTIONS + s
                        dest = (((tx * SIDE + ty) * 2 + tz) * 2 + tc) * SECTIONS + ts
                        pairs.append((source, dest))
    return pairs


def send(block, target):
    return lax.ppermute(block, AXES, route(target))


def mate_z(x, y, z, c, s):
    return (x, y, 1 - z, c, s)


def mate_core(x, y, z, c, s):
    return (x, y, z, 1 - c, s)


def mate_x(mask):
    def target(x, y, z, c, s):
        return (((((x + c) % SIDE) ^ mask) - c) % SIDE, y, z, c, s)

    return target


def mate_y(mask):
    def target(x, y, z, c, s):
        return (x, ((((y + c) % SIDE) ^ mask) - c) % SIDE, z, c, s)

    return target


def shifted(distance, only=None):
    def target(x, y, z, c, s):
        if only is not None and s != only:
            return None
        if not 0 <= s + distance < SECTIONS:
            return None
        return (x, y, z, c, s + distance)

    return target


def turned(distance):
    def target(x, y, z, c, s):
        if s == 0:
            return None
        return (x, y, z, c, (s + distance) % SECTIONS)

    return target


def both(mine, theirs, bit, axis):
    low = jnp.where(bit == 0, mine, theirs)
    high = jnp.where(bit == 0, theirs, mine)
    return jnp.concatenate([low, high], axis=axis)


def place():
    index = lax.axis_index("dp")
    core = index % 2
    z = (index // 2) % 2
    y = (index // 4) % SIDE
    x = index // (4 * SIDE)
    return x, y, z, core


def gather_shards(shard):
    x, y, z, core = place()
    xs = (x + core) % SIDE
    ys = (y + core) % SIDE
    other = send(shard, mate_z)
    blocks = [jnp.where(z == 0, shard, other), jnp.where(z == 0, other, shard)]
    halves = []
    for color, block in enumerate(blocks):
        first, second = ((xs, mate_x), (ys, mate_y)) if color == 0 else ((ys, mate_y), (xs, mate_x))
        now = block[None, None]
        for axis, (label, mate) in ((1, first), (0, second)):
            now = both(now, send(now, mate(1)), label % 2, axis)
            now = both(now, send(now, mate(3)), label // 2, axis)
        if color == 0:
            now = now.transpose(1, 0, 2, 3)
        halves.append(now)
    own = jnp.stack(halves, axis=2)
    sibling = send(own, mate_core)
    zero = jnp.where(core == 0, own, sibling)
    one = jnp.where(core == 0, sibling, own)
    one = jnp.roll(one, (-1, -1), (0, 1))
    return jnp.stack([zero, one], axis=3)


def halve(now, label, mate, axis):
    for mask, bit, size in ((3, label // 2, 2), (1, label % 2, 1)):
        kept = lax.dynamic_slice_in_dim(now, bit * size, size, axis)
        away = lax.dynamic_slice_in_dim(now, (1 - bit) * size, size, axis)
        came = send(away, mate(mask))
        now = (kept.astype(F32) + came.astype(F32)).astype(BF)
    return now


def scatter_sum(total):
    x, y, z, core = place()
    xs = (x + core) % SIDE
    ys = (y + core) % SIDE
    cols = total.shape[1]
    total = total.reshape(SIDE, SIDE, 2, 2, -1, cols)
    zero = total[:, :, :, 0]
    one = jnp.roll(total[:, :, :, 1], (1, 1), (0, 1))
    kept = jnp.where(core == 0, zero, one)
    came = send(jnp.where(core == 0, one, zero), mate_core)
    chip = (kept.astype(F32) + came.astype(F32)).astype(BF)
    parts = []
    for color in range(2):
        now = chip[:, :, color]
        if color == 0:
            now = halve(now, xs, mate_x, 0)
            now = halve(now, ys, mate_y, 1)
        else:
            now = halve(now, ys, mate_y, 1)
            now = halve(now, xs, mate_x, 0)
        parts.append(now[0, 0])
    mine = jnp.where(z == 0, parts[0], parts[1])
    away = jnp.where(z == 0, parts[1], parts[0])
    return mine.astype(F32) + send(away, mate_z).astype(F32)


def dot(a, b, contract):
    return lax.dot_general(a, b, ((contract[0], contract[1]), ((), ())), preferred_element_type=F32)


def on_device(saved_inputs, cotangent, adapter_down, adapter_up, image_rows):
    section = lax.axis_index("pipe")
    micro, tokens, width = cotangent.shape
    rank = adapter_down.shape[2]
    count = micro * tokens
    factor = (count * lax.axis_size("dp")) ** (-0.5)
    hidden = saved_inputs.reshape(count, width)
    cot = cotangent.reshape(count, width)

    up_shard = adapter_up[0].T
    extra = [send(up_shard, shifted(d)) for d in (1, 2, 3)]
    weights = gather_shards(jnp.concatenate([adapter_down[0]] + extra + [up_shard], axis=1))
    weights = weights.reshape(width, 5 * rank)
    down = weights[:, :rank]

    hf = hidden.astype(F32)
    inverse = lax.rsqrt(jnp.mean(hf * hf, axis=-1, keepdims=True) + 1e-06)
    products = dot(hidden, weights[:, : 4 * rank], ((1,), (0,)))
    pre = inverse * products[:, :rank]
    cross = products[:, rank:]
    back = dot(cot, weights[:, 4 * rank :], ((1,), (0,)))
    mixed = dot(down, weights[:, rank : 4 * rank], ((0,), (0,))).astype(BF)
    sigma = jax.nn.sigmoid(pre)
    act = (pre * sigma).astype(BF)
    slope = sigma * (1.0 + pre * (1.0 - sigma))
    acts = jnp.concatenate([send(act, shifted(d)) for d in (1, 2, 3)], axis=1)

    def local(back):
        back_pre = (back * slope).astype(BF)
        wide = back_pre.astype(F32)
        along = jnp.sum(wide * pre, axis=-1, keepdims=True) / width
        return back_pre, wide * inverse, along * inverse * inverse

    def columns(back, levels):
        _, scaled, pull = local(back)
        scaled = scaled.astype(BF)
        right = acts[:, : levels * rank]
        joint = dot(scaled, right, ((0,), (0,))).astype(BF)
        pulled = (-pull * right.astype(F32)).astype(BF)
        whole = dot(hidden, jnp.concatenate([scaled, pulled], axis=1), ((0,), (0,)))
        inner = dot(down, joint, ((1,), (0,)))
        return jnp.concatenate([whole[:, :rank], whole[:, rank:] + inner], axis=1).astype(BF)

    early = None
    for s in (3, 2, 1):
        back_pre, scaled, pull = local(back)
        if s == 3:
            own_up = dot(cot, act, ((0,), (0,))).astype(BF)
            early = scatter_sum(jnp.concatenate([own_up, columns(back, 3)], axis=1))
        pushed = dot(back_pre, mixed[:, : s * rank], ((1,), (0,)))
        pushed = (inverse * pushed - pull * cross[:, : s * rank]).astype(BF)
        for d in range(1, s + 1):
            came = send(pushed[:, (d - 1) * rank : d * rank], shifted(-d, s))
            back = back + came.astype(F32)
    late = scatter_sum(columns(back, 2))

    back_pre, scaled, pull = local(back)
    picks = (image_rows[:, :, None] == jnp.arange(tokens, dtype=jnp.int32)).astype(BF)

    def rows_of(array):
        array = array.reshape(micro, tokens, -1)
        out = lax.dot_general(picks, array, (((2,), (1,)), ((0,), (0,))), preferred_element_type=F32)
        return out.reshape(-1, out.shape[-1])

    def rows_exact(column):
        index = (image_rows + jnp.arange(micro, dtype=jnp.int32)[:, None] * tokens).reshape(-1)
        return jnp.take(column, index, axis=0)

    picked = rows_of(scaled.astype(BF)).astype(BF)
    moved = dot(picked, down, ((1,), (1,))) - rows_exact(pull) * rows_of(hidden)
    part = width // SECTIONS
    moved = moved.astype(BF)
    mine = rows_of(lax.dynamic_slice_in_dim(cot, section * part, part, 1))
    feature = [mine, mine, mine]
    for turn in range(SECTIONS):
        goal = (section + turn) % SECTIONS
        block = lax.dynamic_slice_in_dim(moved, goal * part, part, 1)
        origin = (section - turn) % SECTIONS
        if turn:
            block = send(block, turned(turn))
        for level in range(LEVELS):
            feature[level] = feature[level] + jnp.where(origin > level, block.astype(F32), 0.0)
    feature_grads = jnp.stack(feature).astype(BF).reshape(LEVELS, micro, -1, part)

    sums = jnp.where(section == 3, early[:, rank : 4 * rank], late)
    down_grad = (sums[:, :rank] * factor)[None]
    up_sum = early[:, :rank]
    for d, piece in ((1, sums[:, rank : 2 * rank]), (2, sums[:, 2 * rank :]), (3, early[:, 4 * rank :])):
        up_sum = up_sum + send(piece, shifted(-d))
    up_grad = (up_sum.T * factor)[None]
    return (down_grad, up_grad, feature_grads)


def solution(mesh):
    placed = (
        P("pipe", None, "dp", None),
        P(None, "dp", None),
        P("pipe", "dp", None),
        P("pipe", None, "dp"),
        P(None, "dp"),
    )
    return jax.shard_map(
        on_device,
        mesh=mesh,
        in_specs=placed,
        out_specs=(P("pipe", "dp", None), P("pipe", None, "dp"), P(None, None, "dp", "pipe")),
        check_vma=False,
    )
```

```python
import jax
import jax.numpy as jnp
from jax import lax
from jax.experimental import pallas as pl
from jax.experimental.pallas import tpu as pltpu
from jax.sharding import PartitionSpec as P

LEVELS = 3
SIDE = 4
SECTIONS = 4
AXES = ("dp", "pipe")
BF = jnp.bfloat16
F32 = jnp.float32
VMEM_BYTES = 48 * 1024 * 1024
barrier = lax.optimization_barrier


def route(target):
    pairs = []
    for x in range(SIDE):
        for y in range(SIDE):
            for z in range(2):
                for c in range(2):
                    for s in range(SECTIONS):
                        to = target(x, y, z, c, s)
                        if to is None:
                            continue
                        tx, ty, tz, tc, ts = to
                        source = (((x * SIDE + y) * 2 + z) * 2 + c) * SECTIONS + s
                        dest = (((tx * SIDE + ty) * 2 + tz) * 2 + tc) * SECTIONS + ts
                        pairs.append((source, dest))
    return pairs


def send(block, target):
    return lax.ppermute(block, AXES, route(target))


def mate_z(x, y, z, c, s):
    return (x, y, 1 - z, c, s)


def mate_core(x, y, z, c, s):
    return (x, y, z, 1 - c, s)


def mate_x(mask):
    def target(x, y, z, c, s):
        return (((((x + c) % SIDE) ^ mask) - c) % SIDE, y, z, c, s)

    return target


def mate_y(mask):
    def target(x, y, z, c, s):
        return (x, ((((y + c) % SIDE) ^ mask) - c) % SIDE, z, c, s)

    return target


def shifted(distance, only=None):
    def target(x, y, z, c, s):
        if only is not None and s != only:
            return None
        if not 0 <= s + distance < SECTIONS:
            return None
        return (x, y, z, c, s + distance)

    return target


def turned(distance):
    def target(x, y, z, c, s):
        if s == 0:
            return None
        return (x, y, z, c, (s + distance) % SECTIONS)

    return target


def both(mine, theirs, bit, axis):
    low = jnp.where(bit == 0, mine, theirs)
    high = jnp.where(bit == 0, theirs, mine)
    return jnp.concatenate([low, high], axis=axis)


def place():
    index = lax.axis_index("dp")
    core = index % 2
    z = (index // 2) % 2
    y = (index // 4) % SIDE
    x = index // (4 * SIDE)
    return x, y, z, core


def gather_ring(shard):
    x, y, z, core = place()
    xs = (x + core) % SIDE
    ys = (y + core) % SIDE
    other = send(shard, mate_z)
    blocks = [jnp.where(z == 0, shard, other), jnp.where(z == 0, other, shard)]
    halves = []
    for color, block in enumerate(blocks):
        first, second = ((xs, mate_x), (ys, mate_y)) if color == 0 else ((ys, mate_y), (xs, mate_x))
        now = block[None, None]
        for axis, (label, mate) in ((1, first), (0, second)):
            now = both(now, send(now, mate(1)), label % 2, axis)
            now = both(now, send(now, mate(3)), label // 2, axis)
        halves.append(now)
    return halves


def gather_cores(halves):
    core = lax.axis_index("dp") % 2
    siblings = [send(half, mate_core) for half in halves]
    pieces = []
    for color, (own, sibling) in enumerate(zip(halves, siblings)):
        zero = jnp.where(core == 0, own, sibling)
        one = jnp.where(core == 0, sibling, own)
        one = jnp.roll(one, (-1, -1), (0, 1))
        pair = jnp.stack([zero, one], axis=2)
        if color == 0:
            pair = pair.transpose(1, 0, 2, 3, 4)
        pieces.append(pair)
    whole = jnp.stack(pieces, axis=2)
    return whole.reshape(-1, whole.shape[-1])


def halve(now, label, mate, axis):
    for mask, bit, size in ((3, label // 2, 2), (1, label % 2, 1)):
        kept = lax.dynamic_slice_in_dim(now, bit * size, size, axis)
        away = lax.dynamic_slice_in_dim(now, (1 - bit) * size, size, axis)
        came = send(away.astype(BF), mate(mask))
        now = kept.astype(F32) + came.astype(F32)
    return now


def add_cores(kept, away):
    return (kept.astype(F32) + send(away, mate_core).astype(F32)).astype(BF)


def scatter_ring(chip):
    x, y, z, core = place()
    xs = (x + core) % SIDE
    ys = (y + core) % SIDE
    first = halve(halve(chip[0], xs, mate_x, 0), ys, mate_y, 1)[0, 0]
    second = halve(halve(chip[1], ys, mate_y, 1), xs, mate_x, 0)[0, 0]
    mine = jnp.where(z == 0, first, second)
    away = jnp.where(z == 0, second, first)
    return mine + send(away.astype(BF), mate_z).astype(F32)


def product_kernel(rank, with_up, core_ref, hidden_ref, right_ref, down_ref, joint_ref, *rest):
    if with_up:
        cot_ref, act_ref, kept_ref, away_ref = rest
    else:
        kept_ref, away_ref = rest
    core = core_ref[0]
    rows = kept_ref.shape[3]
    chunk = 8 * rows
    base = rank if with_up else 0
    for half in range(2):
        span = pl.ds(half * chunk, chunk)
        main = dot(hidden_ref[:, span], right_ref[...], ((0,), (0,)))
        inner = dot(down_ref[span, :], joint_ref[...], ((1,), (0,)))
        parts = [(base, main[:, :rank]), (base + rank, main[:, rank:] + inner)]
        if with_up:
            parts.append((0, dot(cot_ref[:, span], act_ref[...], ((0,), (0,)))))
        parts = [(start, part.astype(BF)) for start, part in parts]

        def store(targets):
            for y2 in range(2):
                for z in range(2):
                    for c in range(2):
                        low = ((y2 * 2 + z) * 2 + c) * rows
                        label = (half * 2 + y2 + c) % SIDE
                        for start, part in parts:
                            targets[c][z, 0, label, :, pl.ds(start, part.shape[1])] = part[
                                low : low + rows
                            ]

        @pl.when(core == 0)
        def _():
            store((kept_ref, away_ref))

        @pl.when(core != 0)
        def _():
            store((away_ref, kept_ref))


def products(hidden, right, weights, joint, cot=None, act=None):
    count, width = hidden.shape
    rank = right.shape[1] - joint.shape[1]
    with_up = cot is not None
    cols = right.shape[1] + (rank if with_up else 0)
    rows = width // (SIDE * SIDE * 4)
    part = width // SIDE
    core = (lax.axis_index("dp") % 2).astype(jnp.int32).reshape(1)
    tokens = pl.BlockSpec((count, part), lambda i, core: (0, i))
    in_specs = [
        tokens,
        pl.BlockSpec(right.shape, lambda i, core: (0, 0)),
        pl.BlockSpec((part, rank), lambda i, core: (i, 0)),
        pl.BlockSpec(joint.shape, lambda i, core: (0, 0)),
    ]
    operands = [hidden, right, weights, joint]
    if with_up:
        in_specs += [tokens, pl.BlockSpec(act.shape, lambda i, core: (0, 0))]
        operands += [cot, act]
    shape = (2, SIDE, SIDE, rows, cols)
    block = (2, 1, SIDE, rows, cols)
    out_specs = [
        pl.BlockSpec(block, lambda i, core: (0, (i + core[0]) % SIDE, 0, 0, 0)),
        pl.BlockSpec(block, lambda i, core: (0, (i + 1 - core[0]) % SIDE, 0, 0, 0)),
    ]
    flops = 2 * width * (count * cols + rank * joint.shape[1])
    return pl.pallas_call(
        lambda *refs: product_kernel(rank, with_up, *refs),
        grid_spec=pltpu.PrefetchScalarGridSpec(
            num_scalar_prefetch=1, grid=(SIDE,), in_specs=in_specs, out_specs=out_specs
        ),
        out_shape=[jax.ShapeDtypeStruct(shape, BF)] * 2,
        compiler_params=pltpu.CompilerParams(vmem_limit_bytes=VMEM_BYTES),
        cost_estimate=pl.CostEstimate(
            flops=flops, bytes_accessed=2 * width * (2 * count + 2 * cols), transcendentals=0
        ),
        name="products",
    )(core, *operands)


def dot(a, b, contract):
    return lax.dot_general(a, b, ((contract[0], contract[1]), ((), ())), preferred_element_type=F32)


def on_device(saved_inputs, cotangent, adapter_down, adapter_up, image_rows):
    section = lax.axis_index("pipe")
    micro, tokens, width = cotangent.shape
    rank = adapter_down.shape[2]
    count = micro * tokens
    factor = (count * lax.axis_size("dp")) ** (-0.5)
    hidden = saved_inputs.reshape(count, width)
    cot = cotangent.reshape(count, width)

    up_shard = adapter_up[0].T
    extra = [send(up_shard, shifted(d)) for d in (1, 2, 3)]
    ring = gather_ring(jnp.concatenate([adapter_down[0], extra[0], up_shard], axis=1))
    far_shard, ring = barrier((jnp.concatenate(extra[1:], axis=1), ring))
    far_ring = gather_ring(far_shard)
    weights = gather_cores(ring)
    down = weights[:, :rank]

    hf = hidden.astype(F32)
    inverse = lax.rsqrt(jnp.mean(hf * hf, axis=-1, keepdims=True) + 1e-06)
    near = dot(hidden, weights[:, : 2 * rank], ((1,), (0,)))
    pre = inverse * near[:, :rank]
    back = dot(cot, weights[:, 2 * rank :], ((1,), (0,)))
    near_mixed = dot(down, weights[:, rank : 2 * rank], ((0,), (0,))).astype(BF)
    sigma = jax.nn.sigmoid(pre)
    act = (pre * sigma).astype(BF)
    slope = sigma * (1.0 + pre * (1.0 - sigma))
    acts = [send(act, shifted(d)) for d in (1, 2, 3)]

    def local(back):
        back_pre = (back * slope).astype(BF)
        wide = back_pre.astype(F32)
        along = jnp.sum(wide * pre, axis=-1, keepdims=True) / width
        return back_pre, wide * inverse, along * inverse * inverse

    def columns(scaled, pull, levels, **up):
        scaled = scaled.astype(BF)
        right = jnp.concatenate(acts[:levels], axis=1)
        joint = dot(scaled, right, ((0,), (0,))).astype(BF)
        pulled = (-pull * right.astype(F32)).astype(BF)
        return products(hidden, jnp.concatenate([scaled, pulled], axis=1), weights, joint, **up)

    def push(back_pre, pull, mixed, cross):
        pushed = dot(back_pre, mixed, ((1,), (0,)))
        return (inverse * pushed - pull * cross).astype(BF)

    back_pre, scaled, pull = local(back)
    came = send(push(back_pre, pull, near_mixed, near[:, rank:]), shifted(-1, 3))
    early = columns(scaled, pull, 3, cot=cot, act=act)
    far = gather_cores(far_ring)
    far_cross = dot(hidden, far, ((1,), (0,)))
    far_mixed = dot(down, far, ((0,), (0,))).astype(BF)
    far_push = push(back_pre, pull, far_mixed, far_cross)
    came, far_push, early = barrier((came, far_push, early))
    back = back + came.astype(F32)
    back_pre, scaled, pull = local(back)
    came = send(push(back_pre, pull, near_mixed, near[:, rank:]), shifted(-1, 2))
    came_far = send(far_push[:, :rank], shifted(-2, 3))
    early = add_cores(*early)
    far_push_2 = push(back_pre, pull, far_mixed[:, :rank], far_cross[:, :rank])
    came, came_far, early, far_push_2 = barrier((came, came_far, early, far_push_2))
    back = back + came.astype(F32) + came_far.astype(F32)
    back_pre, scaled, pull = local(back)
    came = send(push(back_pre, pull, near_mixed, near[:, rank:]), shifted(-1, 1))
    came_far = send(far_push_2, shifted(-2, 2))
    came_last = send(far_push[:, rank:], shifted(-3, 3))
    back = back + came.astype(F32) + came_far.astype(F32) + came_last.astype(F32)
    early = scatter_ring(early)
    back_pre, scaled, pull = local(back)
    late = columns(scaled, pull, 2)
    scaled, pull, late = barrier((scaled, pull, late))
    late = add_cores(*late)

    picks = (image_rows[:, :, None] == jnp.arange(tokens, dtype=jnp.int32)).astype(BF)

    def rows_of(array):
        array = array.reshape(micro, tokens, -1)
        out = lax.dot_general(picks, array, (((2,), (1,)), ((0,), (0,))), preferred_element_type=F32)
        return out.reshape(-1, out.shape[-1])

    def rows_exact(column):
        index = (image_rows + jnp.arange(micro, dtype=jnp.int32)[:, None] * tokens).reshape(-1)
        return jnp.take(column, index, axis=0)

    picked = rows_of(scaled.astype(BF)).astype(BF)
    moved = dot(picked, down, ((1,), (1,))) - rows_exact(pull) * rows_of(hidden)
    part = width // SECTIONS
    moved, late = barrier((moved.astype(BF), late))
    late = scatter_ring(late)
    mine = rows_of(lax.dynamic_slice_in_dim(cot, section * part, part, 1))
    feature = [mine, mine, mine]
    for turn in range(SECTIONS):
        goal = (section + turn) % SECTIONS
        block = lax.dynamic_slice_in_dim(moved, goal * part, part, 1)
        origin = (section - turn) % SECTIONS
        if turn:
            block = send(block, turned(turn))
        for level in range(LEVELS):
            feature[level] = feature[level] + jnp.where(origin > level, block.astype(F32), 0.0)
    feature_grads = jnp.stack(feature).astype(BF).reshape(LEVELS, micro, -1, part)

    sums = jnp.where(section == 3, early[:, rank : 4 * rank], late)
    down_grad = (sums[:, :rank] * factor)[None]
    up_sum = early[:, :rank]
    for d, piece in ((1, sums[:, rank : 2 * rank]), (2, sums[:, 2 * rank :]), (3, early[:, 4 * rank :])):
        up_sum = up_sum + send(piece, shifted(-d))
    up_grad = (up_sum.T * factor)[None]
    return (down_grad, up_grad, feature_grads)


def solution(mesh):
    placed = (
        P("pipe", None, "dp", None),
        P(None, "dp", None),
        P("pipe", "dp", None),
        P("pipe", None, "dp"),
        P(None, "dp"),
    )
    return jax.shard_map(
        on_device,
        mesh=mesh,
        in_specs=placed,
        out_specs=(P("pipe", "dp", None), P("pipe", None, "dp"), P(None, None, "dp", "pipe")),
        check_vma=False,
    )
```

```python
import jax
import jax.numpy as jnp
from jax import lax
from jax.experimental import pallas as pl
from jax.experimental.pallas import tpu as pltpu
from jax.sharding import PartitionSpec as P

LEVELS = 3
SIDE = 4
SECTIONS = 4
AXES = ("dp", "pipe")
BF = jnp.bfloat16
F32 = jnp.float32
VMEM_BYTES = 48 * 1024 * 1024
barrier = lax.optimization_barrier


def route(target):
    pairs = []
    for x in range(SIDE):
        for y in range(SIDE):
            for z in range(2):
                for c in range(2):
                    for s in range(SECTIONS):
                        to = target(x, y, z, c, s)
                        if to is None:
                            continue
                        tx, ty, tz, tc, ts = to
                        source = (((x * SIDE + y) * 2 + z) * 2 + c) * SECTIONS + s
                        dest = (((tx * SIDE + ty) * 2 + tz) * 2 + tc) * SECTIONS + ts
                        pairs.append((source, dest))
    return pairs


def send(block, target):
    return lax.ppermute(block, AXES, route(target))


def mate_z(x, y, z, c, s):
    return (x, y, 1 - z, c, s)


def mate_core(x, y, z, c, s):
    return (x, y, z, 1 - c, s)


def mate_cross(x, y, z, c, s):
    return (x, y, 1 - z, 1 - c, s)


def mate_x(mask):
    def target(x, y, z, c, s):
        return (((((x + c) % SIDE) ^ mask) - c) % SIDE, y, z, c, s)

    return target


def mate_y(mask):
    def target(x, y, z, c, s):
        return (x, ((((y + c) % SIDE) ^ mask) - c) % SIDE, z, c, s)

    return target


def shifted(distance, only=None):
    def target(x, y, z, c, s):
        if only is not None and s != only:
            return None
        if not 0 <= s + distance < SECTIONS:
            return None
        return (x, y, z, c, s + distance)

    return target


def turned(distance):
    def target(x, y, z, c, s):
        if s == 0:
            return None
        return (x, y, z, c, (s + distance) % SECTIONS)

    return target


def both(mine, theirs, bit, axis):
    low = jnp.where(bit == 0, mine, theirs)
    high = jnp.where(bit == 0, theirs, mine)
    return jnp.concatenate([low, high], axis=axis)


def place():
    index = lax.axis_index("dp")
    core = index % 2
    z = (index // 2) % 2
    y = (index // 4) % SIDE
    x = index // (4 * SIDE)
    return x, y, z, core


def gather_ring(blocks):
    x, y, z, core = place()
    xs = (x + core) % SIDE
    ys = (y + core) % SIDE
    halves = []
    for color, block in enumerate(blocks):
        first, second = ((xs, mate_x), (ys, mate_y)) if color == 0 else ((ys, mate_y), (xs, mate_x))
        now = block[None, None]
        for axis, (label, mate) in ((1, first), (0, second)):
            now = both(now, send(now, mate(1)), label % 2, axis)
            now = both(now, send(now, mate(3)), label // 2, axis)
        halves.append(now)
    return halves


def halve(now, label, mate, axis):
    for mask, bit, size in ((3, label // 2, 2), (1, label % 2, 1)):
        kept = lax.dynamic_slice_in_dim(now, bit * size, size, axis)
        away = lax.dynamic_slice_in_dim(now, (1 - bit) * size, size, axis)
        now = kept + send(away.astype(BF), mate(mask)).astype(F32)
    return now


def halve_rest(kept, away, label, mate, axis):
    now = kept.astype(F32) + send(away, mate(3)).astype(F32)
    low = lax.dynamic_slice_in_dim(now, label % 2, 1, axis)
    high = lax.dynamic_slice_in_dim(now, 1 - label % 2, 1, axis)
    return low + send(high.astype(BF), mate(1)).astype(F32)


def scatter_ring(kept_a, away_a, kept_b, away_b):
    x, y, z, core = place()
    xs = (x + core) % SIDE
    ys = (y + core) % SIDE
    first = halve(halve_rest(kept_a, away_a, xs, mate_x, 0), ys, mate_y, 1)[0, 0]
    second = halve(halve_rest(kept_b, away_b, ys, mate_y, 1), xs, mate_x, 0)[0, 0]
    cols = first.shape[1]
    mine = jnp.where(z == 0, first, second).reshape(2, -1, cols)
    away = jnp.where(z == 0, second, first).astype(BF).reshape(2, -1, cols)
    own = lax.dynamic_index_in_dim(mine, core, 0, False)
    own = own + send(lax.dynamic_index_in_dim(away, core, 0, False), mate_z).astype(F32)
    other = send(lax.dynamic_index_in_dim(mine, 1 - core, 0, False), mate_core)
    cross = send(lax.dynamic_index_in_dim(away, 1 - core, 0, False), mate_cross)
    return own, other + cross.astype(F32)


def dot(a, b, contract):
    return lax.dot_general(a, b, ((contract[0], contract[1]), ((), ())), preferred_element_type=F32)


def inner_kernel(
    rank, core_ref, hm_ref, hs_ref, tm_ref, ts_ref, a_ref, b_ref,
    down_ref, raw_ref, nm_ref, ns_ref, um_ref, us_ref, mixed_ref, square_ref, weights,
):
    core = core_ref[0]
    rows = a_ref.shape[2]
    for y in range(SIDE):
        label = lax.rem(core + y, SIDE)
        weights[pl.ds(2 * y * rows, rows), :] = a_ref[label, 0]
        weights[pl.ds((2 * y + 1) * rows, rows), :] = b_ref[0, label]
    down = weights[:, :rank]
    second = weights[:, rank : 2 * rank]
    third = weights[:, 2 * rank :]
    down_ref[...] = down
    hm = hm_ref[0]
    wide = hm.astype(F32)
    results = (
        (raw_ref, dot(hm, down, ((1,), (0,)))),
        (nm_ref, dot(hm, second, ((1,), (0,)))),
        (ns_ref, dot(hs_ref[0], second, ((1,), (0,)))),
        (um_ref, dot(tm_ref[0], third, ((1,), (0,)))),
        (us_ref, dot(ts_ref[0], third, ((1,), (0,)))),
        (mixed_ref, dot(down, weights[:, rank:], ((0,), (0,)))),
        (square_ref, jnp.sum(wide * wide, axis=1, keepdims=True)),
    )
    first = pl.program_id(0) == 0

    @pl.when(first)
    def _():
        for ref, value in results:
            ref[...] = value

    @pl.when(jnp.logical_not(first))
    def _():
        for ref, value in results:
            ref[...] += value


def inner_products(pair, sibling, ring, rank):
    _, count, width = pair.shape
    part = width // SIDE
    rows, cols = ring[0].shape[2:]
    core = (lax.axis_index("dp") % 2).astype(jnp.int32).reshape(1)
    hidden = pl.BlockSpec((1, count, part), lambda i, core: (0, 0, i))
    third = pl.BlockSpec((1, count, part), lambda i, core: (1 - core[0], 0, i))
    whole = lambda shape: pl.BlockSpec(shape, lambda i, core: (0, 0))
    small = (count, rank)
    shapes = [small] * 5 + [(rank, 2 * rank), (count, 1)]
    return pl.pallas_call(
        lambda *refs: inner_kernel(rank, *refs),
        grid_spec=pltpu.PrefetchScalarGridSpec(
            num_scalar_prefetch=1,
            grid=(SIDE,),
            in_specs=[
                hidden,
                hidden,
                third,
                third,
                pl.BlockSpec((SIDE, 1, rows, cols), lambda i, core: (0, (i + core[0]) % SIDE, 0, 0)),
                pl.BlockSpec((1, SIDE, rows, cols), lambda i, core: ((i + core[0]) % SIDE, 0, 0, 0)),
            ],
            out_specs=[pl.BlockSpec((part, rank), lambda i, core: (i, 0))] + [whole(s) for s in shapes],
            scratch_shapes=[pltpu.VMEM((part, cols), BF)],
        ),
        out_shape=[jax.ShapeDtypeStruct((width, rank), BF)]
        + [jax.ShapeDtypeStruct(s, F32) for s in shapes],
        compiler_params=pltpu.CompilerParams(vmem_limit_bytes=VMEM_BYTES),
        cost_estimate=pl.CostEstimate(
            flops=2 * width * rank * (5 * count + 2 * rank),
            bytes_accessed=2 * width * (4 * count + cols + rank),
            transcendentals=0,
        ),
        name="inner_products",
    )(core, pair, sibling, pair, sibling, *ring)


def outer_kernel(
    rank, where_ref, hm_ref, hs_ref, tm_ref, ts_ref, rm_ref, rs_ref, down_ref, joint_ref,
    kept_a, away_a, kept_b, away_b, total,
):
    core, half_x, half_y = where_ref[0], where_ref[1], where_ref[2]
    rows = total.shape[1]
    chunk = 4 * rows
    cols = joint_ref.shape[1]
    for half in range(2):
        span = pl.ds(half * chunk, chunk)
        inner = dot(down_ref[span, :], joint_ref[...], ((1,), (0,)))
        left = dot(tm_ref[0, :, span], rm_ref[:, :rank], ((0,), (0,)))
        left = left + dot(ts_ref[0, :, span], rs_ref[:, :rank], ((0,), (0,)))
        right = dot(hm_ref[0, :, span], rm_ref[:, rank:], ((0,), (0,)))
        right = right + dot(hs_ref[0, :, span], rs_ref[:, rank:], ((0,), (0,)))
        left = (left + inner[:, :rank]).astype(BF)
        right = (right + inner[:, rank:]).astype(BF)
        for k in range(4):
            total[half * 4 + k, :, :rank] = left[k * rows : (k + 1) * rows]
            total[half * 4 + k, :, rank:] = right[k * rows : (k + 1) * rows]
    for t in range(SIDE):
        y = lax.rem(t + SIDE - core, SIDE)
        value = total[2 * y]

        @pl.when(pl.program_id(0) < 2)
        def _():
            away_a[0, t] = value

        @pl.when(pl.program_id(0) >= 2)
        def _():
            kept_a[0, t] = value

    for t in range(2):
        y = lax.rem(2 * half_y + t + SIDE - core, SIDE)
        kept_b[0, t] = total[2 * y + 1]
        y = lax.rem(2 * (1 - half_y) + t + SIDE - core, SIDE)
        away_b[0, t] = total[2 * y + 1]


def outer_products(pair, sibling, right, right_sibling, down, joint):
    _, count, width = pair.shape
    rank, cols = joint.shape
    part = width // SIDE
    rows = part // (2 * SIDE)
    x, y, z, core = place()
    xs = (x + core) % SIDE
    ys = (y + core) % SIDE
    where = jnp.stack([core, xs // 2, ys // 2]).astype(jnp.int32)

    def label(i, w):
        half = jnp.where(i < 2, 1 - w[1], w[1])
        return 2 * half + i % 2

    def block(i, w):
        return (label(i, w) + SIDE - w[0]) % SIDE

    hidden = pl.BlockSpec((1, count, part), lambda i, w: (0, 0, block(i, w)))
    third = pl.BlockSpec((1, count, part), lambda i, w: (1 - w[0], 0, block(i, w)))
    same = lambda shape: pl.BlockSpec(shape, lambda i, w: (0, 0))
    return pl.pallas_call(
        lambda *refs: outer_kernel(rank, *refs),
        grid_spec=pltpu.PrefetchScalarGridSpec(
            num_scalar_prefetch=1,
            grid=(SIDE,),
            in_specs=[
                hidden,
                hidden,
                third,
                third,
                same(right.shape),
                same(right.shape),
                pl.BlockSpec((part, rank), lambda i, w: (block(i, w), 0)),
                same(joint.shape),
            ],
            out_specs=[
                pl.BlockSpec((1, SIDE, rows, cols), lambda i, w: (jnp.maximum(i - 2, 0), 0, 0, 0)),
                pl.BlockSpec((1, SIDE, rows, cols), lambda i, w: (jnp.minimum(i, 1), 0, 0, 0)),
                pl.BlockSpec((1, 2, rows, cols), lambda i, w: (label(i, w), 0, 0, 0)),
                pl.BlockSpec((1, 2, rows, cols), lambda i, w: (label(i, w), 0, 0, 0)),
            ],
            scratch_shapes=[pltpu.VMEM((2 * SIDE, rows, cols), BF)],
        ),
        out_shape=[jax.ShapeDtypeStruct((2, SIDE, rows, cols), BF)] * 2
        + [jax.ShapeDtypeStruct((SIDE, 2, rows, cols), BF)] * 2,
        compiler_params=pltpu.CompilerParams(vmem_limit_bytes=VMEM_BYTES),
        cost_estimate=pl.CostEstimate(
            flops=2 * width * cols * (2 * count + rank),
            bytes_accessed=2 * width * (4 * count + cols + rank),
            transcendentals=0,
        ),
        name="outer_products",
    )(where, pair, sibling, pair, sibling, right, right_sibling, down, joint)


def on_device(saved_inputs, cotangent, adapter_down, adapter_up, image_rows):
    section = lax.axis_index("pipe")
    x, y, z, core = place()
    micro, tokens, width = cotangent.shape
    rank = adapter_down.shape[2]
    count = micro * tokens
    factor = (count * lax.axis_size("dp")) ** (-0.5)
    hidden = saved_inputs.reshape(count, width)
    cot = cotangent.reshape(count, width)

    up_shard = adapter_up[0].T
    extra = [send(up_shard, shifted(d)) for d in (1, 2, 3)]
    sets = [
        jnp.concatenate([adapter_down[0], extra[0], up_shard], axis=1),
        jnp.concatenate([adapter_down[0], extra[1], extra[2]], axis=1),
    ]
    mine = jnp.where(core == 0, sets[0], sets[1])
    away = jnp.where(core == 0, sets[1], sets[0])
    by_z = send(mine, mate_z)
    by_core = send(away, mate_core)
    by_both = send(away, mate_cross)
    here = both(mine, by_core, core, 0)
    there = both(by_z, by_both, core, 0)
    blocks = [jnp.where(z == 0, here, there), jnp.where(z == 0, there, here)]
    pair, blocks = barrier((jnp.stack([hidden, cot]), blocks))
    sibling = send(pair, mate_core)
    ring = gather_ring(blocks)

    down, raw, near_m, near_s, last_m, last_s, mixed, square = inner_products(
        pair, sibling, ring, rank
    )
    swap = jnp.concatenate([jnp.concatenate([near_s, last_s], axis=1), mixed], axis=0).astype(BF)
    swap = send(swap, mate_core)
    inverse = lax.rsqrt(square / width + 1e-06)
    pre = inverse * raw
    sigma = jax.nn.sigmoid(pre)
    act = (pre * sigma).astype(BF)
    slope = sigma * (1.0 + pre * (1.0 - sigma))
    acts = [send(act, shifted(d)) for d in (1, 2, 3)]
    came = swap[:count].astype(F32)
    back = jnp.where(core == 0, last_m, came[:, rank:])
    cross = jnp.concatenate(
        [
            jnp.where(core == 0, near_m, came[:, :rank]),
            jnp.where(core == 0, came[:, :rank], near_m),
            jnp.where(core == 0, came[:, rank:], last_m),
        ],
        axis=1,
    )
    ours = mixed.astype(BF)
    theirs = swap[count:]
    mixes = jnp.concatenate(
        [jnp.where(core == 0, ours, theirs)[:, :rank], jnp.where(core == 0, theirs, ours)], axis=1
    )

    def local(back):
        back_pre = (back * slope).astype(BF)
        wide = back_pre.astype(F32)
        along = jnp.sum(wide * pre, axis=-1, keepdims=True) / width
        return back_pre, wide * inverse, along * inverse * inverse

    for s in (3, 2, 1):
        back_pre, scaled, pull = local(back)
        pushed = dot(back_pre, mixes[:, : s * rank], ((1,), (0,)))
        pushed = (inverse * pushed - pull * cross[:, : s * rank]).astype(BF)
        if s == 3:
            every = jnp.concatenate([act] + acts, axis=1)
            every_sibling = send(every, mate_core)
        for d in range(1, s + 1):
            came = send(pushed[:, (d - 1) * rank : d * rank], shifted(-d, s))
            back = back + came.astype(F32)
    back_pre, scaled, pull = local(back)
    scaled = scaled.astype(BF)

    def bases(every):
        split = rank + rank // 2
        low = jnp.concatenate(
            [jnp.zeros((count, 2 * rank), BF), every[:, rank : rank + rank // 2]], axis=1
        )
        high = jnp.concatenate([every[:, 2 * rank :], every[:, split : 2 * rank]], axis=1)
        return jnp.where(core == 0, low, high)

    def right_side(every, base, scaled, pull):
        direct = jnp.concatenate(
            [every[:, :rank], scaled, jnp.zeros((count, rank // 2), BF)], axis=1
        )
        pulled = (-pull * base.astype(F32)).astype(BF)
        return jnp.where(core == 0, direct, 0) + pulled

    base_m, base_s = bases(every), bases(every_sibling)
    wire = jnp.concatenate(
        [scaled, jnp.broadcast_to(pull, (count, rank // 2)).astype(BF)], axis=1
    )
    wire = send(wire, mate_core)
    scaled_s, pull_s = wire[:, :rank], wire[:, rank : rank + 1].astype(F32)
    joint = dot(scaled, base_m, ((0,), (0,))) + dot(scaled_s, base_s, ((0,), (0,)))
    sums = outer_products(
        pair,
        sibling,
        right_side(every, base_m, scaled, pull),
        right_side(every_sibling, base_s, scaled_s, pull_s),
        down,
        joint.astype(BF),
    )
    scaled, pull, sums = barrier((scaled, pull, sums))

    picks = (image_rows[:, :, None] == jnp.arange(tokens, dtype=jnp.int32)).astype(BF)

    def rows_of(array):
        array = array.reshape(micro, tokens, -1)
        out = lax.dot_general(picks, array, (((2,), (1,)), ((0,), (0,))), preferred_element_type=F32)
        return out.reshape(-1, out.shape[-1])

    def rows_exact(column):
        index = (image_rows + jnp.arange(micro, dtype=jnp.int32)[:, None] * tokens).reshape(-1)
        return jnp.take(column, index, axis=0)

    picked = rows_of(scaled).astype(BF)
    moved = dot(picked, down, ((1,), (1,))) - rows_exact(pull) * rows_of(hidden)
    part = width // SECTIONS
    moved = moved.astype(BF)
    mine = rows_of(lax.dynamic_slice_in_dim(cot, section * part, part, 1))
    feature = [mine, mine, mine]
    for turn in range(SECTIONS):
        goal = (section + turn) % SECTIONS
        block = lax.dynamic_slice_in_dim(moved, goal * part, part, 1)
        origin = (section - turn) % SECTIONS
        if turn:
            block = send(block, turned(turn))
        for level in range(LEVELS):
            feature[level] = feature[level] + jnp.where(origin > level, block.astype(F32), 0.0)
    feature_grads = jnp.stack(feature).astype(BF).reshape(LEVELS, micro, -1, part)

    own, other = scatter_ring(*sums)
    zero = jnp.where(core == 0, own, other)
    one = jnp.where(core == 0, other, own)
    down_grad = (zero[:, rank : 2 * rank] * factor)[None]
    near = jnp.concatenate([zero[:, 2 * rank :], one[:, 2 * rank :]], axis=1)
    up_sum = zero[:, :rank]
    for d, piece in ((1, near), (2, one[:, :rank]), (3, one[:, rank : 2 * rank])):
        up_sum = up_sum + send(piece, shifted(-d))
    up_grad = (up_sum.T * factor)[None]
    return (down_grad, up_grad, feature_grads)


def solution(mesh):
    placed = (
        P("pipe", None, "dp", None),
        P(None, "dp", None),
        P("pipe", "dp", None),
        P("pipe", None, "dp"),
        P(None, "dp"),
    )
    return jax.shard_map(
        on_device,
        mesh=mesh,
        in_specs=placed,
        out_specs=(P("pipe", "dp", None), P("pipe", None, "dp"), P(None, None, "dp", "pipe")),
        check_vma=False,
    )
```

```python
import jax
import jax.numpy as jnp
from jax import lax
from jax.experimental import pallas as pl
from jax.experimental.pallas import tpu as pltpu
from jax.sharding import PartitionSpec as P

LEVELS = 3
SIDE = 4
SECTIONS = 4
AXES = ("dp", "pipe")
BF = jnp.bfloat16
F32 = jnp.float32
VMEM_BYTES = 48 * 1024 * 1024
barrier = lax.optimization_barrier


def route(target):
    pairs = []
    for x in range(SIDE):
        for y in range(SIDE):
            for z in range(2):
                for c in range(2):
                    for s in range(SECTIONS):
                        to = target(x, y, z, c, s)
                        if to is None:
                            continue
                        tx, ty, tz, tc, ts = to
                        source = (((x * SIDE + y) * 2 + z) * 2 + c) * SECTIONS + s
                        dest = (((tx * SIDE + ty) * 2 + tz) * 2 + tc) * SECTIONS + ts
                        pairs.append((source, dest))
    return pairs


def send(block, target):
    return lax.ppermute(block, AXES, route(target))


def mate_z(x, y, z, c, s):
    return (x, y, 1 - z, c, s)


def mate_core(x, y, z, c, s):
    return (x, y, z, 1 - c, s)


def mate_cross(x, y, z, c, s):
    return (x, y, 1 - z, 1 - c, s)


def mate_x(mask):
    def target(x, y, z, c, s):
        return (((((x + c) % SIDE) ^ mask) - c) % SIDE, y, z, c, s)

    return target


def mate_y(mask):
    def target(x, y, z, c, s):
        return (x, ((((y + c) % SIDE) ^ mask) - c) % SIDE, z, c, s)

    return target


def shifted(distance, only=None):
    def target(x, y, z, c, s):
        if only is not None and s != only:
            return None
        if not 0 <= s + distance < SECTIONS:
            return None
        return (x, y, z, c, s + distance)

    return target


def turned(distance):
    def target(x, y, z, c, s):
        if s == 0:
            return None
        return (x, y, z, c, (s + distance) % SECTIONS)

    return target


def both(mine, theirs, bit, axis):
    low = jnp.where(bit == 0, mine, theirs)
    high = jnp.where(bit == 0, theirs, mine)
    return jnp.concatenate([low, high], axis=axis)


def place():
    index = lax.axis_index("dp")
    core = index % 2
    z = (index // 2) % 2
    y = (index // 4) % SIDE
    x = index // (4 * SIDE)
    return x, y, z, core


def gather_ring(blocks):
    x, y, z, core = place()
    xs = (x + core) % SIDE
    ys = (y + core) % SIDE
    halves = []
    for color, block in enumerate(blocks):
        first, second = ((xs, mate_x), (ys, mate_y)) if color == 0 else ((ys, mate_y), (xs, mate_x))
        now = block[None, None]
        for axis, (label, mate) in ((1, first), (0, second)):
            now = both(now, send(now, mate(1)), label % 2, axis)
            far = send(now, mate(3))
            if axis == 1:
                now = both(now, far, label // 2, axis)
        halves += [now, far]
    return halves


def halve(now, label, mate, axis):
    for mask, bit, size in ((3, label // 2, 2), (1, label % 2, 1)):
        kept = lax.dynamic_slice_in_dim(now, bit * size, size, axis)
        away = lax.dynamic_slice_in_dim(now, (1 - bit) * size, size, axis)
        now = kept + send(away.astype(BF), mate(mask)).astype(F32)
    return now


def halve_rest(kept, away, label, mate, axis):
    now = kept.astype(F32) + send(away, mate(3)).astype(F32)
    low = lax.dynamic_slice_in_dim(now, label % 2, 1, axis)
    high = lax.dynamic_slice_in_dim(now, 1 - label % 2, 1, axis)
    return low + send(high.astype(BF), mate(1)).astype(F32)


def scatter_ring(kept_a, away_a, kept_b, away_b, beside):
    x, y, z, core = place()
    xs = (x + core) % SIDE
    ys = (y + core) % SIDE
    first = halve_rest(kept_a, away_a, xs, mate_x, 0)
    second = halve_rest(kept_b, away_b, ys, mate_y, 1)
    first, second, beside = barrier((first, second, beside))
    first = halve(first, ys, mate_y, 1)[0, 0]
    second = halve(second, xs, mate_x, 0)[0, 0]
    cols = first.shape[1]
    mine = jnp.where(z == 0, first, second).reshape(2, -1, cols)
    away = jnp.where(z == 0, second, first).astype(BF).reshape(2, -1, cols)
    own = lax.dynamic_index_in_dim(mine, core, 0, False)
    own = own + send(lax.dynamic_index_in_dim(away, core, 0, False), mate_z).astype(F32)
    other = send(lax.dynamic_index_in_dim(mine, 1 - core, 0, False), mate_core)
    cross = send(lax.dynamic_index_in_dim(away, 1 - core, 0, False), mate_cross)
    return (own, other + cross.astype(F32)), beside


def dot(a, b, contract):
    return lax.dot_general(a, b, ((contract[0], contract[1]), ((), ())), preferred_element_type=F32)


def step_label(i, half):
    return 2 * jnp.where(i < 2, half, 1 - half) + i % 2


def inner_kernel(
    rank, where_ref, hm_ref, hs_ref, tm_ref, ts_ref, am_ref, at_ref, bm_ref, bt_ref,
    down_ref, raw_ref, nm_ref, ns_ref, um_ref, us_ref, mixed_ref, square_ref, weights,
):
    core, half_y = where_ref[0], where_ref[2]
    step = pl.program_id(0)
    rows = am_ref.shape[2]
    for y in range(SIDE):
        label = lax.rem(core + y, SIDE)
        odd = lax.rem(label, 2)
        weights[pl.ds(2 * y * rows, rows), :] = jnp.where(
            label // 2 == half_y, am_ref[odd, 0], at_ref[odd, 0]
        )
        weights[pl.ds((2 * y + 1) * rows, rows), :] = jnp.where(
            step < 2, bm_ref[0, label], bt_ref[0, label]
        )
    down = weights[:, :rank]
    second = weights[:, rank : 2 * rank]
    third = weights[:, 2 * rank :]
    down_ref[...] = down
    hm, hs = hm_ref[...], hs_ref[...]
    tm = jnp.where(core == 0, tm_ref[...], hm)
    ts = jnp.where(core == 0, ts_ref[...], hs)
    wide = hm.astype(F32)
    results = (
        (raw_ref, dot(hm, down, ((1,), (0,)))),
        (nm_ref, dot(hm, second, ((1,), (0,)))),
        (ns_ref, dot(hs, second, ((1,), (0,)))),
        (um_ref, dot(tm, third, ((1,), (0,)))),
        (us_ref, dot(ts, third, ((1,), (0,)))),
        (mixed_ref, dot(down, weights[:, rank:], ((0,), (0,)))),
        (square_ref, jnp.sum(wide * wide, axis=1, keepdims=True)),
    )

    @pl.when(step == 0)
    def _():
        for ref, value in results:
            ref[...] = value

    @pl.when(step > 0)
    def _():
        for ref, value in results:
            ref[...] += value


def position():
    x, y, z, core = place()
    return jnp.stack([core, (x + core) % SIDE // 2, (y + core) % SIDE // 2]).astype(jnp.int32)


def inner_products(hidden, hidden_s, cot, cot_s, ring, rank):
    count, width = hidden.shape
    part = width // SIDE
    rows, cols = ring[0].shape[2:]

    def label(i, w):
        return step_label(i, w[1])

    def block(i, w):
        return (label(i, w) + SIDE - w[0]) % SIDE

    first = pl.BlockSpec((count, part), lambda i, w: (0, block(i, w)))
    third = pl.BlockSpec((count, part), lambda i, w: (0, (1 - w[0]) * block(i, w)))
    one = pl.BlockSpec((2, 1, rows, cols), lambda i, w: (0, label(i, w), 0, 0))
    whole = lambda shape: pl.BlockSpec(shape, lambda i, w: (0, 0))
    small = (count, rank)
    shapes = [small] * 5 + [(rank, 2 * rank), (count, 1)]
    return pl.pallas_call(
        lambda *refs: inner_kernel(rank, *refs),
        grid_spec=pltpu.PrefetchScalarGridSpec(
            num_scalar_prefetch=1,
            grid=(SIDE,),
            in_specs=[
                first,
                first,
                third,
                third,
                one,
                one,
                pl.BlockSpec((1, SIDE, rows, cols), lambda i, w: (jnp.minimum(i, 1), 0, 0, 0)),
                pl.BlockSpec((1, SIDE, rows, cols), lambda i, w: (jnp.maximum(i - 2, 0), 0, 0, 0)),
            ],
            out_specs=[pl.BlockSpec((part, rank), lambda i, w: (block(i, w), 0))]
            + [whole(s) for s in shapes],
            scratch_shapes=[pltpu.VMEM((part, cols), BF)],
        ),
        out_shape=[jax.ShapeDtypeStruct((width, rank), BF)]
        + [jax.ShapeDtypeStruct(s, F32) for s in shapes],
        compiler_params=pltpu.CompilerParams(vmem_limit_bytes=VMEM_BYTES),
        cost_estimate=pl.CostEstimate(
            flops=2 * width * rank * (5 * count + 2 * rank),
            bytes_accessed=2 * width * (4 * count + cols + rank),
            transcendentals=0,
        ),
        name="inner_products",
    )(position(), hidden, hidden_s, cot, cot_s, *ring)


def outer_kernel(
    rank, where_ref, hm_ref, hs_ref, tm_ref, ts_ref, rm_ref, rs_ref, down_ref, joint_ref,
    kept_a, away_a, kept_b, away_b, total,
):
    core, half_y = where_ref[0], where_ref[2]
    rows = total.shape[1]
    chunk = 4 * rows
    cols = joint_ref.shape[1]
    for half in range(2):
        span = pl.ds(half * chunk, chunk)
        inner = dot(down_ref[span, :], joint_ref[...], ((1,), (0,)))
        hm, hs = hm_ref[:, span], hs_ref[:, span]
        tm = jnp.where(core == 0, tm_ref[:, span], hm)
        ts = jnp.where(core == 0, ts_ref[:, span], hs)
        left = dot(tm, rm_ref[:, :rank], ((0,), (0,)))
        left = left + dot(ts, rs_ref[:, :rank], ((0,), (0,)))
        right = dot(hm, rm_ref[:, rank:], ((0,), (0,)))
        right = right + dot(hs, rs_ref[:, rank:], ((0,), (0,)))
        left = (left + inner[:, :rank]).astype(BF)
        right = (right + inner[:, rank:]).astype(BF)
        for k in range(4):
            total[half * 4 + k, :, :rank] = left[k * rows : (k + 1) * rows]
            total[half * 4 + k, :, rank:] = right[k * rows : (k + 1) * rows]
    for t in range(SIDE):
        y = lax.rem(t + SIDE - core, SIDE)
        value = total[2 * y]

        @pl.when(pl.program_id(0) < 2)
        def _():
            away_a[0, t] = value

        @pl.when(pl.program_id(0) >= 2)
        def _():
            kept_a[0, t] = value

    for t in range(2):
        y = lax.rem(2 * half_y + t + SIDE - core, SIDE)
        kept_b[0, t] = total[2 * y + 1]
        y = lax.rem(2 * (1 - half_y) + t + SIDE - core, SIDE)
        away_b[0, t] = total[2 * y + 1]


def outer_products(hidden, hidden_s, cot, cot_s, right, right_sibling, down, joint):
    count, width = hidden.shape
    rank, cols = joint.shape
    part = width // SIDE
    rows = part // (2 * SIDE)

    def label(i, w):
        return step_label(i, 1 - w[1])

    def block(i, w):
        return (label(i, w) + SIDE - w[0]) % SIDE

    first = pl.BlockSpec((count, part), lambda i, w: (0, block(i, w)))
    third = pl.BlockSpec((count, part), lambda i, w: (0, (1 - w[0]) * block(i, w)))
    same = lambda shape: pl.BlockSpec(shape, lambda i, w: (0, 0))
    return pl.pallas_call(
        lambda *refs: outer_kernel(rank, *refs),
        grid_spec=pltpu.PrefetchScalarGridSpec(
            num_scalar_prefetch=1,
            grid=(SIDE,),
            in_specs=[
                first,
                first,
                third,
                third,
                same(right.shape),
                same(right.shape),
                pl.BlockSpec((part, rank), lambda i, w: (block(i, w), 0)),
                same(joint.shape),
            ],
            out_specs=[
                pl.BlockSpec((1, SIDE, rows, cols), lambda i, w: (jnp.maximum(i - 2, 0), 0, 0, 0)),
                pl.BlockSpec((1, SIDE, rows, cols), lambda i, w: (jnp.minimum(i, 1), 0, 0, 0)),
                pl.BlockSpec((1, 2, rows, cols), lambda i, w: (label(i, w), 0, 0, 0)),
                pl.BlockSpec((1, 2, rows, cols), lambda i, w: (label(i, w), 0, 0, 0)),
            ],
            scratch_shapes=[pltpu.VMEM((2 * SIDE, rows, cols), BF)],
        ),
        out_shape=[jax.ShapeDtypeStruct((2, SIDE, rows, cols), BF)] * 2
        + [jax.ShapeDtypeStruct((SIDE, 2, rows, cols), BF)] * 2,
        compiler_params=pltpu.CompilerParams(vmem_limit_bytes=VMEM_BYTES),
        cost_estimate=pl.CostEstimate(
            flops=2 * width * cols * (2 * count + rank),
            bytes_accessed=2 * width * (4 * count + cols + rank),
            transcendentals=0,
        ),
        name="outer_products",
    )(position(), hidden, hidden_s, cot, cot_s, right, right_sibling, down, joint)


def moved_kernel(rank, place_ref, picked_ref, down_ref, rows_ref, *outs):
    pull = picked_ref[:, rank : rank + 1].astype(F32)
    value = dot(picked_ref[:, :rank], down_ref[...], ((1,), (1,)))
    value = (value - pull * rows_ref[...].astype(F32)).astype(BF)
    half = value.shape[0] // 2
    for t in range(SECTIONS):

        @pl.when(pl.program_id(0) == t)
        def _():
            outs[2 * t][...] = value[:half]
            outs[2 * t + 1][...] = value[half:]


def moved_blocks(picked, down, rows, section):
    count, width = rows.shape
    rank = down.shape[1]
    part = width // SECTIONS
    half = jax.ShapeDtypeStruct((count // 2, part), BF)
    return pl.pallas_call(
        lambda *refs: moved_kernel(rank, *refs),
        grid_spec=pltpu.PrefetchScalarGridSpec(
            num_scalar_prefetch=1,
            grid=(SECTIONS,),
            in_specs=[
                pl.BlockSpec(picked.shape, lambda t, w: (0, 0)),
                pl.BlockSpec((part, rank), lambda t, w: ((w[0] + t) % SECTIONS, 0)),
                pl.BlockSpec((count, part), lambda t, w: (0, (w[0] + t) % SECTIONS)),
            ],
            out_specs=[pl.BlockSpec(half.shape, lambda t, w: (0, 0))] * (2 * SECTIONS),
        ),
        out_shape=[half] * (2 * SECTIONS),
        compiler_params=pltpu.CompilerParams(vmem_limit_bytes=VMEM_BYTES),
        cost_estimate=pl.CostEstimate(
            flops=2 * count * width * rank, bytes_accessed=4 * count * width, transcendentals=0
        ),
        name="moved_blocks",
    )(section.astype(jnp.int32).reshape(1), picked, down, rows)


def on_device(saved_inputs, cotangent, adapter_down, adapter_up, image_rows):
    section = lax.axis_index("pipe")
    x, y, z, core = place()
    micro, tokens, width = cotangent.shape
    rank = adapter_down.shape[2]
    count = micro * tokens
    factor = (count * lax.axis_size("dp")) ** (-0.5)
    hidden = saved_inputs.reshape(count, width)
    cot = cotangent.reshape(count, width)

    up_shard = adapter_up[0].T
    extra = [send(up_shard, shifted(d)) for d in (1, 2, 3)]
    sets = [
        jnp.concatenate([adapter_down[0], extra[0], up_shard], axis=1),
        jnp.concatenate([adapter_down[0], extra[1], extra[2]], axis=1),
    ]
    mine = jnp.where(core == 0, sets[0], sets[1])
    away = jnp.where(core == 0, sets[1], sets[0])
    by_z = send(mine, mate_z)
    by_core = send(away, mate_core)
    by_both = send(away, mate_cross)
    here = both(mine, by_core, core, 0)
    there = both(by_z, by_both, core, 0)
    blocks = [jnp.where(z == 0, here, there), jnp.where(z == 0, there, here)]
    hidden, cot, blocks = barrier((hidden, cot, blocks))
    hidden_s = send(hidden, mate_core)
    cot_s = send(cot, mate_core)
    ring = gather_ring(blocks)

    picks = (image_rows[:, :, None] == jnp.arange(tokens, dtype=jnp.int32)).astype(BF)

    def rows_of(array):
        array = array.reshape(micro, tokens, -1)
        out = lax.dot_general(picks, array, (((2,), (1,)), ((0,), (0,))), preferred_element_type=F32)
        return out.reshape(-1, out.shape[-1]).astype(BF)

    part = width // SECTIONS
    hidden_rows = rows_of(hidden)
    cot_rows = rows_of(lax.dynamic_slice_in_dim(cot, section * part, part, 1))
    ring, hidden_rows, cot_rows = barrier((ring, hidden_rows, cot_rows))

    down, raw, near_m, near_s, last_m, last_s, mixed, square = inner_products(
        hidden, hidden_s, cot, cot_s, ring, rank
    )
    swap = jnp.concatenate([jnp.concatenate([near_s, last_s], axis=1), mixed], axis=0).astype(BF)
    swap = send(swap, mate_core)
    inverse = lax.rsqrt(square / width + 1e-06)
    pre = inverse * raw
    sigma = jax.nn.sigmoid(pre)
    act = (pre * sigma).astype(BF)
    slope = sigma * (1.0 + pre * (1.0 - sigma))
    acts = [send(act, shifted(d)) for d in (1, 2, 3)]
    came = swap[:count].astype(F32)
    back = jnp.where(core == 0, last_m, came[:, rank:])
    cross = jnp.concatenate(
        [
            jnp.where(core == 0, near_m, came[:, :rank]),
            jnp.where(core == 0, came[:, :rank], near_m),
            jnp.where(core == 0, came[:, rank:], last_m),
        ],
        axis=1,
    )
    ours = mixed.astype(BF)
    theirs = swap[count:]
    mixes = jnp.concatenate(
        [jnp.where(core == 0, ours, theirs)[:, :rank], jnp.where(core == 0, theirs, ours)], axis=1
    )

    def local(back):
        back_pre = (back * slope).astype(BF)
        wide = back_pre.astype(F32)
        along = jnp.sum(wide * pre, axis=-1, keepdims=True) / width
        return back_pre, wide * inverse, along * inverse * inverse

    def bases(every):
        split = rank + rank // 2
        low = jnp.concatenate(
            [jnp.zeros((count, 2 * rank), BF), every[:, rank : rank + rank // 2]], axis=1
        )
        high = jnp.concatenate([every[:, 2 * rank :], every[:, split : 2 * rank]], axis=1)
        return jnp.where(core == 0, low, high)

    def right_side(every, base, scaled, pull):
        direct = jnp.concatenate(
            [every[:, :rank], scaled, jnp.zeros((count, rank // 2), BF)], axis=1
        )
        pulled = (-pull * base.astype(F32)).astype(BF)
        return jnp.where(core == 0, direct, 0) + pulled

    far = {}
    for s in (3, 2, 1):
        back_pre, scaled, pull = local(back)
        pushed = dot(back_pre, mixes[:, :rank], ((1,), (0,)))
        pushed = (inverse * pushed - pull * cross[:, :rank]).astype(BF)
        came = send(pushed, shifted(-1, s))
        if s > 1:
            pushed = dot(back_pre, mixes[:, rank : s * rank], ((1,), (0,)))
            pushed = (inverse * pushed - pull * cross[:, rank : s * rank]).astype(BF)
            for d in range(2, s + 1):
                far[s, s - d] = send(pushed[:, (d - 2) * rank : (d - 1) * rank], shifted(-d, s))
        if s == 3:
            came, acts = barrier((came, acts))
            every = jnp.concatenate([act] + acts, axis=1)
            every_s = send(every, mate_core)
        if s == 2:
            came, every_s = barrier((came, every_s))
            base_m, base_s = bases(every), bases(every_s)
        if s == 1:
            came, base_m, base_s = barrier((came, base_m, base_s))
        back = back + came.astype(F32)
        for k in range(s + 1, SECTIONS):
            back = back + far[k, s - 1].astype(F32)
    back_pre, scaled, pull = local(back)
    scaled = scaled.astype(BF)

    wire = jnp.concatenate(
        [scaled, jnp.broadcast_to(pull, (count, rank // 2)).astype(BF)], axis=1
    )
    wire_s = send(wire, mate_core)
    blocks = moved_blocks(rows_of(wire), down, hidden_rows, section)
    wire_s, blocks = barrier((wire_s, blocks))

    def features_of(which):
        came = [blocks[which]]
        for turn in range(1, SECTIONS):
            came.append(send(blocks[2 * turn + which], turned(turn)))
        return came

    scaled_s, pull_s = wire_s[:, :rank], wire_s[:, rank : rank + 1].astype(F32)
    joint = dot(scaled, base_m, ((0,), (0,))) + dot(scaled_s, base_s, ((0,), (0,)))
    sums = outer_products(
        hidden,
        hidden_s,
        cot,
        cot_s,
        right_side(every, base_m, scaled, pull),
        right_side(every_s, base_s, scaled_s, pull_s),
        down,
        joint.astype(BF),
    )
    sums, front = barrier((sums, features_of(0)))
    (own, other), rear = scatter_ring(*sums, features_of(1))

    feature = [[], [], []]
    for level in range(LEVELS):
        for rows, blocks in ((cot_rows[: cot_rows.shape[0] // 2], front), (cot_rows[cot_rows.shape[0] // 2 :], rear)):
            total = rows.astype(F32)
            for turn in range(SECTIONS):
                origin = (section - turn) % SECTIONS
                total = total + jnp.where(origin > level, blocks[turn].astype(F32), 0.0)
            feature[level].append(total.astype(BF).reshape(micro // 2, -1, part))
    feature_grads = jnp.stack([jnp.concatenate(pieces, axis=0) for pieces in feature])

    zero = jnp.where(core == 0, own, other)
    one = jnp.where(core == 0, other, own)
    down_grad = (zero[:, rank : 2 * rank] * factor)[None]
    near = jnp.concatenate([zero[:, 2 * rank :], one[:, 2 * rank :]], axis=1)
    up_sum = zero[:, :rank]
    for d, piece in ((1, near), (2, one[:, :rank]), (3, one[:, rank : 2 * rank])):
        up_sum = up_sum + send(piece, shifted(-d))
    up_grad = (up_sum.T * factor)[None]
    return (down_grad, up_grad, feature_grads)


def solution(mesh):
    placed = (
        P("pipe", None, "dp", None),
        P(None, "dp", None),
        P("pipe", "dp", None),
        P("pipe", None, "dp"),
        P(None, "dp"),
    )
    return jax.shard_map(
        on_device,
        mesh=mesh,
        in_specs=placed,
        out_specs=(P("pipe", "dp", None), P("pipe", None, "dp"), P(None, None, "dp", "pipe")),
        check_vma=False,
    )
```

```python
import jax
import jax.numpy as jnp
from jax import lax
from jax.experimental import pallas as pl
from jax.experimental.pallas import tpu as pltpu
from jax.sharding import PartitionSpec as P

LEVELS = 3
SIDE = 4
SECTIONS = 4
AXES = ("dp", "pipe")
BF = jnp.bfloat16
F32 = jnp.float32
VMEM_BYTES = 48 * 1024 * 1024
barrier = lax.optimization_barrier


def route(target):
    pairs = []
    for x in range(SIDE):
        for y in range(SIDE):
            for z in range(2):
                for c in range(2):
                    for s in range(SECTIONS):
                        to = target(x, y, z, c, s)
                        if to is None:
                            continue
                        tx, ty, tz, tc, ts = to
                        source = (((x * SIDE + y) * 2 + z) * 2 + c) * SECTIONS + s
                        dest = (((tx * SIDE + ty) * 2 + tz) * 2 + tc) * SECTIONS + ts
                        pairs.append((source, dest))
    return pairs


def send(block, target):
    return lax.ppermute(block, AXES, route(target))


def mate_z(x, y, z, c, s):
    return (x, y, 1 - z, c, s)


def mate_core(x, y, z, c, s):
    return (x, y, z, 1 - c, s)


def mate_cross(x, y, z, c, s):
    return (x, y, 1 - z, 1 - c, s)


def mate_x(mask):
    def target(x, y, z, c, s):
        return (((((x + c) % SIDE) ^ mask) - c) % SIDE, y, z, c, s)

    return target


def mate_y(mask):
    def target(x, y, z, c, s):
        return (x, ((((y + c) % SIDE) ^ mask) - c) % SIDE, z, c, s)

    return target


def shifted(distance, only=None):
    def target(x, y, z, c, s):
        if only is not None and s != only:
            return None
        if not 0 <= s + distance < SECTIONS:
            return None
        return (x, y, z, c, s + distance)

    return target


def between(*pairs):
    def target(x, y, z, c, s):
        goal = dict(pairs).get(s)
        return None if goal is None else (x, y, z, c, goal)

    return target


def turned(distance):
    def target(x, y, z, c, s):
        if s == 0:
            return None
        return (x, y, z, c, (s + distance) % SECTIONS)

    return target


def both(mine, theirs, bit, axis):
    low = jnp.where(bit == 0, mine, theirs)
    high = jnp.where(bit == 0, theirs, mine)
    return jnp.concatenate([low, high], axis=axis)


def place():
    index = lax.axis_index("dp")
    core = index % 2
    z = (index // 2) % 2
    y = (index // 4) % SIDE
    x = index // (4 * SIDE)
    return x, y, z, core


def gather_ring(blocks):
    x, y, z, core = place()
    xs = (x + core) % SIDE
    ys = (y + core) % SIDE
    halves = []
    for color, block in enumerate(blocks):
        first, second = ((xs, mate_x), (ys, mate_y)) if color == 0 else ((ys, mate_y), (xs, mate_x))
        now = block[None, None]
        for axis, (label, mate) in ((1, first), (0, second)):
            now = both(now, send(now, mate(1)), label % 2, axis)
            far = send(now, mate(3))
            if axis == 1:
                now = both(now, far, label // 2, axis)
        halves += [now, far]
    return halves


def halve(now, label, mate, axis):
    for mask, bit, size in ((3, label // 2, 2), (1, label % 2, 1)):
        kept = lax.dynamic_slice_in_dim(now, bit * size, size, axis)
        away = lax.dynamic_slice_in_dim(now, (1 - bit) * size, size, axis)
        now = kept + send(away.astype(BF), mate(mask)).astype(F32)
    return now


def halve_rest(kept, away, label, mate, axis):
    now = kept.astype(F32) + send(away, mate(3)).astype(F32)
    low = lax.dynamic_slice_in_dim(now, label % 2, 1, axis)
    high = lax.dynamic_slice_in_dim(now, 1 - label % 2, 1, axis)
    return low + send(high.astype(BF), mate(1)).astype(F32)


def scatter_ring(kept_a, away_a, kept_b, away_b, beside):
    x, y, z, core = place()
    xs = (x + core) % SIDE
    ys = (y + core) % SIDE
    first = halve_rest(kept_a, away_a, xs, mate_x, 0)
    second = halve_rest(kept_b, away_b, ys, mate_y, 1)
    first, second, beside = barrier((first, second, beside))
    first = halve(first, ys, mate_y, 1)[0, 0]
    second = halve(second, xs, mate_x, 0)[0, 0]
    cols = first.shape[1]
    mine = jnp.where(z == 0, first, second).reshape(2, -1, cols)
    away = jnp.where(z == 0, second, first).astype(BF).reshape(2, -1, cols)
    own = lax.dynamic_index_in_dim(mine, core, 0, False)
    own = own + send(lax.dynamic_index_in_dim(away, core, 0, False), mate_z).astype(F32)
    other = send(lax.dynamic_index_in_dim(mine, 1 - core, 0, False), mate_core)
    cross = send(lax.dynamic_index_in_dim(away, 1 - core, 0, False), mate_cross)
    return (own, other + cross.astype(F32)), beside


def dot(a, b, contract):
    return lax.dot_general(a, b, ((contract[0], contract[1]), ((), ())), preferred_element_type=F32)


def step_label(i, half):
    return 2 * jnp.where(i < 2, half, 1 - half) + i % 2


def inner_kernel(
    rank, where_ref, hm_ref, hs_ref, tm_ref, ts_ref, am_ref, at_ref, bm_ref, bt_ref,
    down_ref, raw_ref, nm_ref, ns_ref, um_ref, us_ref, mixed_ref, square_ref, weights,
):
    core, half_y = where_ref[0], where_ref[2]
    step = pl.program_id(0)
    rows = am_ref.shape[2]
    for y in range(SIDE):
        label = lax.rem(core + y, SIDE)
        odd = lax.rem(label, 2)
        weights[pl.ds(2 * y * rows, rows), :] = jnp.where(
            label // 2 == half_y, am_ref[odd, 0], at_ref[odd, 0]
        )
        weights[pl.ds((2 * y + 1) * rows, rows), :] = jnp.where(
            step < 2, bm_ref[0, label], bt_ref[0, label]
        )
    down = weights[:, :rank]
    second = weights[:, rank : 2 * rank]
    third = weights[:, 2 * rank :]
    down_ref[...] = down
    hm, hs = hm_ref[...], hs_ref[...]
    tm = jnp.where(core == 0, tm_ref[...], hm)
    ts = jnp.where(core == 0, ts_ref[...], hs)
    wide = hm.astype(F32)
    results = (
        (raw_ref, dot(hm, down, ((1,), (0,)))),
        (nm_ref, dot(hm, second, ((1,), (0,)))),
        (ns_ref, dot(hs, second, ((1,), (0,)))),
        (um_ref, dot(tm, third, ((1,), (0,)))),
        (us_ref, dot(ts, third, ((1,), (0,)))),
        (mixed_ref, dot(down, weights[:, rank:], ((0,), (0,)))),
        (square_ref, jnp.sum(wide * wide, axis=1, keepdims=True)),
    )

    @pl.when(step == 0)
    def _():
        for ref, value in results:
            ref[...] = value

    @pl.when(step > 0)
    def _():
        for ref, value in results:
            ref[...] += value


def position():
    x, y, z, core = place()
    return jnp.stack([core, (x + core) % SIDE // 2, (y + core) % SIDE // 2]).astype(jnp.int32)


def inner_products(hidden, hidden_s, cot, cot_s, ring, rank):
    count, width = hidden.shape
    part = width // SIDE
    rows, cols = ring[0].shape[2:]

    def label(i, w):
        return step_label(i, w[1])

    def block(i, w):
        return (label(i, w) + SIDE - w[0]) % SIDE

    first = pl.BlockSpec((count, part), lambda i, w: (0, block(i, w)))
    third = pl.BlockSpec((count, part), lambda i, w: (0, (1 - w[0]) * block(i, w)))
    one = pl.BlockSpec((2, 1, rows, cols), lambda i, w: (0, label(i, w), 0, 0))
    whole = lambda shape: pl.BlockSpec(shape, lambda i, w: (0, 0))
    small = (count, rank)
    shapes = [small] * 5 + [(rank, 2 * rank), (count, 1)]
    return pl.pallas_call(
        lambda *refs: inner_kernel(rank, *refs),
        grid_spec=pltpu.PrefetchScalarGridSpec(
            num_scalar_prefetch=1,
            grid=(SIDE,),
            in_specs=[
                first,
                first,
                third,
                third,
                one,
                one,
                pl.BlockSpec((1, SIDE, rows, cols), lambda i, w: (jnp.minimum(i, 1), 0, 0, 0)),
                pl.BlockSpec((1, SIDE, rows, cols), lambda i, w: (jnp.maximum(i - 2, 0), 0, 0, 0)),
            ],
            out_specs=[pl.BlockSpec((part, rank), lambda i, w: (block(i, w), 0))]
            + [whole(s) for s in shapes],
            scratch_shapes=[pltpu.VMEM((part, cols), BF)],
        ),
        out_shape=[jax.ShapeDtypeStruct((width, rank), BF)]
        + [jax.ShapeDtypeStruct(s, F32) for s in shapes],
        compiler_params=pltpu.CompilerParams(vmem_limit_bytes=VMEM_BYTES),
        cost_estimate=pl.CostEstimate(
            flops=2 * width * rank * (5 * count + 2 * rank),
            bytes_accessed=2 * width * (4 * count + cols + rank),
            transcendentals=0,
        ),
        name="inner_products",
    )(position(), hidden, hidden_s, cot, cot_s, *ring)


def outer_kernel(
    rank, where_ref, hm_ref, hs_ref, tm_ref, ts_ref, rm_ref, rs_ref, down_ref, joint_ref,
    kept_a, away_a, kept_b, away_b, total,
):
    core, half_y = where_ref[0], where_ref[2]
    rows = total.shape[1]
    chunk = 4 * rows
    cols = joint_ref.shape[1]
    for half in range(2):
        span = pl.ds(half * chunk, chunk)
        inner = dot(down_ref[span, :], joint_ref[...], ((1,), (0,)))
        hm, hs = hm_ref[:, span], hs_ref[:, span]
        tm = jnp.where(core == 0, tm_ref[:, span], hm)
        ts = jnp.where(core == 0, ts_ref[:, span], hs)
        left = dot(tm, rm_ref[:, :rank], ((0,), (0,)))
        left = left + dot(ts, rs_ref[:, :rank], ((0,), (0,)))
        right = dot(hm, rm_ref[:, rank:], ((0,), (0,)))
        right = right + dot(hs, rs_ref[:, rank:], ((0,), (0,)))
        left = (left + inner[:, :rank]).astype(BF)
        right = (right + inner[:, rank:]).astype(BF)
        for k in range(4):
            total[half * 4 + k, :, :rank] = left[k * rows : (k + 1) * rows]
            total[half * 4 + k, :, rank:] = right[k * rows : (k + 1) * rows]
    for t in range(SIDE):
        y = lax.rem(t + SIDE - core, SIDE)
        value = total[2 * y]

        @pl.when(pl.program_id(0) < 2)
        def _():
            away_a[0, t] = value

        @pl.when(pl.program_id(0) >= 2)
        def _():
            kept_a[0, t] = value

    for t in range(2):
        y = lax.rem(2 * half_y + t + SIDE - core, SIDE)
        kept_b[0, t] = total[2 * y + 1]
        y = lax.rem(2 * (1 - half_y) + t + SIDE - core, SIDE)
        away_b[0, t] = total[2 * y + 1]


def outer_products(hidden, hidden_s, cot, cot_s, right, right_sibling, down, joint):
    count, width = hidden.shape
    rank, cols = joint.shape
    part = width // SIDE
    rows = part // (2 * SIDE)

    def label(i, w):
        return step_label(i, 1 - w[1])

    def block(i, w):
        return (label(i, w) + SIDE - w[0]) % SIDE

    first = pl.BlockSpec((count, part), lambda i, w: (0, block(i, w)))
    third = pl.BlockSpec((count, part), lambda i, w: (0, (1 - w[0]) * block(i, w)))
    same = lambda shape: pl.BlockSpec(shape, lambda i, w: (0, 0))
    return pl.pallas_call(
        lambda *refs: outer_kernel(rank, *refs),
        grid_spec=pltpu.PrefetchScalarGridSpec(
            num_scalar_prefetch=1,
            grid=(SIDE,),
            in_specs=[
                first,
                first,
                third,
                third,
                same(right.shape),
                same(right.shape),
                pl.BlockSpec((part, rank), lambda i, w: (block(i, w), 0)),
                same(joint.shape),
            ],
            out_specs=[
                pl.BlockSpec((1, SIDE, rows, cols), lambda i, w: (jnp.maximum(i - 2, 0), 0, 0, 0)),
                pl.BlockSpec((1, SIDE, rows, cols), lambda i, w: (jnp.minimum(i, 1), 0, 0, 0)),
                pl.BlockSpec((1, 2, rows, cols), lambda i, w: (label(i, w), 0, 0, 0)),
                pl.BlockSpec((1, 2, rows, cols), lambda i, w: (label(i, w), 0, 0, 0)),
            ],
            scratch_shapes=[pltpu.VMEM((2 * SIDE, rows, cols), BF)],
        ),
        out_shape=[jax.ShapeDtypeStruct((2, SIDE, rows, cols), BF)] * 2
        + [jax.ShapeDtypeStruct((SIDE, 2, rows, cols), BF)] * 2,
        compiler_params=pltpu.CompilerParams(vmem_limit_bytes=VMEM_BYTES),
        cost_estimate=pl.CostEstimate(
            flops=2 * width * cols * (2 * count + rank),
            bytes_accessed=2 * width * (4 * count + cols + rank),
            transcendentals=0,
        ),
        name="outer_products",
    )(position(), hidden, hidden_s, cot, cot_s, right, right_sibling, down, joint)


def moved_kernel(rank, place_ref, picked_ref, down_ref, rows_ref, *outs):
    pull = picked_ref[:, rank : rank + 1].astype(F32)
    value = dot(picked_ref[:, :rank], down_ref[...], ((1,), (1,)))
    value = (value - pull * rows_ref[...].astype(F32)).astype(BF)
    half = value.shape[0] // 2
    for t in range(SECTIONS):

        @pl.when(pl.program_id(0) == t)
        def _():
            outs[2 * t][...] = value[:half]
            outs[2 * t + 1][...] = value[half:]


def moved_blocks(picked, down, rows, section):
    count, width = rows.shape
    rank = down.shape[1]
    part = width // SECTIONS
    half = jax.ShapeDtypeStruct((count // 2, part), BF)
    return pl.pallas_call(
        lambda *refs: moved_kernel(rank, *refs),
        grid_spec=pltpu.PrefetchScalarGridSpec(
            num_scalar_prefetch=1,
            grid=(SECTIONS,),
            in_specs=[
                pl.BlockSpec(picked.shape, lambda t, w: (0, 0)),
                pl.BlockSpec((part, rank), lambda t, w: ((w[0] + t) % SECTIONS, 0)),
                pl.BlockSpec((count, part), lambda t, w: (0, (w[0] + t) % SECTIONS)),
            ],
            out_specs=[pl.BlockSpec(half.shape, lambda t, w: (0, 0))] * (2 * SECTIONS),
        ),
        out_shape=[half] * (2 * SECTIONS),
        compiler_params=pltpu.CompilerParams(vmem_limit_bytes=VMEM_BYTES),
        cost_estimate=pl.CostEstimate(
            flops=2 * count * width * rank, bytes_accessed=4 * count * width, transcendentals=0
        ),
        name="moved_blocks",
    )(section.astype(jnp.int32).reshape(1), picked, down, rows)


def on_device(saved_inputs, cotangent, adapter_down, adapter_up, image_rows):
    section = lax.axis_index("pipe")
    x, y, z, core = place()
    micro, tokens, width = cotangent.shape
    rank = adapter_down.shape[2]
    count = micro * tokens
    factor = (count * lax.axis_size("dp")) ** (-0.5)
    hidden = saved_inputs.reshape(count, width)
    cot = cotangent.reshape(count, width)

    up_shard = adapter_up[0].T
    extra = [send(up_shard, shifted(d)) for d in (1, 2, 3)]
    sets = [
        jnp.concatenate([adapter_down[0], extra[0], up_shard], axis=1),
        jnp.concatenate([adapter_down[0], extra[1], extra[2]], axis=1),
    ]
    mine = jnp.where(core == 0, sets[0], sets[1])
    away = jnp.where(core == 0, sets[1], sets[0])
    by_z = send(mine, mate_z)
    by_core = send(away, mate_core)
    by_both = send(away, mate_cross)
    here = both(mine, by_core, core, 0)
    there = both(by_z, by_both, core, 0)
    blocks = [jnp.where(z == 0, here, there), jnp.where(z == 0, there, here)]
    hidden, cot, blocks = barrier((hidden, cot, blocks))
    hidden_s = send(hidden, mate_core)
    cot_s = send(cot, mate_core)
    ring = gather_ring(blocks)

    picks = (image_rows[:, :, None] == jnp.arange(tokens, dtype=jnp.int32)).astype(BF)

    def rows_of(array):
        array = array.reshape(micro, tokens, -1)
        out = lax.dot_general(picks, array, (((2,), (1,)), ((0,), (0,))), preferred_element_type=F32)
        return out.reshape(-1, out.shape[-1]).astype(BF)

    part = width // SECTIONS
    hidden_rows = rows_of(hidden)
    cot_rows = rows_of(lax.dynamic_slice_in_dim(cot, section * part, part, 1))
    ring, hidden_rows, cot_rows = barrier((ring, hidden_rows, cot_rows))

    down, raw, near_m, near_s, last_m, last_s, mixed, square = inner_products(
        hidden, hidden_s, cot, cot_s, ring, rank
    )
    swap = jnp.concatenate([jnp.concatenate([near_s, last_s], axis=1), mixed], axis=0).astype(BF)
    swap = send(swap, mate_core)
    inverse = lax.rsqrt(square / width + 1e-06)
    pre = inverse * raw
    sigma = jax.nn.sigmoid(pre)
    act = (pre * sigma).astype(BF)
    slope = sigma * (1.0 + pre * (1.0 - sigma))
    came = swap[:count].astype(F32)
    back = jnp.where(core == 0, last_m, came[:, rank:])
    cross = jnp.concatenate(
        [
            jnp.where(core == 0, near_m, came[:, :rank]),
            jnp.where(core == 0, came[:, :rank], near_m),
            jnp.where(core == 0, came[:, rank:], last_m),
        ],
        axis=1,
    )
    ours = mixed.astype(BF)
    theirs = swap[count:]
    mixes = jnp.concatenate(
        [jnp.where(core == 0, ours, theirs)[:, :rank], jnp.where(core == 0, theirs, ours)], axis=1
    )

    def local(back):
        back_pre = (back * slope).astype(BF)
        wide = back_pre.astype(F32)
        along = jnp.sum(wide * pre, axis=-1, keepdims=True) / width
        return back_pre, wide * inverse, along * inverse * inverse

    def bases(every):
        split = rank + rank // 2
        low = jnp.concatenate(
            [jnp.zeros((count, 2 * rank), BF), every[:, rank : rank + rank // 2]], axis=1
        )
        high = jnp.concatenate([every[:, 2 * rank :], every[:, split : 2 * rank]], axis=1)
        return jnp.where(core == 0, low, high)

    def right_side(every, base, scaled, pull):
        direct = jnp.concatenate(
            [every[:, :rank], scaled, jnp.zeros((count, rank // 2), BF)], axis=1
        )
        pulled = (-pull * base.astype(F32)).astype(BF)
        return jnp.where(core == 0, direct, 0) + pulled

    def push(back_pre, pull, low, high):
        pushed = dot(back_pre, mixes[:, low * rank : high * rank], ((1,), (0,)))
        return (inverse * pushed - pull * cross[:, low * rank : high * rank]).astype(BF)

    back_pre, scaled, pull = local(back)
    near, act = barrier((push(back_pre, pull, 0, 1), act))
    came = send(near, between((3, 2)))
    far = push(back_pre, pull, 1, 3)
    hop = send(far[:, :rank], between((3, 0)))
    one_back = send(act, shifted(1))
    three_back = send(act, shifted(3))
    came, one_back, three_back = barrier((came, one_back, three_back))
    back = back + came.astype(F32)
    back_pre, scaled, pull = local(back)
    turn = jnp.where(section == 2, push(back_pre, pull, 1, 2), far[:, rank:])
    turn = jnp.where(section == 0, hop, turn)
    two_back = jnp.where(section == 2, one_back, three_back)
    near, turn, two_back = barrier((push(back_pre, pull, 0, 1), turn, two_back))
    came = send(near, between((2, 1)))
    turn = send(turn, between((0, 1), (2, 3), (3, 0)))
    two_back = send(two_back, between((2, 3), (3, 2)))
    came, turn, two_back = barrier((came, turn, two_back))
    back = back + came.astype(F32) + jnp.where(section == 3, 0.0, turn.astype(F32))
    back_pre, scaled, pull = local(back)
    every = jnp.concatenate([act, one_back, two_back, three_back], axis=1)
    near, turn, every = barrier((push(back_pre, pull, 0, 1), turn, every))
    came = send(near, between((1, 0)))
    turn = send(turn, between((3, 0)))
    every_s = send(every, mate_core)
    base_m, base_s = bases(every), bases(every_s)
    came, turn, base_m, base_s = barrier((came, turn, base_m, base_s))
    back = back + came.astype(F32) + turn.astype(F32)
    back_pre, scaled, pull = local(back)
    scaled = scaled.astype(BF)

    wire = jnp.concatenate(
        [scaled, jnp.broadcast_to(pull, (count, rank // 2)).astype(BF)], axis=1
    )
    wire_s = send(wire, mate_core)
    blocks = moved_blocks(rows_of(wire), down, hidden_rows, section)
    wire_s, blocks = barrier((wire_s, blocks))

    def features_of(which):
        came = [blocks[which]]
        for turn in range(1, SECTIONS):
            came.append(send(blocks[2 * turn + which], turned(turn)))
        return came

    scaled_s, pull_s = wire_s[:, :rank], wire_s[:, rank : rank + 1].astype(F32)
    joint = dot(scaled, base_m, ((0,), (0,))) + dot(scaled_s, base_s, ((0,), (0,)))
    sums = outer_products(
        hidden,
        hidden_s,
        cot,
        cot_s,
        right_side(every, base_m, scaled, pull),
        right_side(every_s, base_s, scaled_s, pull_s),
        down,
        joint.astype(BF),
    )
    sums, front = barrier((sums, features_of(0)))
    (own, other), rear = scatter_ring(*sums, features_of(1))

    feature = [[], [], []]
    for level in range(LEVELS):
        for rows, blocks in ((cot_rows[: cot_rows.shape[0] // 2], front), (cot_rows[cot_rows.shape[0] // 2 :], rear)):
            total = rows.astype(F32)
            for turn in range(SECTIONS):
                origin = (section - turn) % SECTIONS
                total = total + jnp.where(origin > level, blocks[turn].astype(F32), 0.0)
            feature[level].append(total.astype(BF).reshape(micro // 2, -1, part))
    feature_grads = jnp.stack([jnp.concatenate(pieces, axis=0) for pieces in feature])

    zero = jnp.where(core == 0, own, other)
    one = jnp.where(core == 0, other, own)
    down_grad = (zero[:, rank : 2 * rank] * factor)[None]
    near = jnp.concatenate([zero[:, 2 * rank :], one[:, 2 * rank :]], axis=1)
    up_sum = zero[:, :rank]
    for d, piece in ((1, near), (2, one[:, :rank]), (3, one[:, rank : 2 * rank])):
        up_sum = up_sum + send(piece, shifted(-d))
    up_grad = (up_sum.T * factor)[None]
    return (down_grad, up_grad, feature_grads)


def solution(mesh):
    placed = (
        P("pipe", None, "dp", None),
        P(None, "dp", None),
        P("pipe", "dp", None),
        P("pipe", None, "dp"),
        P(None, "dp"),
    )
    return jax.shard_map(
        on_device,
        mesh=mesh,
        in_specs=placed,
        out_specs=(P("pipe", "dp", None), P("pipe", None, "dp"), P(None, None, "dp", "pipe")),
        check_vma=False,
    )
```

```python
import jax
import jax.numpy as jnp
from jax import lax
from jax.experimental import pallas as pl
from jax.experimental.pallas import tpu as pltpu
from jax.sharding import PartitionSpec as P

LEVELS = 3
SIDE = 4
SECTIONS = 4
AXES = ("dp", "pipe")
BF = jnp.bfloat16
F32 = jnp.float32
VMEM_BYTES = 48 * 1024 * 1024
barrier = lax.optimization_barrier


def route(target):
    pairs = []
    for x in range(SIDE):
        for y in range(SIDE):
            for z in range(2):
                for c in range(2):
                    for s in range(SECTIONS):
                        to = target(x, y, z, c, s)
                        if to is None:
                            continue
                        tx, ty, tz, tc, ts = to
                        source = (((x * SIDE + y) * 2 + z) * 2 + c) * SECTIONS + s
                        dest = (((tx * SIDE + ty) * 2 + tz) * 2 + tc) * SECTIONS + ts
                        pairs.append((source, dest))
    return pairs


def send(block, target):
    return lax.ppermute(block, AXES, route(target))


def mate_z(x, y, z, c, s):
    return (x, y, 1 - z, c, s)


def mate_core(x, y, z, c, s):
    return (x, y, z, 1 - c, s)


def mate_cross(x, y, z, c, s):
    return (x, y, 1 - z, 1 - c, s)


def mate_x(mask):
    def target(x, y, z, c, s):
        return (((((x + c) % SIDE) ^ mask) - c) % SIDE, y, z, c, s)

    return target


def mate_y(mask):
    def target(x, y, z, c, s):
        return (x, ((((y + c) % SIDE) ^ mask) - c) % SIDE, z, c, s)

    return target


def shifted(distance, only=None):
    def target(x, y, z, c, s):
        if only is not None and s != only:
            return None
        if not 0 <= s + distance < SECTIONS:
            return None
        return (x, y, z, c, s + distance)

    return target


def between(*pairs):
    def target(x, y, z, c, s):
        goal = dict(pairs).get(s)
        return None if goal is None else (x, y, z, c, goal)

    return target


def turned(distance):
    def target(x, y, z, c, s):
        if s == 0:
            return None
        return (x, y, z, c, (s + distance) % SECTIONS)

    return target


def both(mine, theirs, bit, axis):
    low = jnp.where(bit == 0, mine, theirs)
    high = jnp.where(bit == 0, theirs, mine)
    return jnp.concatenate([low, high], axis=axis)


def place():
    index = lax.axis_index("dp")
    core = index % 2
    z = (index // 2) % 2
    y = (index // 4) % SIDE
    x = index // (4 * SIDE)
    return x, y, z, core


def gather_ring(blocks):
    x, y, z, core = place()
    xs = (x + core) % SIDE
    ys = (y + core) % SIDE
    halves = []
    for color, block in enumerate(blocks):
        first, second = ((xs, mate_x), (ys, mate_y)) if color == 0 else ((ys, mate_y), (xs, mate_x))
        now = block[None, None]
        for axis, (label, mate) in ((1, first), (0, second)):
            now = both(now, send(now, mate(1)), label % 2, axis)
            far = send(now, mate(3))
            if axis == 1:
                now = both(now, far, label // 2, axis)
        halves += [now, far]
    return halves


def halve(now, label, mate, axis):
    for mask, bit, size in ((3, label // 2, 2), (1, label % 2, 1)):
        kept = lax.dynamic_slice_in_dim(now, bit * size, size, axis)
        away = lax.dynamic_slice_in_dim(now, (1 - bit) * size, size, axis)
        now = kept + send(away.astype(BF), mate(mask)).astype(F32)
    return now


def halve_rest(kept, away, label, mate, axis):
    now = kept.astype(F32) + send(away, mate(3)).astype(F32)
    low = lax.dynamic_slice_in_dim(now, label % 2, 1, axis)
    high = lax.dynamic_slice_in_dim(now, 1 - label % 2, 1, axis)
    return low + send(high.astype(BF), mate(1)).astype(F32)


def scatter_ring(kept_a, away_a, kept_b, away_b, beside):
    x, y, z, core = place()
    xs = (x + core) % SIDE
    ys = (y + core) % SIDE
    first = halve_rest(kept_a, away_a, xs, mate_x, 0)
    second = halve_rest(kept_b, away_b, ys, mate_y, 1)
    first, second, beside = barrier((first, second, beside))
    first = halve(first, ys, mate_y, 1)[0, 0]
    second = halve(second, xs, mate_x, 0)[0, 0]
    cols = first.shape[1]
    mine = jnp.where(z == 0, first, second).reshape(2, -1, cols)
    away = jnp.where(z == 0, second, first).astype(BF).reshape(2, -1, cols)
    own = lax.dynamic_index_in_dim(mine, core, 0, False)
    own = own + send(lax.dynamic_index_in_dim(away, core, 0, False), mate_z).astype(F32)
    other = send(lax.dynamic_index_in_dim(mine, 1 - core, 0, False), mate_core)
    cross = send(lax.dynamic_index_in_dim(away, 1 - core, 0, False), mate_cross)
    return (own, other + cross.astype(F32)), beside


def dot(a, b, contract):
    return lax.dot_general(a, b, ((contract[0], contract[1]), ((), ())), preferred_element_type=F32)


def step_label(i, half):
    return 2 * jnp.where(i < 2, half, 1 - half) + i % 2


def inner_kernel(
    rank, where_ref, hm_ref, hs_ref, tm_ref, ts_ref, am_ref, at_ref, bm_ref, bt_ref,
    down_ref, pre_ref, slope_ref, act_ref, inverse_ref, nm_ref, um_ref, mixed_ref, swap_ref,
    weights, raw_ref, ns_ref, us_ref, blend_ref, square_ref,
):
    core, half_y = where_ref[0], where_ref[2]
    step = pl.program_id(0)
    rows = am_ref.shape[2]
    for y in range(SIDE):
        label = lax.rem(core + y, SIDE)
        odd = lax.rem(label, 2)
        weights[pl.ds(2 * y * rows, rows), :] = jnp.where(
            label // 2 == half_y, am_ref[odd, 0], at_ref[odd, 0]
        )
        weights[pl.ds((2 * y + 1) * rows, rows), :] = jnp.where(
            step < 2, bm_ref[0, label], bt_ref[0, label]
        )
    down = weights[:, :rank]
    second = weights[:, rank : 2 * rank]
    third = weights[:, 2 * rank :]
    down_ref[...] = down
    hm, hs = hm_ref[...], hs_ref[...]
    tm = jnp.where(core == 0, tm_ref[...], hm)
    ts = jnp.where(core == 0, ts_ref[...], hs)
    wide = hm.astype(F32)
    results = (
        (raw_ref, dot(hm, down, ((1,), (0,)))),
        (nm_ref, dot(hm, second, ((1,), (0,)))),
        (ns_ref, dot(hs, second, ((1,), (0,)))),
        (um_ref, dot(tm, third, ((1,), (0,)))),
        (us_ref, dot(ts, third, ((1,), (0,)))),
        (blend_ref, dot(down, weights[:, rank:], ((0,), (0,)))),
        (square_ref, jnp.sum(wide * wide, axis=1, keepdims=True)),
    )

    @pl.when(step == 0)
    def _():
        for ref, value in results:
            ref[...] = value

    @pl.when(step > 0)
    def _():
        for ref, value in results:
            ref[...] += value

    @pl.when(step == SIDE - 1)
    def _():
        count = hm_ref.shape[0]
        inverse = lax.rsqrt(square_ref[...] / (hm_ref.shape[1] * SIDE) + 1e-06)
        pre = inverse * raw_ref[...]
        sigma = 1.0 / (1.0 + jnp.exp(-pre))
        pre_ref[...] = pre
        inverse_ref[...] = inverse
        slope_ref[...] = sigma * (1.0 + pre * (1.0 - sigma))
        act_ref[...] = (pre * sigma).astype(BF)
        mixed = blend_ref[...].astype(BF)
        mixed_ref[...] = mixed
        swap_ref[:count, :rank] = ns_ref[...].astype(BF)
        swap_ref[:count, rank:] = us_ref[...].astype(BF)
        swap_ref[count:, :] = mixed


def position():
    x, y, z, core = place()
    return jnp.stack([core, (x + core) % SIDE // 2, (y + core) % SIDE // 2]).astype(jnp.int32)


def inner_products(hidden, hidden_s, cot, cot_s, ring, rank):
    count, width = hidden.shape
    part = width // SIDE
    rows, cols = ring[0].shape[2:]

    def label(i, w):
        return step_label(i, w[1])

    def block(i, w):
        return (label(i, w) + SIDE - w[0]) % SIDE

    first = pl.BlockSpec((count, part), lambda i, w: (0, block(i, w)))
    third = pl.BlockSpec((count, part), lambda i, w: (0, (1 - w[0]) * block(i, w)))
    one = pl.BlockSpec((2, 1, rows, cols), lambda i, w: (0, label(i, w), 0, 0))
    whole = lambda shape: pl.BlockSpec(shape, lambda i, w: (0, 0))
    small = (count, rank)
    shapes = [
        (small, F32),
        (small, F32),
        (small, BF),
        ((count, 1), F32),
        (small, F32),
        (small, F32),
        ((rank, 2 * rank), BF),
        ((count + rank, 2 * rank), BF),
    ]
    return pl.pallas_call(
        lambda *refs: inner_kernel(rank, *refs),
        grid_spec=pltpu.PrefetchScalarGridSpec(
            num_scalar_prefetch=1,
            grid=(SIDE,),
            in_specs=[
                first,
                first,
                third,
                third,
                one,
                one,
                pl.BlockSpec((1, SIDE, rows, cols), lambda i, w: (jnp.minimum(i, 1), 0, 0, 0)),
                pl.BlockSpec((1, SIDE, rows, cols), lambda i, w: (jnp.maximum(i - 2, 0), 0, 0, 0)),
            ],
            out_specs=[pl.BlockSpec((part, rank), lambda i, w: (block(i, w), 0))]
            + [whole(shape) for shape, _ in shapes],
            scratch_shapes=[pltpu.VMEM((part, cols), BF)]
            + [pltpu.VMEM(small, F32)] * 3
            + [pltpu.VMEM((rank, 2 * rank), F32), pltpu.VMEM((count, 1), F32)],
        ),
        out_shape=[jax.ShapeDtypeStruct((width, rank), BF)]
        + [jax.ShapeDtypeStruct(shape, dtype) for shape, dtype in shapes],
        compiler_params=pltpu.CompilerParams(vmem_limit_bytes=VMEM_BYTES),
        cost_estimate=pl.CostEstimate(
            flops=2 * width * rank * (5 * count + 2 * rank),
            bytes_accessed=2 * width * (4 * count + cols + rank),
            transcendentals=0,
        ),
        name="inner_products",
    )(position(), hidden, hidden_s, cot, cot_s, *ring)


def outer_kernel(
    rank, where_ref, hm_ref, hs_ref, tm_ref, ts_ref, rm_ref, rs_ref, down_ref, joint_ref,
    kept_a, away_a, kept_b, away_b, total,
):
    core, half_y = where_ref[0], where_ref[2]
    rows = total.shape[1]
    chunk = 4 * rows
    cols = joint_ref.shape[1]
    for half in range(2):
        span = pl.ds(half * chunk, chunk)
        inner = dot(down_ref[span, :], joint_ref[...], ((1,), (0,)))
        hm, hs = hm_ref[:, span], hs_ref[:, span]
        tm = jnp.where(core == 0, tm_ref[:, span], hm)
        ts = jnp.where(core == 0, ts_ref[:, span], hs)
        left = dot(tm, rm_ref[:, :rank], ((0,), (0,)))
        left = left + dot(ts, rs_ref[:, :rank], ((0,), (0,)))
        right = dot(hm, rm_ref[:, rank:], ((0,), (0,)))
        right = right + dot(hs, rs_ref[:, rank:], ((0,), (0,)))
        left = (left + inner[:, :rank]).astype(BF)
        right = (right + inner[:, rank:]).astype(BF)
        for k in range(4):
            total[half * 4 + k, :, :rank] = left[k * rows : (k + 1) * rows]
            total[half * 4 + k, :, rank:] = right[k * rows : (k + 1) * rows]
    for t in range(SIDE):
        y = lax.rem(t + SIDE - core, SIDE)
        value = total[2 * y]

        @pl.when(pl.program_id(0) < 2)
        def _():
            away_a[0, t] = value

        @pl.when(pl.program_id(0) >= 2)
        def _():
            kept_a[0, t] = value

    for t in range(2):
        y = lax.rem(2 * half_y + t + SIDE - core, SIDE)
        kept_b[0, t] = total[2 * y + 1]
        y = lax.rem(2 * (1 - half_y) + t + SIDE - core, SIDE)
        away_b[0, t] = total[2 * y + 1]


def outer_products(hidden, hidden_s, cot, cot_s, right, right_sibling, down, joint):
    count, width = hidden.shape
    rank, cols = joint.shape
    part = width // SIDE
    rows = part // (2 * SIDE)

    def label(i, w):
        return step_label(i, 1 - w[1])

    def block(i, w):
        return (label(i, w) + SIDE - w[0]) % SIDE

    first = pl.BlockSpec((count, part), lambda i, w: (0, block(i, w)))
    third = pl.BlockSpec((count, part), lambda i, w: (0, (1 - w[0]) * block(i, w)))
    same = lambda shape: pl.BlockSpec(shape, lambda i, w: (0, 0))
    return pl.pallas_call(
        lambda *refs: outer_kernel(rank, *refs),
        grid_spec=pltpu.PrefetchScalarGridSpec(
            num_scalar_prefetch=1,
            grid=(SIDE,),
            in_specs=[
                first,
                first,
                third,
                third,
                same(right.shape),
                same(right.shape),
                pl.BlockSpec((part, rank), lambda i, w: (block(i, w), 0)),
                same(joint.shape),
            ],
            out_specs=[
                pl.BlockSpec((1, SIDE, rows, cols), lambda i, w: (jnp.maximum(i - 2, 0), 0, 0, 0)),
                pl.BlockSpec((1, SIDE, rows, cols), lambda i, w: (jnp.minimum(i, 1), 0, 0, 0)),
                pl.BlockSpec((1, 2, rows, cols), lambda i, w: (label(i, w), 0, 0, 0)),
                pl.BlockSpec((1, 2, rows, cols), lambda i, w: (label(i, w), 0, 0, 0)),
            ],
            scratch_shapes=[pltpu.VMEM((2 * SIDE, rows, cols), BF)],
        ),
        out_shape=[jax.ShapeDtypeStruct((2, SIDE, rows, cols), BF)] * 2
        + [jax.ShapeDtypeStruct((SIDE, 2, rows, cols), BF)] * 2,
        compiler_params=pltpu.CompilerParams(vmem_limit_bytes=VMEM_BYTES),
        cost_estimate=pl.CostEstimate(
            flops=2 * width * cols * (2 * count + rank),
            bytes_accessed=2 * width * (4 * count + cols + rank),
            transcendentals=0,
        ),
        name="outer_products",
    )(position(), hidden, hidden_s, cot, cot_s, right, right_sibling, down, joint)


def step_values(width, back, pre, slope, inverse):
    back_pre = (back * slope).astype(BF)
    wide = back_pre.astype(F32)
    pull = jnp.sum(wide * pre, axis=1, keepdims=True) / width * inverse * inverse
    return back_pre, wide, pull


def start_kernel(
    width, flag_ref, pre_ref, slope_ref, inverse_ref, near_ref, last_ref, mixed_ref, came_ref,
    back_ref, cross_ref, mixes_ref, step_ref, pull_ref, push_ref,
):
    count, rank = pre_ref.shape
    zero = flag_ref[0] == 0
    came = came_ref[:count, :].astype(F32)
    back = jnp.where(zero, last_ref[...], came[:, rank:])
    cross = jnp.where(zero, near_ref[...], came[:, :rank])
    cross_ref[:, :rank] = cross
    cross_ref[:, rank : 2 * rank] = jnp.where(zero, came[:, :rank], near_ref[...])
    cross_ref[:, 2 * rank :] = jnp.where(zero, came[:, rank:], last_ref[...])
    ours, theirs = mixed_ref[...], came_ref[count:, :]
    mix = jnp.where(zero, ours[:, :rank], theirs[:, :rank])
    mixes_ref[:, :rank] = mix
    mixes_ref[:, rank:] = jnp.where(zero, theirs, ours)
    inverse = inverse_ref[...]
    back_pre, wide, pull = step_values(width, back, pre_ref[...], slope_ref[...], inverse)
    back_ref[...] = back
    step_ref[...] = back_pre
    pull_ref[...] = pull
    push_ref[...] = (inverse * dot(back_pre, mix, ((1,), (0,))) - pull * cross).astype(BF)


def link_kernel(
    width, last, flag_ref, back_ref, one_ref, two_ref, pre_ref, slope_ref, inverse_ref, cross_ref,
    mixes_ref, *outs,
):
    rank = pre_ref.shape[1]
    gain = flag_ref[1].astype(F32)
    back = back_ref[...] + one_ref[...].astype(F32) + gain * two_ref[...].astype(F32)
    inverse = inverse_ref[...]
    back_pre, wide, pull = step_values(width, back, pre_ref[...], slope_ref[...], inverse)
    if last:
        wire_ref, pull_ref = outs
        wire_ref[:, :rank] = (wide * inverse).astype(BF)
        wire_ref[:, rank:] = jnp.broadcast_to(pull, (back.shape[0], rank // 2)).astype(BF)
        pull_ref[...] = pull
        return
    out_ref, step_ref, pull_ref, push_ref = outs
    out_ref[...] = back
    step_ref[...] = back_pre
    pull_ref[...] = pull
    pushed = inverse * dot(back_pre, mixes_ref[:, :rank], ((1,), (0,)))
    push_ref[...] = (pushed - pull * cross_ref[:, :rank]).astype(BF)


def small_call(kernel, name, flags, operands, shapes):
    whole = lambda shape: pl.BlockSpec(shape, lambda i, flags: (0, 0))
    return pl.pallas_call(
        kernel,
        grid_spec=pltpu.PrefetchScalarGridSpec(
            num_scalar_prefetch=1,
            grid=(1,),
            in_specs=[whole(operand.shape) for operand in operands],
            out_specs=[whole(shape) for shape, _ in shapes],
        ),
        out_shape=[jax.ShapeDtypeStruct(shape, dtype) for shape, dtype in shapes],
        compiler_params=pltpu.CompilerParams(vmem_limit_bytes=VMEM_BYTES),
        name=name,
    )(flags, *operands)


def moved_kernel(rank, place_ref, picked_ref, down_ref, rows_ref, *outs):
    pull = picked_ref[:, rank : rank + 1].astype(F32)
    value = dot(picked_ref[:, :rank], down_ref[...], ((1,), (1,)))
    value = (value - pull * rows_ref[...].astype(F32)).astype(BF)
    half = value.shape[0] // 2
    for t in range(SECTIONS):

        @pl.when(pl.program_id(0) == t)
        def _():
            outs[2 * t][...] = value[:half]
            outs[2 * t + 1][...] = value[half:]


def moved_blocks(picked, down, rows, section):
    count, width = rows.shape
    rank = down.shape[1]
    part = width // SECTIONS
    half = jax.ShapeDtypeStruct((count // 2, part), BF)
    return pl.pallas_call(
        lambda *refs: moved_kernel(rank, *refs),
        grid_spec=pltpu.PrefetchScalarGridSpec(
            num_scalar_prefetch=1,
            grid=(SECTIONS,),
            in_specs=[
                pl.BlockSpec(picked.shape, lambda t, w: (0, 0)),
                pl.BlockSpec((part, rank), lambda t, w: ((w[0] + t) % SECTIONS, 0)),
                pl.BlockSpec((count, part), lambda t, w: (0, (w[0] + t) % SECTIONS)),
            ],
            out_specs=[pl.BlockSpec(half.shape, lambda t, w: (0, 0))] * (2 * SECTIONS),
        ),
        out_shape=[half] * (2 * SECTIONS),
        compiler_params=pltpu.CompilerParams(vmem_limit_bytes=VMEM_BYTES),
        cost_estimate=pl.CostEstimate(
            flops=2 * count * width * rank, bytes_accessed=4 * count * width, transcendentals=0
        ),
        name="moved_blocks",
    )(section.astype(jnp.int32).reshape(1), picked, down, rows)


def on_device(saved_inputs, cotangent, adapter_down, adapter_up, image_rows):
    section = lax.axis_index("pipe")
    x, y, z, core = place()
    micro, tokens, width = cotangent.shape
    rank = adapter_down.shape[2]
    count = micro * tokens
    factor = (count * lax.axis_size("dp")) ** (-0.5)
    hidden = saved_inputs.reshape(count, width)
    cot = cotangent.reshape(count, width)

    up_shard = adapter_up[0].T
    extra = [send(up_shard, shifted(d)) for d in (1, 2, 3)]
    sets = [
        jnp.concatenate([adapter_down[0], extra[0], up_shard], axis=1),
        jnp.concatenate([adapter_down[0], extra[1], extra[2]], axis=1),
    ]
    mine = jnp.where(core == 0, sets[0], sets[1])
    away = jnp.where(core == 0, sets[1], sets[0])
    by_z = send(mine, mate_z)
    by_core = send(away, mate_core)
    by_both = send(away, mate_cross)
    here = both(mine, by_core, core, 0)
    there = both(by_z, by_both, core, 0)
    blocks = [jnp.where(z == 0, here, there), jnp.where(z == 0, there, here)]
    hidden, cot, blocks = barrier((hidden, cot, blocks))
    hidden_s = send(hidden, mate_core)
    cot_s = send(cot, mate_core)
    ring = gather_ring(blocks)

    picks = (image_rows[:, :, None] == jnp.arange(tokens, dtype=jnp.int32)).astype(BF)

    def rows_of(array):
        array = array.reshape(micro, tokens, -1)
        out = lax.dot_general(picks, array, (((2,), (1,)), ((0,), (0,))), preferred_element_type=F32)
        return out.reshape(-1, out.shape[-1]).astype(BF)

    part = width // SECTIONS
    hidden_rows = rows_of(hidden)
    cot_rows = rows_of(lax.dynamic_slice_in_dim(cot, section * part, part, 1))
    ring, hidden_rows, cot_rows = barrier((ring, hidden_rows, cot_rows))

    down, pre, slope, act, inverse, near_m, last_m, mixed, swap = inner_products(
        hidden, hidden_s, cot, cot_s, ring, rank
    )
    swap = send(swap, mate_core)
    flags = jnp.stack([core, (section != 3).astype(jnp.int32)]).astype(jnp.int32)
    plain = jnp.stack([core, jnp.int32(1)]).astype(jnp.int32)
    square = (count, rank)
    step_shapes = [(square, BF), ((count, 1), F32), (square, BF)]
    back, cross, mixes, back_pre, pull, near = small_call(
        lambda *refs: start_kernel(width, *refs),
        "start",
        flags,
        [pre, slope, inverse, near_m, last_m, mixed, swap],
        [(square, F32), ((count, 3 * rank), F32), ((rank, 3 * rank), BF)] + step_shapes,
    )

    def link(flags, back, one, two, last):
        shapes = [(square, F32)] + step_shapes
        if last:
            shapes = [((count, rank + rank // 2), BF), ((count, 1), F32)]
        return small_call(
            lambda *refs: link_kernel(width, last, *refs),
            "last" if last else "link",
            flags,
            [back, one, two, pre, slope, inverse, cross, mixes],
            shapes,
        )

    def bases(every):
        split = rank + rank // 2
        low = jnp.concatenate(
            [jnp.zeros((count, 2 * rank), BF), every[:, rank : rank + rank // 2]], axis=1
        )
        high = jnp.concatenate([every[:, 2 * rank :], every[:, split : 2 * rank]], axis=1)
        return jnp.where(core == 0, low, high)

    def right_side(every, base, scaled, pull):
        direct = jnp.concatenate(
            [every[:, :rank], scaled, jnp.zeros((count, rank // 2), BF)], axis=1
        )
        pulled = (-pull * base.astype(F32)).astype(BF)
        return jnp.where(core == 0, direct, 0) + pulled

    def push(back_pre, pull, low, high):
        pushed = dot(back_pre, mixes[:, low * rank : high * rank], ((1,), (0,)))
        return (inverse * pushed - pull * cross[:, low * rank : high * rank]).astype(BF)

    came = send(near, between((3, 2)))
    far = push(back_pre, pull, 1, 3)
    far, act = barrier((far, act))
    hop = send(far[:, :rank], between((3, 0)))
    one_back = send(act, shifted(1))
    three_back = send(act, shifted(3))
    back, back_pre, pull, near = link(plain, back, came, jnp.zeros(square, BF), False)
    came = send(near, between((2, 1)))
    turn = jnp.where(section == 2, push(back_pre, pull, 1, 2), far[:, rank:])
    turn = jnp.where(section == 0, hop, turn)
    turn = send(turn, between((0, 1), (2, 3), (3, 0)))
    came, turn, one_back, three_back = barrier((came, turn, one_back, three_back))
    back, back_pre, pull, near = link(flags, back, came, turn, False)
    came = send(near, between((1, 0)))
    near, turn, two_back = barrier((near, turn, jnp.where(section == 2, one_back, three_back)))
    turn = send(turn, between((3, 0)))
    two_back = send(two_back, between((2, 3), (3, 2)))
    came, turn, two_back = barrier((came, turn, two_back))
    wire, pull = link(plain, back, came, turn, True)
    every = jnp.concatenate([act, one_back, two_back, three_back], axis=1)
    wire, every = barrier((wire, every))
    wire_s = send(wire, mate_core)
    every_s = send(every, mate_core)
    base_m = bases(every)
    blocks = moved_blocks(rows_of(wire), down, hidden_rows, section)
    wire_s, every_s, base_m, blocks = barrier((wire_s, every_s, base_m, blocks))
    base_s = bases(every_s)
    scaled = wire[:, :rank]

    def features_of(which):
        came = [blocks[which]]
        for turn in range(1, SECTIONS):
            came.append(send(blocks[2 * turn + which], turned(turn)))
        return came

    scaled_s, pull_s = wire_s[:, :rank], wire_s[:, rank : rank + 1].astype(F32)
    joint = dot(scaled, base_m, ((0,), (0,))) + dot(scaled_s, base_s, ((0,), (0,)))
    sums = outer_products(
        hidden,
        hidden_s,
        cot,
        cot_s,
        right_side(every, base_m, scaled, pull),
        right_side(every_s, base_s, scaled_s, pull_s),
        down,
        joint.astype(BF),
    )
    sums, front = barrier((sums, features_of(0)))
    (own, other), rear = scatter_ring(*sums, features_of(1))

    feature = [[], [], []]
    for level in range(LEVELS):
        for rows, blocks in ((cot_rows[: cot_rows.shape[0] // 2], front), (cot_rows[cot_rows.shape[0] // 2 :], rear)):
            total = rows.astype(F32)
            for turn in range(SECTIONS):
                origin = (section - turn) % SECTIONS
                total = total + jnp.where(origin > level, blocks[turn].astype(F32), 0.0)
            feature[level].append(total.astype(BF).reshape(micro // 2, -1, part))
    feature_grads = jnp.stack([jnp.concatenate(pieces, axis=0) for pieces in feature])

    zero = jnp.where(core == 0, own, other)
    one = jnp.where(core == 0, other, own)
    down_grad = (zero[:, rank : 2 * rank] * factor)[None]
    near = jnp.concatenate([zero[:, 2 * rank :], one[:, 2 * rank :]], axis=1)
    up_sum = zero[:, :rank]
    for d, piece in ((1, near), (2, one[:, :rank]), (3, one[:, rank : 2 * rank])):
        up_sum = up_sum + send(piece, shifted(-d))
    up_grad = (up_sum.T * factor)[None]
    return (down_grad, up_grad, feature_grads)


def solution(mesh):
    placed = (
        P("pipe", None, "dp", None),
        P(None, "dp", None),
        P("pipe", "dp", None),
        P("pipe", None, "dp"),
        P(None, "dp"),
    )
    return jax.shard_map(
        on_device,
        mesh=mesh,
        in_specs=placed,
        out_specs=(P("pipe", "dp", None), P("pipe", None, "dp"), P(None, None, "dp", "pipe")),
        check_vma=False,
    )
```

```python
import jax
import jax.numpy as jnp
from jax import lax
from jax.experimental import pallas as pl
from jax.experimental.pallas import tpu as pltpu
from jax.sharding import PartitionSpec as P

LEVELS = 3
SIDE = 4
SECTIONS = 4
AXES = ("dp", "pipe")
BF = jnp.bfloat16
F32 = jnp.float32
VMEM_BYTES = 48 * 1024 * 1024
barrier = lax.optimization_barrier


def route(target):
    pairs = []
    for x in range(SIDE):
        for y in range(SIDE):
            for z in range(2):
                for c in range(2):
                    for s in range(SECTIONS):
                        to = target(x, y, z, c, s)
                        if to is None:
                            continue
                        tx, ty, tz, tc, ts = to
                        source = (((x * SIDE + y) * 2 + z) * 2 + c) * SECTIONS + s
                        dest = (((tx * SIDE + ty) * 2 + tz) * 2 + tc) * SECTIONS + ts
                        pairs.append((source, dest))
    return pairs


def send(block, target):
    return lax.ppermute(block, AXES, route(target))


def mate_z(x, y, z, c, s):
    return (x, y, 1 - z, c, s)


def mate_core(x, y, z, c, s):
    return (x, y, z, 1 - c, s)


def mate_cross(x, y, z, c, s):
    return (x, y, 1 - z, 1 - c, s)


def mate_x(mask):
    def target(x, y, z, c, s):
        return (((((x + c) % SIDE) ^ mask) - c) % SIDE, y, z, c, s)

    return target


def mate_y(mask):
    def target(x, y, z, c, s):
        return (x, ((((y + c) % SIDE) ^ mask) - c) % SIDE, z, c, s)

    return target


def shifted(distance, only=None):
    def target(x, y, z, c, s):
        if only is not None and s != only:
            return None
        if not 0 <= s + distance < SECTIONS:
            return None
        return (x, y, z, c, s + distance)

    return target


def between(*pairs):
    def target(x, y, z, c, s):
        goal = dict(pairs).get(s)
        return None if goal is None else (x, y, z, c, goal)

    return target


def turned(distance):
    def target(x, y, z, c, s):
        if s == 0:
            return None
        return (x, y, z, c, (s + distance) % SECTIONS)

    return target


def both(mine, theirs, bit, axis):
    low = jnp.where(bit == 0, mine, theirs)
    high = jnp.where(bit == 0, theirs, mine)
    return jnp.concatenate([low, high], axis=axis)


def place():
    index = lax.axis_index("dp")
    core = index % 2
    z = (index // 2) % 2
    y = (index // 4) % SIDE
    x = index // (4 * SIDE)
    return x, y, z, core


def gather_ring(blocks):
    x, y, z, core = place()
    xs = (x + core) % SIDE
    ys = (y + core) % SIDE
    halves = []
    for color, block in enumerate(blocks):
        first, second = ((xs, mate_x), (ys, mate_y)) if color == 0 else ((ys, mate_y), (xs, mate_x))
        now = block[None, None]
        for axis, (label, mate) in ((1, first), (0, second)):
            now = both(now, send(now, mate(1)), label % 2, axis)
            far = send(now, mate(3))
            if axis == 1:
                now = both(now, far, label // 2, axis)
        halves += [now, far]
    return halves


def halve(now, label, mate, axis):
    for mask, bit, size in ((3, label // 2, 2), (1, label % 2, 1)):
        kept = lax.dynamic_slice_in_dim(now, bit * size, size, axis)
        away = lax.dynamic_slice_in_dim(now, (1 - bit) * size, size, axis)
        now = kept + send(away.astype(BF), mate(mask)).astype(F32)
    return now


def halve_rest(kept, away, label, mate, axis):
    now = kept.astype(F32) + send(away, mate(3)).astype(F32)
    low = lax.dynamic_slice_in_dim(now, label % 2, 1, axis)
    high = lax.dynamic_slice_in_dim(now, 1 - label % 2, 1, axis)
    return low + send(high.astype(BF), mate(1)).astype(F32)


def scatter_ring(kept_a, away_a, kept_b, away_b, beside):
    x, y, z, core = place()
    xs = (x + core) % SIDE
    ys = (y + core) % SIDE
    first = halve_rest(kept_a, away_a, xs, mate_x, 0)
    second = halve_rest(kept_b, away_b, ys, mate_y, 1)
    first, second, beside = barrier((first, second, beside))
    first = halve(first, ys, mate_y, 1)[0, 0]
    second = halve(second, xs, mate_x, 0)[0, 0]
    cols = first.shape[1]
    mine = jnp.where(z == 0, first, second).reshape(2, -1, cols)
    away = jnp.where(z == 0, second, first).astype(BF).reshape(2, -1, cols)
    own = lax.dynamic_index_in_dim(mine, core, 0, False)
    own = own + send(lax.dynamic_index_in_dim(away, core, 0, False), mate_z).astype(F32)
    other = send(lax.dynamic_index_in_dim(mine, 1 - core, 0, False), mate_core)
    cross = send(lax.dynamic_index_in_dim(away, 1 - core, 0, False), mate_cross)
    return (own, other + cross.astype(F32)), beside


def dot(a, b, contract):
    return lax.dot_general(a, b, ((contract[0], contract[1]), ((), ())), preferred_element_type=F32)


def step_label(i, half):
    return 2 * jnp.where(i < 2, half, 1 - half) + i % 2


def inner_kernel(
    rank, where_ref, hm_ref, hs_ref, tm_ref, ts_ref, am_ref, at_ref, bm_ref, bt_ref, inverse_ref,
    down_ref, pre_ref, slope_ref, act_ref, nm_ref, um_ref, mixed_ref, swap_ref,
    weights, raw_ref, ns_ref, us_ref, blend_ref,
):
    core, half_y = where_ref[0], where_ref[2]
    step = pl.program_id(0)
    rows = am_ref.shape[2]
    for y in range(SIDE):
        label = lax.rem(core + y, SIDE)
        odd = lax.rem(label, 2)
        weights[pl.ds(2 * y * rows, rows), :] = jnp.where(
            label // 2 == half_y, am_ref[odd, 0], at_ref[odd, 0]
        )
        weights[pl.ds((2 * y + 1) * rows, rows), :] = jnp.where(
            step < 2, bm_ref[0, label], bt_ref[0, label]
        )
    down = weights[:, :rank]
    second = weights[:, rank : 2 * rank]
    third = weights[:, 2 * rank :]
    down_ref[...] = down
    hm, hs = hm_ref[...], hs_ref[...]

    @pl.when(step == 0)
    def _():
        for ref in (raw_ref, nm_ref, ns_ref, um_ref, us_ref, blend_ref):
            ref[...] = jnp.zeros_like(ref)

    raw_ref[...] += dot(hm, down, ((1,), (0,)))
    nm_ref[...] += dot(hm, second, ((1,), (0,)))
    ns_ref[...] += dot(hs, second, ((1,), (0,)))
    blend_ref[...] += dot(down, weights[:, rank:], ((0,), (0,)))

    @pl.when(core == 0)
    def _():
        um_ref[...] += dot(tm_ref[...], third, ((1,), (0,)))
        us_ref[...] += dot(ts_ref[...], third, ((1,), (0,)))

    @pl.when(core != 0)
    def _():
        um_ref[...] += dot(hm, third, ((1,), (0,)))
        us_ref[...] += dot(hs, third, ((1,), (0,)))

    @pl.when(step == SIDE - 1)
    def _():
        count = hm_ref.shape[0]
        pre = inverse_ref[...] * raw_ref[...]
        sigma = 1.0 / (1.0 + jnp.exp(-pre))
        pre_ref[...] = pre
        slope_ref[...] = sigma * (1.0 + pre * (1.0 - sigma))
        act_ref[...] = (pre * sigma).astype(BF)
        mixed = blend_ref[...].astype(BF)
        mixed_ref[...] = mixed
        swap_ref[:count, :rank] = ns_ref[...].astype(BF)
        swap_ref[:count, rank:] = us_ref[...].astype(BF)
        swap_ref[count:, :] = mixed


def position():
    x, y, z, core = place()
    return jnp.stack([core, (x + core) % SIDE // 2, (y + core) % SIDE // 2]).astype(jnp.int32)


def inner_products(hidden, hidden_s, cot, cot_s, ring, inverse, rank):
    count, width = hidden.shape
    part = width // SIDE
    rows, cols = ring[0].shape[2:]

    def label(i, w):
        return step_label(i, w[1])

    def block(i, w):
        return (label(i, w) + SIDE - w[0]) % SIDE

    first = pl.BlockSpec((count, part), lambda i, w: (0, block(i, w)))
    third = pl.BlockSpec((count, part), lambda i, w: (0, (1 - w[0]) * block(i, w)))
    one = pl.BlockSpec((2, 1, rows, cols), lambda i, w: (0, label(i, w), 0, 0))
    whole = lambda shape: pl.BlockSpec(shape, lambda i, w: (0, 0))
    small = (count, rank)
    shapes = [
        (small, F32),
        (small, F32),
        (small, BF),
        (small, F32),
        (small, F32),
        ((rank, 2 * rank), BF),
        ((count + rank, 2 * rank), BF),
    ]
    return pl.pallas_call(
        lambda *refs: inner_kernel(rank, *refs),
        grid_spec=pltpu.PrefetchScalarGridSpec(
            num_scalar_prefetch=1,
            grid=(SIDE,),
            in_specs=[
                first,
                first,
                third,
                third,
                one,
                one,
                pl.BlockSpec((1, SIDE, rows, cols), lambda i, w: (jnp.minimum(i, 1), 0, 0, 0)),
                pl.BlockSpec((1, SIDE, rows, cols), lambda i, w: (jnp.maximum(i - 2, 0), 0, 0, 0)),
                whole((count, 1)),
            ],
            out_specs=[pl.BlockSpec((part, rank), lambda i, w: (block(i, w), 0))]
            + [whole(shape) for shape, _ in shapes],
            scratch_shapes=[pltpu.VMEM((part, cols), BF)]
            + [pltpu.VMEM(small, F32)] * 3
            + [pltpu.VMEM((rank, 2 * rank), F32)],
        ),
        out_shape=[jax.ShapeDtypeStruct((width, rank), BF)]
        + [jax.ShapeDtypeStruct(shape, dtype) for shape, dtype in shapes],
        compiler_params=pltpu.CompilerParams(vmem_limit_bytes=VMEM_BYTES),
        cost_estimate=pl.CostEstimate(
            flops=2 * width * rank * (5 * count + 2 * rank),
            bytes_accessed=2 * width * (4 * count + cols + rank),
            transcendentals=0,
        ),
        name="inner_products",
    )(position(), hidden, hidden_s, cot, cot_s, *ring, inverse)


def outer_kernel(
    rank, where_ref, hm_ref, hs_ref, tm_ref, ts_ref, rm_ref, rs_ref, down_ref, joint_ref,
    kept_a, away_a, kept_b, away_b, total,
):
    core, half_y = where_ref[0], where_ref[2]
    rows = total.shape[1]
    chunk = 4 * rows
    cols = joint_ref.shape[1]
    for half in range(2):
        span = pl.ds(half * chunk, chunk)
        inner = dot(down_ref[span, :], joint_ref[...], ((1,), (0,)))

        def keep(value, low, high):
            value = (value + inner[:, low:high]).astype(BF)
            for k in range(4):
                total[half * 4 + k, :, low:high] = value[k * rows : (k + 1) * rows]

        @pl.when(core == 0)
        def _():
            left = dot(tm_ref[:, span], rm_ref[:, :rank], ((0,), (0,)))
            left = left + dot(ts_ref[:, span], rs_ref[:, :rank], ((0,), (0,)))
            keep(left, 0, rank)
            right = dot(hm_ref[:, span], rm_ref[:, rank:], ((0,), (0,)))
            right = right + dot(hs_ref[:, span], rs_ref[:, rank:], ((0,), (0,)))
            keep(right, rank, cols)

        @pl.when(core != 0)
        def _():
            whole = dot(hm_ref[:, span], rm_ref[...], ((0,), (0,)))
            whole = whole + dot(hs_ref[:, span], rs_ref[...], ((0,), (0,)))
            keep(whole, 0, cols)

    for t in range(SIDE):
        y = lax.rem(t + SIDE - core, SIDE)
        value = total[2 * y]

        @pl.when(pl.program_id(0) < 2)
        def _():
            away_a[0, t] = value

        @pl.when(pl.program_id(0) >= 2)
        def _():
            kept_a[0, t] = value

    for t in range(2):
        y = lax.rem(2 * half_y + t + SIDE - core, SIDE)
        kept_b[0, t] = total[2 * y + 1]
        y = lax.rem(2 * (1 - half_y) + t + SIDE - core, SIDE)
        away_b[0, t] = total[2 * y + 1]


def outer_products(hidden, hidden_s, cot, cot_s, right, right_sibling, down, joint):
    count, width = hidden.shape
    rank, cols = joint.shape
    part = width // SIDE
    rows = part // (2 * SIDE)

    def label(i, w):
        return step_label(i, 1 - w[1])

    def block(i, w):
        return (label(i, w) + SIDE - w[0]) % SIDE

    first = pl.BlockSpec((count, part), lambda i, w: (0, block(i, w)))
    third = pl.BlockSpec((count, part), lambda i, w: (0, (1 - w[0]) * block(i, w)))
    same = lambda shape: pl.BlockSpec(shape, lambda i, w: (0, 0))
    return pl.pallas_call(
        lambda *refs: outer_kernel(rank, *refs),
        grid_spec=pltpu.PrefetchScalarGridSpec(
            num_scalar_prefetch=1,
            grid=(SIDE,),
            in_specs=[
                first,
                first,
                third,
                third,
                same(right.shape),
                same(right.shape),
                pl.BlockSpec((part, rank), lambda i, w: (block(i, w), 0)),
                same(joint.shape),
            ],
            out_specs=[
                pl.BlockSpec((1, SIDE, rows, cols), lambda i, w: (jnp.maximum(i - 2, 0), 0, 0, 0)),
                pl.BlockSpec((1, SIDE, rows, cols), lambda i, w: (jnp.minimum(i, 1), 0, 0, 0)),
                pl.BlockSpec((1, 2, rows, cols), lambda i, w: (label(i, w), 0, 0, 0)),
                pl.BlockSpec((1, 2, rows, cols), lambda i, w: (label(i, w), 0, 0, 0)),
            ],
            scratch_shapes=[pltpu.VMEM((2 * SIDE, rows, cols), BF)],
        ),
        out_shape=[jax.ShapeDtypeStruct((2, SIDE, rows, cols), BF)] * 2
        + [jax.ShapeDtypeStruct((SIDE, 2, rows, cols), BF)] * 2,
        compiler_params=pltpu.CompilerParams(vmem_limit_bytes=VMEM_BYTES),
        cost_estimate=pl.CostEstimate(
            flops=2 * width * cols * (2 * count + rank),
            bytes_accessed=2 * width * (4 * count + cols + rank),
            transcendentals=0,
        ),
        name="outer_products",
    )(position(), hidden, hidden_s, cot, cot_s, right, right_sibling, down, joint)


def step_values(width, back, pre, slope, inverse):
    back_pre = (back * slope).astype(BF)
    wide = back_pre.astype(F32)
    pull = jnp.sum(wide * pre, axis=1, keepdims=True) / width * inverse * inverse
    return back_pre, wide, pull


def start_kernel(
    width, flag_ref, pre_ref, slope_ref, inverse_ref, near_ref, last_ref, mixed_ref, came_ref,
    back_ref, cross_ref, mixes_ref, step_ref, pull_ref, push_ref,
):
    count, rank = pre_ref.shape
    zero = flag_ref[0] == 0
    came = came_ref[:count, :].astype(F32)
    back = jnp.where(zero, last_ref[...], came[:, rank:])
    cross = jnp.where(zero, near_ref[...], came[:, :rank])
    cross_ref[:, :rank] = cross
    cross_ref[:, rank : 2 * rank] = jnp.where(zero, came[:, :rank], near_ref[...])
    cross_ref[:, 2 * rank :] = jnp.where(zero, came[:, rank:], last_ref[...])
    ours, theirs = mixed_ref[...], came_ref[count:, :]
    mix = jnp.where(zero, ours[:, :rank], theirs[:, :rank])
    mixes_ref[:, :rank] = mix
    mixes_ref[:, rank:] = jnp.where(zero, theirs, ours)
    inverse = inverse_ref[...]
    back_pre, wide, pull = step_values(width, back, pre_ref[...], slope_ref[...], inverse)
    back_ref[...] = back
    step_ref[...] = back_pre
    pull_ref[...] = pull
    push_ref[...] = (inverse * dot(back_pre, mix, ((1,), (0,))) - pull * cross).astype(BF)


def link_kernel(
    width, pushes, flag_ref, back_ref, *refs
):
    came, (pre_ref, slope_ref, inverse_ref, cross_ref, mixes_ref, *outs) = refs[:3], refs[3:]
    rank = pre_ref.shape[1]
    back = back_ref[...]
    for ref in came:
        back = back + ref[...].astype(F32)
    inverse = inverse_ref[...]
    back_pre, wide, pull = step_values(width, back, pre_ref[...], slope_ref[...], inverse)
    if not pushes:
        wire_ref, pull_ref = outs
        wire_ref[:, :rank] = (wide * inverse).astype(BF)
        wire_ref[:, rank:] = jnp.broadcast_to(pull, (back.shape[0], rank // 2)).astype(BF)
        pull_ref[...] = pull
        return
    outs[0][...] = back
    for k in range(pushes):
        span = pl.ds(k * rank, rank)
        pushed = inverse * dot(back_pre, mixes_ref[:, span], ((1,), (0,)))
        outs[1 + k][...] = (pushed - pull * cross_ref[:, span]).astype(BF)


def small_call(kernel, name, flags, operands, shapes):
    whole = lambda shape: pl.BlockSpec(shape, lambda i, flags: (0, 0))
    return pl.pallas_call(
        kernel,
        grid_spec=pltpu.PrefetchScalarGridSpec(
            num_scalar_prefetch=1,
            grid=(1,),
            in_specs=[whole(operand.shape) for operand in operands],
            out_specs=[whole(shape) for shape, _ in shapes],
        ),
        out_shape=[jax.ShapeDtypeStruct(shape, dtype) for shape, dtype in shapes],
        compiler_params=pltpu.CompilerParams(vmem_limit_bytes=VMEM_BYTES),
        name=name,
    )(flags, *operands)


def moved_kernel(rank, place_ref, picked_ref, down_ref, rows_ref, *outs):
    pull = picked_ref[:, rank : rank + 1].astype(F32)
    value = dot(picked_ref[:, :rank], down_ref[...], ((1,), (1,)))
    value = (value - pull * rows_ref[...].astype(F32)).astype(BF)
    half = value.shape[0] // 2
    for t in range(SECTIONS):

        @pl.when(pl.program_id(0) == t)
        def _():
            outs[2 * t][...] = value[:half]
            outs[2 * t + 1][...] = value[half:]


def moved_blocks(picked, down, rows, section):
    count, width = rows.shape
    rank = down.shape[1]
    part = width // SECTIONS
    half = jax.ShapeDtypeStruct((count // 2, part), BF)
    return pl.pallas_call(
        lambda *refs: moved_kernel(rank, *refs),
        grid_spec=pltpu.PrefetchScalarGridSpec(
            num_scalar_prefetch=1,
            grid=(SECTIONS,),
            in_specs=[
                pl.BlockSpec(picked.shape, lambda t, w: (0, 0)),
                pl.BlockSpec((part, rank), lambda t, w: ((w[0] + t) % SECTIONS, 0)),
                pl.BlockSpec((count, part), lambda t, w: (0, (w[0] + t) % SECTIONS)),
            ],
            out_specs=[pl.BlockSpec(half.shape, lambda t, w: (0, 0))] * (2 * SECTIONS),
        ),
        out_shape=[half] * (2 * SECTIONS),
        compiler_params=pltpu.CompilerParams(vmem_limit_bytes=VMEM_BYTES),
        cost_estimate=pl.CostEstimate(
            flops=2 * count * width * rank, bytes_accessed=4 * count * width, transcendentals=0
        ),
        name="moved_blocks",
    )(section.astype(jnp.int32).reshape(1), picked, down, rows)


def on_device(saved_inputs, cotangent, adapter_down, adapter_up, image_rows):
    section = lax.axis_index("pipe")
    x, y, z, core = place()
    micro, tokens, width = cotangent.shape
    rank = adapter_down.shape[2]
    count = micro * tokens
    factor = (count * lax.axis_size("dp")) ** (-0.5)
    hidden = saved_inputs.reshape(count, width)
    cot = cotangent.reshape(count, width)

    up_shard = adapter_up[0].T
    extra = [send(up_shard, shifted(d)) for d in (1, 2, 3)]
    sets = [
        jnp.concatenate([adapter_down[0], extra[0], up_shard], axis=1),
        jnp.concatenate([adapter_down[0], extra[1], extra[2]], axis=1),
    ]
    mine = jnp.where(core == 0, sets[0], sets[1])
    away = jnp.where(core == 0, sets[1], sets[0])
    by_z = send(mine, mate_z)
    by_core = send(away, mate_core)
    by_both = send(away, mate_cross)
    here = both(mine, by_core, core, 0)
    there = both(by_z, by_both, core, 0)
    blocks = [jnp.where(z == 0, here, there), jnp.where(z == 0, there, here)]
    hidden, cot, blocks = barrier((hidden, cot, blocks))
    hidden_s = send(hidden, mate_core)
    cot_s = send(cot, mate_core)
    ring = gather_ring(blocks)

    picks = (image_rows[:, :, None] == jnp.arange(tokens, dtype=jnp.int32)).astype(BF)

    def rows_of(array):
        array = array.reshape(micro, tokens, -1)
        out = lax.dot_general(picks, array, (((2,), (1,)), ((0,), (0,))), preferred_element_type=F32)
        return out.reshape(-1, out.shape[-1]).astype(BF)

    part = width // SECTIONS
    hidden_rows = rows_of(hidden)
    cot_rows = rows_of(lax.dynamic_slice_in_dim(cot, section * part, part, 1))
    wide = hidden.astype(F32)
    inverse = lax.rsqrt(jnp.mean(wide * wide, axis=1, keepdims=True) + 1e-06)
    ring, hidden_rows, cot_rows, inverse = barrier((ring, hidden_rows, cot_rows, inverse))

    down, pre, slope, act, near_m, last_m, mixed, swap = inner_products(
        hidden, hidden_s, cot, cot_s, ring, inverse, rank
    )
    swap = send(swap, mate_core)
    flags = core.astype(jnp.int32).reshape(1)
    square = (count, rank)
    step_shapes = [(square, BF), ((count, 1), F32), (square, BF)]
    back, cross, mixes, back_pre, pull, near = small_call(
        lambda *refs: start_kernel(width, *refs),
        "start",
        flags,
        [pre, slope, inverse, near_m, last_m, mixed, swap],
        [(square, F32), ((count, 3 * rank), F32), ((rank, 3 * rank), BF)] + step_shapes,
    )

    none = jnp.zeros(square, BF)

    def link(back, came, pushes):
        shapes = [(square, F32)] + [(square, BF)] * pushes
        if not pushes:
            shapes = [((count, rank + rank // 2), BF), ((count, 1), F32)]
        came = came + [none] * (3 - len(came))
        return small_call(
            lambda *refs: link_kernel(width, pushes, *refs),
            "link%d" % pushes,
            flags,
            [back] + came + [pre, slope, inverse, cross, mixes],
            shapes,
        )

    def bases(every):
        split = rank + rank // 2
        low = jnp.concatenate(
            [jnp.zeros((count, 2 * rank), BF), every[:, rank : rank + rank // 2]], axis=1
        )
        high = jnp.concatenate([every[:, 2 * rank :], every[:, split : 2 * rank]], axis=1)
        return jnp.where(core == 0, low, high)

    def right_side(every, base, scaled, pull):
        direct = jnp.concatenate(
            [every[:, :rank], scaled, jnp.zeros((count, rank // 2), BF)], axis=1
        )
        pulled = (-pull * base.astype(F32)).astype(BF)
        return jnp.where(core == 0, direct, 0) + pulled

    def push(back_pre, pull, low, high):
        pushed = dot(back_pre, mixes[:, low * rank : high * rank], ((1,), (0,)))
        return (inverse * pushed - pull * cross[:, low * rank : high * rank]).astype(BF)

    came = send(near, between((3, 2)))
    far = push(back_pre, pull, 1, 3)
    far_1 = send(far[:, :rank], between((3, 1)))
    one_back = send(act, shifted(1))
    came, one_back, far = barrier((came, one_back, far))
    back, near, far_2 = link(back, [came], 2)
    came = send(near, between((2, 1)))
    far_0 = [send(far_2, between((2, 0))), send(far[:, rank:], between((3, 0)))]
    two_back = send(one_back, shifted(1))
    came, far_1, two_back = barrier((came, far_1, two_back))
    back, near = link(back, [came, far_1], 1)
    came = send(near, between((1, 0)))
    three_back = send(two_back, shifted(1))
    came, far_0, three_back = barrier((came, far_0, three_back))
    wire, pull = link(back, [came] + far_0, 0)
    every = jnp.concatenate([act, one_back, two_back, three_back], axis=1)
    wire, every = barrier((wire, every))
    wire_s = send(wire, mate_core)
    every_s = send(every, mate_core)
    base_m = bases(every)
    blocks = moved_blocks(rows_of(wire), down, hidden_rows, section)
    wire_s, every_s, base_m, blocks = barrier((wire_s, every_s, base_m, blocks))
    base_s = bases(every_s)
    scaled = wire[:, :rank]

    def features_of(which):
        came = [blocks[which]]
        for turn in range(1, SECTIONS):
            came.append(send(blocks[2 * turn + which], turned(turn)))
        return came

    scaled_s, pull_s = wire_s[:, :rank], wire_s[:, rank : rank + 1].astype(F32)
    joint = dot(scaled, base_m, ((0,), (0,))) + dot(scaled_s, base_s, ((0,), (0,)))
    sums = outer_products(
        hidden,
        hidden_s,
        cot,
        cot_s,
        right_side(every, base_m, scaled, pull),
        right_side(every_s, base_s, scaled_s, pull_s),
        down,
        joint.astype(BF),
    )
    sums, front = barrier((sums, features_of(0)))
    (own, other), rear = scatter_ring(*sums, features_of(1))

    feature = [[], [], []]
    for level in range(LEVELS):
        for rows, blocks in ((cot_rows[: cot_rows.shape[0] // 2], front), (cot_rows[cot_rows.shape[0] // 2 :], rear)):
            total = rows.astype(F32)
            for turn in range(SECTIONS):
                origin = (section - turn) % SECTIONS
                total = total + jnp.where(origin > level, blocks[turn].astype(F32), 0.0)
            feature[level].append(total.astype(BF).reshape(micro // 2, -1, part))
    feature_grads = jnp.stack([jnp.concatenate(pieces, axis=0) for pieces in feature])

    zero = jnp.where(core == 0, own, other)
    one = jnp.where(core == 0, other, own)
    down_grad = (zero[:, rank : 2 * rank] * factor)[None]
    near = jnp.concatenate([zero[:, 2 * rank :], one[:, 2 * rank :]], axis=1)
    up_sum = zero[:, :rank]
    for d, piece in ((1, near), (2, one[:, :rank]), (3, one[:, rank : 2 * rank])):
        up_sum = up_sum + send(piece, shifted(-d))
    up_grad = (up_sum.T * factor)[None]
    return (down_grad, up_grad, feature_grads)


def solution(mesh):
    placed = (
        P("pipe", None, "dp", None),
        P(None, "dp", None),
        P("pipe", "dp", None),
        P("pipe", None, "dp"),
        P(None, "dp"),
    )
    return jax.shard_map(
        on_device,
        mesh=mesh,
        in_specs=placed,
        out_specs=(P("pipe", "dp", None), P("pipe", None, "dp"), P(None, None, "dp", "pipe")),
        check_vma=False,
    )
```

```python
import jax
import jax.numpy as jnp
from jax import lax
from jax.experimental import pallas as pl
from jax.experimental.pallas import tpu as pltpu
from jax.sharding import PartitionSpec as P

LEVELS = 3
SIDE = 4
SECTIONS = 4
AXES = ("dp", "pipe")
BF = jnp.bfloat16
F32 = jnp.float32
VMEM_BYTES = 48 * 1024 * 1024
barrier = lax.optimization_barrier


def route(target):
    pairs = []
    for x in range(SIDE):
        for y in range(SIDE):
            for z in range(2):
                for c in range(2):
                    for s in range(SECTIONS):
                        to = target(x, y, z, c, s)
                        if to is None:
                            continue
                        tx, ty, tz, tc, ts = to
                        source = (((x * SIDE + y) * 2 + z) * 2 + c) * SECTIONS + s
                        dest = (((tx * SIDE + ty) * 2 + tz) * 2 + tc) * SECTIONS + ts
                        pairs.append((source, dest))
    return pairs


def send(block, target):
    return lax.ppermute(block, AXES, route(target))


def mate_z(x, y, z, c, s):
    return (x, y, 1 - z, c, s)


def mate_core(x, y, z, c, s):
    return (x, y, z, 1 - c, s)


def mate_cross(x, y, z, c, s):
    return (x, y, 1 - z, 1 - c, s)


def mate_x(mask):
    def target(x, y, z, c, s):
        return (((((x + c) % SIDE) ^ mask) - c) % SIDE, y, z, c, s)

    return target


def mate_y(mask):
    def target(x, y, z, c, s):
        return (x, ((((y + c) % SIDE) ^ mask) - c) % SIDE, z, c, s)

    return target


def shifted(distance, only=None):
    def target(x, y, z, c, s):
        if only is not None and s != only:
            return None
        if not 0 <= s + distance < SECTIONS:
            return None
        return (x, y, z, c, s + distance)

    return target


def between(*pairs):
    def target(x, y, z, c, s):
        goal = dict(pairs).get(s)
        return None if goal is None else (x, y, z, c, goal)

    return target


def ahead(distance):
    def target(x, y, z, c, s):
        return (x, y, z, c, (s + distance) % SECTIONS)

    return target


def turned(distance):
    def target(x, y, z, c, s):
        if s == 0:
            return None
        return (x, y, z, c, (s + distance) % SECTIONS)

    return target


def both(mine, theirs, bit, axis):
    low = jnp.where(bit == 0, mine, theirs)
    high = jnp.where(bit == 0, theirs, mine)
    return jnp.concatenate([low, high], axis=axis)


def place():
    index = lax.axis_index("dp")
    core = index % 2
    z = (index // 2) % 2
    y = (index // 4) % SIDE
    x = index // (4 * SIDE)
    return x, y, z, core


def gather_ring(blocks):
    x, y, z, core = place()
    xs = (x + core) % SIDE
    ys = (y + core) % SIDE
    halves = []
    for color, block in enumerate(blocks):
        first, second = ((xs, mate_x), (ys, mate_y)) if color == 0 else ((ys, mate_y), (xs, mate_x))
        now = block[None, None]
        for axis, (label, mate) in ((1, first), (0, second)):
            now = both(now, send(now, mate(1)), label % 2, axis)
            far = send(now, mate(3))
            if axis == 1:
                now = both(now, far, label // 2, axis)
        halves += [now, far]
    return halves


def halve(now, label, mate, axis):
    for mask, bit, size in ((3, label // 2, 2), (1, label % 2, 1)):
        kept = lax.dynamic_slice_in_dim(now, bit * size, size, axis)
        away = lax.dynamic_slice_in_dim(now, (1 - bit) * size, size, axis)
        now = kept + send(away.astype(BF), mate(mask)).astype(F32)
    return now


def halve_rest(kept, away, label, mate, axis):
    now = kept.astype(F32) + send(away, mate(3)).astype(F32)
    low = lax.dynamic_slice_in_dim(now, label % 2, 1, axis)
    high = lax.dynamic_slice_in_dim(now, 1 - label % 2, 1, axis)
    return low + send(high.astype(BF), mate(1)).astype(F32)


def scatter_ring(kept_a, away_a, kept_b, away_b, beside):
    x, y, z, core = place()
    xs = (x + core) % SIDE
    ys = (y + core) % SIDE
    first = halve_rest(kept_a, away_a, xs, mate_x, 0)
    second = halve_rest(kept_b, away_b, ys, mate_y, 1)
    first, second, beside = barrier((first, second, beside))
    first = halve(first, ys, mate_y, 1)[0, 0]
    second = halve(second, xs, mate_x, 0)[0, 0]
    cols = first.shape[1]
    mine = jnp.where(z == 0, first, second).reshape(2, -1, cols)
    away = jnp.where(z == 0, second, first).astype(BF).reshape(2, -1, cols)
    own = lax.dynamic_index_in_dim(mine, core, 0, False)
    own = own + send(lax.dynamic_index_in_dim(away, core, 0, False), mate_z).astype(F32)
    other = send(lax.dynamic_index_in_dim(mine, 1 - core, 0, False), mate_core)
    cross = send(lax.dynamic_index_in_dim(away, 1 - core, 0, False), mate_cross)
    return (own, other + cross.astype(F32)), beside


def dot(a, b, contract):
    return lax.dot_general(a, b, ((contract[0], contract[1]), ((), ())), preferred_element_type=F32)


def step_label(i, half):
    return 2 * jnp.where(i < 2, half, 1 - half) + i % 2


def inner_kernel(
    rank, where_ref, hm_ref, hs_ref, tm_ref, ts_ref, am_ref, at_ref, bm_ref, bt_ref, inverse_ref,
    down_ref, pre_ref, slope_ref, act_ref, nm_ref, um_ref, mixed_ref, swap_ref,
    weights, raw_ref, ns_ref, us_ref, blend_ref,
):
    core, half_y = where_ref[0], where_ref[2]
    step = pl.program_id(0)
    rows = am_ref.shape[2]
    for y in range(SIDE):
        label = lax.rem(core + y, SIDE)
        odd = lax.rem(label, 2)
        weights[pl.ds(2 * y * rows, rows), :] = jnp.where(
            label // 2 == half_y, am_ref[odd, 0], at_ref[odd, 0]
        )
        weights[pl.ds((2 * y + 1) * rows, rows), :] = jnp.where(
            step < 2, bm_ref[0, label], bt_ref[0, label]
        )
    down = weights[:, :rank]
    second = weights[:, rank : 2 * rank]
    third = weights[:, 2 * rank :]
    down_ref[...] = down
    hm, hs = hm_ref[...], hs_ref[...]

    tm = jnp.where(core == 0, tm_ref[...], hm)
    ts = jnp.where(core == 0, ts_ref[...], hs)
    results = (
        (raw_ref, dot(hm, down, ((1,), (0,)))),
        (nm_ref, dot(hm, second, ((1,), (0,)))),
        (ns_ref, dot(hs, second, ((1,), (0,)))),
        (um_ref, dot(tm, third, ((1,), (0,)))),
        (us_ref, dot(ts, third, ((1,), (0,)))),
        (blend_ref, dot(down, weights[:, rank:], ((0,), (0,)))),
    )

    @pl.when(step == 0)
    def _():
        for ref, value in results:
            ref[...] = value

    @pl.when(step > 0)
    def _():
        for ref, value in results:
            ref[...] += value

    @pl.when(step == SIDE - 1)
    def _():
        count = hm_ref.shape[0]
        pre = inverse_ref[...] * raw_ref[...]
        sigma = 1.0 / (1.0 + jnp.exp(-pre))
        pre_ref[...] = pre
        slope_ref[...] = sigma * (1.0 + pre * (1.0 - sigma))
        act_ref[...] = (pre * sigma).astype(BF)
        mixed = blend_ref[...].astype(BF)
        mixed_ref[...] = mixed
        swap_ref[:count, :rank] = ns_ref[...].astype(BF)
        swap_ref[:count, rank:] = us_ref[...].astype(BF)
        swap_ref[count:, :] = mixed


def position():
    x, y, z, core = place()
    return jnp.stack([core, (x + core) % SIDE // 2, (y + core) % SIDE // 2]).astype(jnp.int32)


def inner_products(hidden, hidden_s, cot, cot_s, ring, inverse, rank):
    count, width = hidden.shape
    part = width // SIDE
    rows, cols = ring[0].shape[2:]

    def label(i, w):
        return step_label(i, w[1])

    def block(i, w):
        return (label(i, w) + SIDE - w[0]) % SIDE

    first = pl.BlockSpec((count, part), lambda i, w: (0, block(i, w)))
    third = pl.BlockSpec((count, part), lambda i, w: (0, (1 - w[0]) * block(i, w)))
    one = pl.BlockSpec((2, 1, rows, cols), lambda i, w: (0, label(i, w), 0, 0))
    whole = lambda shape: pl.BlockSpec(shape, lambda i, w: (0, 0))
    small = (count, rank)
    shapes = [
        (small, F32),
        (small, F32),
        (small, BF),
        (small, F32),
        (small, F32),
        ((rank, 2 * rank), BF),
        ((count + rank, 2 * rank), BF),
    ]
    return pl.pallas_call(
        lambda *refs: inner_kernel(rank, *refs),
        grid_spec=pltpu.PrefetchScalarGridSpec(
            num_scalar_prefetch=1,
            grid=(SIDE,),
            in_specs=[
                first,
                first,
                third,
                third,
                one,
                one,
                pl.BlockSpec((1, SIDE, rows, cols), lambda i, w: (jnp.minimum(i, 1), 0, 0, 0)),
                pl.BlockSpec((1, SIDE, rows, cols), lambda i, w: (jnp.maximum(i - 2, 0), 0, 0, 0)),
                whole((count, 1)),
            ],
            out_specs=[pl.BlockSpec((part, rank), lambda i, w: (block(i, w), 0))]
            + [whole(shape) for shape, _ in shapes],
            scratch_shapes=[pltpu.VMEM((part, cols), BF)]
            + [pltpu.VMEM(small, F32)] * 3
            + [pltpu.VMEM((rank, 2 * rank), F32)],
        ),
        out_shape=[jax.ShapeDtypeStruct((width, rank), BF)]
        + [jax.ShapeDtypeStruct(shape, dtype) for shape, dtype in shapes],
        compiler_params=pltpu.CompilerParams(vmem_limit_bytes=VMEM_BYTES),
        cost_estimate=pl.CostEstimate(
            flops=2 * width * rank * (5 * count + 2 * rank),
            bytes_accessed=2 * width * (4 * count + cols + rank),
            transcendentals=0,
        ),
        name="inner_products",
    )(position(), hidden, hidden_s, cot, cot_s, *ring, inverse)


def outer_kernel(
    rank, where_ref, hm_ref, hs_ref, tm_ref, ts_ref, rm_ref, rs_ref, down_ref, joint_ref,
    kept_a, away_a, kept_b, away_b, total,
):
    core, half_y = where_ref[0], where_ref[2]
    rows = total.shape[1]
    chunk = 4 * rows
    cols = joint_ref.shape[1]
    for half in range(2):
        span = pl.ds(half * chunk, chunk)
        inner = dot(down_ref[span, :], joint_ref[...], ((1,), (0,)))
        hm, hs = hm_ref[:, span], hs_ref[:, span]
        tm = jnp.where(core == 0, tm_ref[:, span], hm)
        ts = jnp.where(core == 0, ts_ref[:, span], hs)
        left = dot(tm, rm_ref[:, :rank], ((0,), (0,)))
        left = left + dot(ts, rs_ref[:, :rank], ((0,), (0,)))
        right = dot(hm, rm_ref[:, rank:], ((0,), (0,)))
        right = right + dot(hs, rs_ref[:, rank:], ((0,), (0,)))
        left = (left + inner[:, :rank]).astype(BF)
        right = (right + inner[:, rank:]).astype(BF)
        for k in range(4):
            total[half * 4 + k, :, :rank] = left[k * rows : (k + 1) * rows]
            total[half * 4 + k, :, rank:] = right[k * rows : (k + 1) * rows]
    for t in range(SIDE):
        y = lax.rem(t + SIDE - core, SIDE)
        value = total[2 * y]

        @pl.when(pl.program_id(0) < 2)
        def _():
            away_a[0, t] = value

        @pl.when(pl.program_id(0) >= 2)
        def _():
            kept_a[0, t] = value

    for t in range(2):
        y = lax.rem(2 * half_y + t + SIDE - core, SIDE)
        kept_b[0, t] = total[2 * y + 1]
        y = lax.rem(2 * (1 - half_y) + t + SIDE - core, SIDE)
        away_b[0, t] = total[2 * y + 1]


def outer_products(hidden, hidden_s, cot, cot_s, right, right_sibling, down, joint):
    count, width = hidden.shape
    rank, cols = joint.shape
    part = width // SIDE
    rows = part // (2 * SIDE)

    def label(i, w):
        return step_label(i, 1 - w[1])

    def block(i, w):
        return (label(i, w) + SIDE - w[0]) % SIDE

    first = pl.BlockSpec((count, part), lambda i, w: (0, block(i, w)))
    third = pl.BlockSpec((count, part), lambda i, w: (0, (1 - w[0]) * block(i, w)))
    same = lambda shape: pl.BlockSpec(shape, lambda i, w: (0, 0))
    return pl.pallas_call(
        lambda *refs: outer_kernel(rank, *refs),
        grid_spec=pltpu.PrefetchScalarGridSpec(
            num_scalar_prefetch=1,
            grid=(SIDE,),
            in_specs=[
                first,
                first,
                third,
                third,
                same(right.shape),
                same(right.shape),
                pl.BlockSpec((part, rank), lambda i, w: (block(i, w), 0)),
                same(joint.shape),
            ],
            out_specs=[
                pl.BlockSpec((1, SIDE, rows, cols), lambda i, w: (jnp.maximum(i - 2, 0), 0, 0, 0)),
                pl.BlockSpec((1, SIDE, rows, cols), lambda i, w: (jnp.minimum(i, 1), 0, 0, 0)),
                pl.BlockSpec((1, 2, rows, cols), lambda i, w: (label(i, w), 0, 0, 0)),
                pl.BlockSpec((1, 2, rows, cols), lambda i, w: (label(i, w), 0, 0, 0)),
            ],
            scratch_shapes=[pltpu.VMEM((2 * SIDE, rows, cols), BF)],
        ),
        out_shape=[jax.ShapeDtypeStruct((2, SIDE, rows, cols), BF)] * 2
        + [jax.ShapeDtypeStruct((SIDE, 2, rows, cols), BF)] * 2,
        compiler_params=pltpu.CompilerParams(vmem_limit_bytes=VMEM_BYTES),
        cost_estimate=pl.CostEstimate(
            flops=2 * width * cols * (2 * count + rank),
            bytes_accessed=2 * width * (4 * count + cols + rank),
            transcendentals=0,
        ),
        name="outer_products",
    )(position(), hidden, hidden_s, cot, cot_s, right, right_sibling, down, joint)


def step_values(width, back, pre, slope, inverse):
    back_pre = (back * slope).astype(BF)
    wide = back_pre.astype(F32)
    pull = jnp.sum(wide * pre, axis=1, keepdims=True) / width * inverse * inverse
    return back_pre, wide, pull


def start_kernel(
    width, flag_ref, pre_ref, slope_ref, inverse_ref, near_ref, last_ref, mixed_ref, came_ref,
    back_ref, cross_ref, mixes_ref, step_ref, pull_ref, push_ref,
):
    count, rank = pre_ref.shape
    zero = flag_ref[0] == 0
    came = came_ref[:count, :].astype(F32)
    back = jnp.where(zero, last_ref[...], came[:, rank:])
    cross = jnp.where(zero, near_ref[...], came[:, :rank])
    cross_ref[:, :rank] = cross
    cross_ref[:, rank : 2 * rank] = jnp.where(zero, came[:, :rank], near_ref[...])
    cross_ref[:, 2 * rank :] = jnp.where(zero, came[:, rank:], last_ref[...])
    ours, theirs = mixed_ref[...], came_ref[count:, :]
    mix = jnp.where(zero, ours[:, :rank], theirs[:, :rank])
    mixes_ref[:, :rank] = mix
    mixes_ref[:, rank:] = jnp.where(zero, theirs, ours)
    inverse = inverse_ref[...]
    back_pre, wide, pull = step_values(width, back, pre_ref[...], slope_ref[...], inverse)
    back_ref[...] = back
    step_ref[...] = back_pre
    pull_ref[...] = pull
    push_ref[...] = (inverse * dot(back_pre, mix, ((1,), (0,))) - pull * cross).astype(BF)


def link_kernel(
    width, pushes, flag_ref, back_ref, *refs
):
    came, (pre_ref, slope_ref, inverse_ref, cross_ref, mixes_ref, *outs) = refs[:3], refs[3:]
    rank = pre_ref.shape[1]
    back = back_ref[...]
    for ref in came:
        back = back + ref[...].astype(F32)
    inverse = inverse_ref[...]
    back_pre, wide, pull = step_values(width, back, pre_ref[...], slope_ref[...], inverse)
    if not pushes:
        wire_ref, pull_ref = outs
        wire_ref[:, :rank] = (wide * inverse).astype(BF)
        wire_ref[:, rank:] = jnp.broadcast_to(pull, (back.shape[0], rank // 2)).astype(BF)
        pull_ref[...] = pull
        return
    outs[0][...] = back
    for k in range(pushes):
        span = pl.ds(k * rank, rank)
        pushed = inverse * dot(back_pre, mixes_ref[:, span], ((1,), (0,)))
        outs[1 + k][...] = (pushed - pull * cross_ref[:, span]).astype(BF)


def small_call(kernel, name, flags, operands, shapes):
    whole = lambda shape: pl.BlockSpec(shape, lambda i, flags: (0, 0))
    return pl.pallas_call(
        kernel,
        grid_spec=pltpu.PrefetchScalarGridSpec(
            num_scalar_prefetch=1,
            grid=(1,),
            in_specs=[whole(operand.shape) for operand in operands],
            out_specs=[whole(shape) for shape, _ in shapes],
        ),
        out_shape=[jax.ShapeDtypeStruct(shape, dtype) for shape, dtype in shapes],
        compiler_params=pltpu.CompilerParams(vmem_limit_bytes=VMEM_BYTES),
        name=name,
    )(flags, *operands)


def moved_kernel(rank, place_ref, picked_ref, down_ref, rows_ref, *outs):
    pull = picked_ref[:, rank : rank + 1].astype(F32)
    value = dot(picked_ref[:, :rank], down_ref[...], ((1,), (1,)))
    value = (value - pull * rows_ref[...].astype(F32)).astype(BF)
    half = value.shape[0] // 2
    for t in range(SECTIONS):

        @pl.when(pl.program_id(0) == t)
        def _():
            outs[2 * t][...] = value[:half]
            outs[2 * t + 1][...] = value[half:]


def moved_blocks(picked, down, rows, section):
    count, width = rows.shape
    rank = down.shape[1]
    part = width // SECTIONS
    half = jax.ShapeDtypeStruct((count // 2, part), BF)
    return pl.pallas_call(
        lambda *refs: moved_kernel(rank, *refs),
        grid_spec=pltpu.PrefetchScalarGridSpec(
            num_scalar_prefetch=1,
            grid=(SECTIONS,),
            in_specs=[
                pl.BlockSpec(picked.shape, lambda t, w: (0, 0)),
                pl.BlockSpec((part, rank), lambda t, w: ((w[0] + t) % SECTIONS, 0)),
                pl.BlockSpec((count, part), lambda t, w: (0, (w[0] + t) % SECTIONS)),
            ],
            out_specs=[pl.BlockSpec(half.shape, lambda t, w: (0, 0))] * (2 * SECTIONS),
        ),
        out_shape=[half] * (2 * SECTIONS),
        compiler_params=pltpu.CompilerParams(vmem_limit_bytes=VMEM_BYTES),
        cost_estimate=pl.CostEstimate(
            flops=2 * count * width * rank, bytes_accessed=4 * count * width, transcendentals=0
        ),
        name="moved_blocks",
    )(section.astype(jnp.int32).reshape(1), picked, down, rows)


def on_device(saved_inputs, cotangent, adapter_down, adapter_up, image_rows):
    section = lax.axis_index("pipe")
    x, y, z, core = place()
    micro, tokens, width = cotangent.shape
    rank = adapter_down.shape[2]
    count = micro * tokens
    factor = (count * lax.axis_size("dp")) ** (-0.5)
    hidden = saved_inputs.reshape(count, width)
    cot = cotangent.reshape(count, width)

    up_shard = adapter_up[0].T
    extra = [send(up_shard, ahead(d)) for d in (1, 2, 3)]
    sets = [
        jnp.concatenate([adapter_down[0], extra[0], up_shard], axis=1),
        jnp.concatenate([adapter_down[0], extra[1], extra[2]], axis=1),
    ]
    mine = jnp.where(core == 0, sets[0], sets[1])
    away = jnp.where(core == 0, sets[1], sets[0])
    by_z = send(mine, mate_z)
    by_core = send(away, mate_core)
    by_both = send(away, mate_cross)
    here = both(mine, by_core, core, 0)
    there = both(by_z, by_both, core, 0)
    blocks = [jnp.where(z == 0, here, there), jnp.where(z == 0, there, here)]
    hidden, cot, blocks = barrier((hidden, cot, blocks))
    hidden_s = send(hidden, mate_core)
    cot_s = send(cot, mate_core)
    ring = gather_ring(blocks)

    picks = (image_rows[:, :, None] == jnp.arange(tokens, dtype=jnp.int32)).astype(BF)

    def rows_of(array):
        array = array.reshape(micro, tokens, -1)
        out = lax.dot_general(picks, array, (((2,), (1,)), ((0,), (0,))), preferred_element_type=F32)
        return out.reshape(-1, out.shape[-1]).astype(BF)

    part = width // SECTIONS
    hidden_rows = rows_of(hidden)
    cot_rows = rows_of(lax.dynamic_slice_in_dim(cot, section * part, part, 1))
    wide = hidden.astype(F32)
    inverse = lax.rsqrt(jnp.mean(wide * wide, axis=1, keepdims=True) + 1e-06)
    ring, hidden_rows, cot_rows, inverse = barrier((ring, hidden_rows, cot_rows, inverse))

    down, pre, slope, act, near_m, last_m, mixed, swap = inner_products(
        hidden, hidden_s, cot, cot_s, ring, inverse, rank
    )
    swap = send(swap, mate_core)
    act_all = lax.all_gather(act, "pipe", axis=0)
    flags = core.astype(jnp.int32).reshape(1)
    square = (count, rank)
    step_shapes = [(square, BF), ((count, 1), F32), (square, BF)]
    back, cross, mixes, back_pre, pull, near = small_call(
        lambda *refs: start_kernel(width, *refs),
        "start",
        flags,
        [pre, slope, inverse, near_m, last_m, mixed, swap],
        [(square, F32), ((count, 3 * rank), F32), ((rank, 3 * rank), BF)] + step_shapes,
    )

    none = jnp.zeros(square, BF)

    def link(back, came, pushes):
        shapes = [(square, F32)] + [(square, BF)] * pushes
        if not pushes:
            shapes = [((count, rank + rank // 2), BF), ((count, 1), F32)]
        came = came + [none] * (3 - len(came))
        return small_call(
            lambda *refs: link_kernel(width, pushes, *refs),
            "link%d" % pushes,
            flags,
            [back] + came + [pre, slope, inverse, cross, mixes],
            shapes,
        )

    def bases(every):
        split = rank + rank // 2
        low = jnp.concatenate(
            [jnp.zeros((count, 2 * rank), BF), every[:, rank : rank + rank // 2]], axis=1
        )
        high = jnp.concatenate([every[:, 2 * rank :], every[:, split : 2 * rank]], axis=1)
        return jnp.where(core == 0, low, high)

    def right_side(every, base, scaled, pull):
        direct = jnp.concatenate(
            [every[:, :rank], scaled, jnp.zeros((count, rank // 2), BF)], axis=1
        )
        pulled = (-pull * base.astype(F32)).astype(BF)
        return jnp.where(core == 0, direct, 0) + pulled

    def push(back_pre, pull, low, high):
        pushed = dot(back_pre, mixes[:, low * rank : high * rank], ((1,), (0,)))
        return (inverse * pushed - pull * cross[:, low * rank : high * rank]).astype(BF)

    came = send(near, between((3, 2)))
    far = push(back_pre, pull, 1, 3)
    far_1 = send(far[:, :rank], between((3, 1)))
    came, far = barrier((came, far))
    back, near, far_2 = link(back, [came], 2)
    came = send(near, between((2, 1)))
    far_0 = [send(far_2, between((2, 0))), send(far[:, rank:], between((3, 0)))]
    came, far_1 = barrier((came, far_1))
    back, near = link(back, [came, far_1], 1)
    came = send(near, between((1, 0)))
    came, far_0 = barrier((came, far_0))
    wire, pull = link(back, [came] + far_0, 0)
    acts = [
        lax.dynamic_index_in_dim(act_all, (section + SECTIONS - d) % SECTIONS, 0, False) for d in (1, 2, 3)
    ]
    every = jnp.concatenate([act] + acts, axis=1)
    wire, every = barrier((wire, every))
    wire_s = send(wire, mate_core)
    every_s = send(every, mate_core)
    base_m = bases(every)
    blocks = moved_blocks(rows_of(wire), down, hidden_rows, section)
    wire_s, every_s, base_m, blocks = barrier((wire_s, every_s, base_m, blocks))
    base_s = bases(every_s)
    scaled = wire[:, :rank]

    def features_of(which):
        came = [blocks[which]]
        for turn in range(1, SECTIONS):
            came.append(send(blocks[2 * turn + which], turned(turn)))
        return came

    scaled_s, pull_s = wire_s[:, :rank], wire_s[:, rank : rank + 1].astype(F32)
    joint = dot(scaled, base_m, ((0,), (0,))) + dot(scaled_s, base_s, ((0,), (0,)))
    sums = outer_products(
        hidden,
        hidden_s,
        cot,
        cot_s,
        right_side(every, base_m, scaled, pull),
        right_side(every_s, base_s, scaled_s, pull_s),
        down,
        joint.astype(BF),
    )
    sums, front = barrier((sums, features_of(0)))
    (own, other), rear = scatter_ring(*sums, features_of(1))

    feature = [[], [], []]
    for level in range(LEVELS):
        for rows, blocks in ((cot_rows[: cot_rows.shape[0] // 2], front), (cot_rows[cot_rows.shape[0] // 2 :], rear)):
            total = rows.astype(F32)
            for turn in range(SECTIONS):
                origin = (section - turn) % SECTIONS
                total = total + jnp.where(origin > level, blocks[turn].astype(F32), 0.0)
            feature[level].append(total.astype(BF).reshape(micro // 2, -1, part))
    feature_grads = jnp.stack([jnp.concatenate(pieces, axis=0) for pieces in feature])

    zero = jnp.where(core == 0, own, other)
    one = jnp.where(core == 0, other, own)
    down_grad = (zero[:, rank : 2 * rank] * factor)[None]
    near = jnp.concatenate([zero[:, 2 * rank :], one[:, 2 * rank :]], axis=1)
    up_sum = zero[:, :rank]
    for d, piece in ((1, near), (2, one[:, :rank]), (3, one[:, rank : 2 * rank])):
        up_sum = up_sum + send(piece, shifted(-d))
    up_grad = (up_sum.T * factor)[None]
    return (down_grad, up_grad, feature_grads)


def solution(mesh):
    placed = (
        P("pipe", None, "dp", None),
        P(None, "dp", None),
        P("pipe", "dp", None),
        P("pipe", None, "dp"),
        P(None, "dp"),
    )
    return jax.shard_map(
        on_device,
        mesh=mesh,
        in_specs=placed,
        out_specs=(P("pipe", "dp", None), P("pipe", None, "dp"), P(None, None, "dp", "pipe")),
        check_vma=False,
    )
```

```python
import jax
import jax.numpy as jnp
from jax import lax
from jax.experimental import pallas as pl
from jax.experimental.pallas import tpu as pltpu
from jax.sharding import PartitionSpec as P

LEVELS = 3
SIDE = 4
SECTIONS = 4
AXES = ("dp", "pipe")
BF = jnp.bfloat16
F32 = jnp.float32
VMEM_BYTES = 48 * 1024 * 1024
barrier = lax.optimization_barrier


def route(target):
    pairs = []
    for x in range(SIDE):
        for y in range(SIDE):
            for z in range(2):
                for c in range(2):
                    for s in range(SECTIONS):
                        to = target(x, y, z, c, s)
                        if to is None:
                            continue
                        tx, ty, tz, tc, ts = to
                        source = (((x * SIDE + y) * 2 + z) * 2 + c) * SECTIONS + s
                        dest = (((tx * SIDE + ty) * 2 + tz) * 2 + tc) * SECTIONS + ts
                        pairs.append((source, dest))
    return pairs


def send(block, target):
    return lax.ppermute(block, AXES, route(target))


def mate_z(x, y, z, c, s):
    return (x, y, 1 - z, c, s)


def mate_core(x, y, z, c, s):
    return (x, y, z, 1 - c, s)


def mate_cross(x, y, z, c, s):
    return (x, y, 1 - z, 1 - c, s)


def mate_x(mask):
    def target(x, y, z, c, s):
        return (((((x + c) % SIDE) ^ mask) - c) % SIDE, y, z, c, s)

    return target


def mate_y(mask):
    def target(x, y, z, c, s):
        return (x, ((((y + c) % SIDE) ^ mask) - c) % SIDE, z, c, s)

    return target


def shifted(distance, only=None):
    def target(x, y, z, c, s):
        if only is not None and s != only:
            return None
        if not 0 <= s + distance < SECTIONS:
            return None
        return (x, y, z, c, s + distance)

    return target


def between(*pairs):
    def target(x, y, z, c, s):
        goal = dict(pairs).get(s)
        return None if goal is None else (x, y, z, c, goal)

    return target


def ahead(distance):
    def target(x, y, z, c, s):
        return (x, y, z, c, (s + distance) % SECTIONS)

    return target


def turned(distance):
    def target(x, y, z, c, s):
        if s == 0:
            return None
        return (x, y, z, c, (s + distance) % SECTIONS)

    return target


def both(mine, theirs, bit, axis):
    low = jnp.where(bit == 0, mine, theirs)
    high = jnp.where(bit == 0, theirs, mine)
    return jnp.concatenate([low, high], axis=axis)


def place():
    index = lax.axis_index("dp")
    core = index % 2
    z = (index // 2) % 2
    y = (index // 4) % SIDE
    x = index // (4 * SIDE)
    return x, y, z, core


def gather_ring(blocks):
    x, y, z, core = place()
    xs = (x + core) % SIDE
    ys = (y + core) % SIDE
    halves = []
    for color, block in enumerate(blocks):
        first, second = ((xs, mate_x), (ys, mate_y)) if color == 0 else ((ys, mate_y), (xs, mate_x))
        now = block[None, None]
        for axis, (label, mate) in ((1, first), (0, second)):
            now = both(now, send(now, mate(1)), label % 2, axis)
            far = send(now, mate(3))
            if axis == 1:
                now = both(now, far, label // 2, axis)
        halves += [now, far]
    return halves


def halve(now, label, mate, axis):
    for mask, bit, size in ((3, label // 2, 2), (1, label % 2, 1)):
        kept = lax.dynamic_slice_in_dim(now, bit * size, size, axis)
        away = lax.dynamic_slice_in_dim(now, (1 - bit) * size, size, axis)
        now = kept + send(away.astype(BF), mate(mask)).astype(F32)
    return now


def halve_rest(kept, away, label, mate, axis):
    now = kept.astype(F32) + send(away, mate(3)).astype(F32)
    low = lax.dynamic_slice_in_dim(now, label % 2, 1, axis)
    high = lax.dynamic_slice_in_dim(now, 1 - label % 2, 1, axis)
    return low + send(high.astype(BF), mate(1)).astype(F32)


def scatter_ring(kept_a, away_a, kept_b, away_b, beside):
    x, y, z, core = place()
    xs = (x + core) % SIDE
    ys = (y + core) % SIDE
    first = halve_rest(kept_a, away_a, xs, mate_x, 0)
    second = halve_rest(kept_b, away_b, ys, mate_y, 1)
    first, second, beside = barrier((first, second, beside))
    first = halve(first, ys, mate_y, 1)[0, 0]
    second = halve(second, xs, mate_x, 0)[0, 0]
    cols = first.shape[1]
    mine = jnp.where(z == 0, first, second).reshape(2, -1, cols)
    away = jnp.where(z == 0, second, first).astype(BF).reshape(2, -1, cols)
    own = lax.dynamic_index_in_dim(mine, core, 0, False)
    own = own + send(lax.dynamic_index_in_dim(away, core, 0, False), mate_z).astype(F32)
    other = send(lax.dynamic_index_in_dim(mine, 1 - core, 0, False).astype(BF), mate_core)
    cross = send(lax.dynamic_index_in_dim(away, 1 - core, 0, False), mate_cross)
    return (own, other.astype(F32) + cross.astype(F32)), beside


def dot(a, b, contract):
    return lax.dot_general(a, b, ((contract[0], contract[1]), ((), ())), preferred_element_type=F32)


def step_label(i, half):
    return 2 * jnp.where(i < 2, half, 1 - half) + i % 2


def inner_kernel(
    rank, where_ref, hm_ref, hs_ref, tm_ref, ts_ref, am_ref, at_ref, bm_ref, bt_ref, inverse_ref,
    down_ref, pre_ref, slope_ref, act_ref, nm_ref, um_ref, mixed_ref, swap_ref,
    weights, raw_ref, ns_ref, us_ref, blend_ref,
):
    core, half_y = where_ref[0], where_ref[2]
    step = pl.program_id(0)
    rows = am_ref.shape[2]
    for y in range(SIDE):
        label = lax.rem(core + y, SIDE)
        odd = lax.rem(label, 2)
        weights[pl.ds(2 * y * rows, rows), :] = jnp.where(
            label // 2 == half_y, am_ref[odd, 0], at_ref[odd, 0]
        )
        weights[pl.ds((2 * y + 1) * rows, rows), :] = jnp.where(
            step < 2, bm_ref[0, label], bt_ref[0, label]
        )
    down = weights[:, :rank]
    second = weights[:, rank : 2 * rank]
    third = weights[:, 2 * rank :]
    down_ref[...] = down
    hm, hs = hm_ref[...], hs_ref[...]

    tm = jnp.where(core == 0, tm_ref[...], hm)
    ts = jnp.where(core == 0, ts_ref[...], hs)
    results = (
        (raw_ref, dot(hm, down, ((1,), (0,)))),
        (nm_ref, dot(hm, second, ((1,), (0,)))),
        (ns_ref, dot(hs, second, ((1,), (0,)))),
        (um_ref, dot(tm, third, ((1,), (0,)))),
        (us_ref, dot(ts, third, ((1,), (0,)))),
        (blend_ref, dot(down, weights[:, rank:], ((0,), (0,)))),
    )

    @pl.when(step == 0)
    def _():
        for ref, value in results:
            ref[...] = value

    @pl.when(step > 0)
    def _():
        for ref, value in results:
            ref[...] += value

    @pl.when(step == SIDE - 1)
    def _():
        count = hm_ref.shape[0]
        pre = inverse_ref[...] * raw_ref[...]
        sigma = 1.0 / (1.0 + jnp.exp(-pre))
        pre_ref[...] = pre
        slope_ref[...] = sigma * (1.0 + pre * (1.0 - sigma))
        act_ref[...] = (pre * sigma).astype(BF)
        mixed = blend_ref[...].astype(BF)
        mixed_ref[...] = mixed
        swap_ref[:count, :rank] = ns_ref[...].astype(BF)
        swap_ref[:count, rank:] = us_ref[...].astype(BF)
        swap_ref[count:, :] = mixed


def position():
    x, y, z, core = place()
    return jnp.stack([core, (x + core) % SIDE // 2, (y + core) % SIDE // 2]).astype(jnp.int32)


def inner_products(hidden, hidden_s, cot, cot_s, ring, inverse, rank):
    count, width = hidden.shape
    part = width // SIDE
    rows, cols = ring[0].shape[2:]

    def label(i, w):
        return step_label(i, w[1])

    def block(i, w):
        return (label(i, w) + SIDE - w[0]) % SIDE

    first = pl.BlockSpec((count, part), lambda i, w: (0, block(i, w)))
    third = pl.BlockSpec((count, part), lambda i, w: (0, (1 - w[0]) * block(i, w)))
    one = pl.BlockSpec((2, 1, rows, cols), lambda i, w: (0, label(i, w), 0, 0))
    whole = lambda shape: pl.BlockSpec(shape, lambda i, w: (0, 0))
    small = (count, rank)
    shapes = [
        (small, F32),
        (small, F32),
        (small, BF),
        (small, F32),
        (small, F32),
        ((rank, 2 * rank), BF),
        ((count + rank, 2 * rank), BF),
    ]
    return pl.pallas_call(
        lambda *refs: inner_kernel(rank, *refs),
        grid_spec=pltpu.PrefetchScalarGridSpec(
            num_scalar_prefetch=1,
            grid=(SIDE,),
            in_specs=[
                first,
                first,
                third,
                third,
                one,
                one,
                pl.BlockSpec((1, SIDE, rows, cols), lambda i, w: (jnp.minimum(i, 1), 0, 0, 0)),
                pl.BlockSpec((1, SIDE, rows, cols), lambda i, w: (jnp.maximum(i - 2, 0), 0, 0, 0)),
                whole((count, 1)),
            ],
            out_specs=[pl.BlockSpec((part, rank), lambda i, w: (block(i, w), 0))]
            + [whole(shape) for shape, _ in shapes],
            scratch_shapes=[pltpu.VMEM((part, cols), BF)]
            + [pltpu.VMEM(small, F32)] * 3
            + [pltpu.VMEM((rank, 2 * rank), F32)],
        ),
        out_shape=[jax.ShapeDtypeStruct((width, rank), BF)]
        + [jax.ShapeDtypeStruct(shape, dtype) for shape, dtype in shapes],
        compiler_params=pltpu.CompilerParams(vmem_limit_bytes=VMEM_BYTES),
        cost_estimate=pl.CostEstimate(
            flops=2 * width * rank * (5 * count + 2 * rank),
            bytes_accessed=2 * width * (4 * count + cols + rank),
            transcendentals=0,
        ),
        name="inner_products",
    )(position(), hidden, hidden_s, cot, cot_s, *ring, inverse)


def outer_kernel(
    rank, where_ref, hm_ref, hs_ref, tm_ref, ts_ref, rm_ref, rs_ref, down_ref, joint_ref,
    kept_a, away_a, kept_b, away_b, total,
):
    core, half_y = where_ref[0], where_ref[2]
    rows = total.shape[1]
    chunk = 4 * rows
    cols = joint_ref.shape[1]
    for half in range(2):
        span = pl.ds(half * chunk, chunk)
        inner = dot(down_ref[span, :], joint_ref[...], ((1,), (0,)))
        hm, hs = hm_ref[:, span], hs_ref[:, span]
        tm = jnp.where(core == 0, tm_ref[:, span], hm)
        ts = jnp.where(core == 0, ts_ref[:, span], hs)
        left = dot(tm, rm_ref[:, :rank], ((0,), (0,)))
        left = left + dot(ts, rs_ref[:, :rank], ((0,), (0,)))
        right = dot(hm, rm_ref[:, rank:], ((0,), (0,)))
        right = right + dot(hs, rs_ref[:, rank:], ((0,), (0,)))
        left = (left + inner[:, :rank]).astype(BF)
        right = (right + inner[:, rank:]).astype(BF)
        for k in range(4):
            total[half * 4 + k, :, :rank] = left[k * rows : (k + 1) * rows]
            total[half * 4 + k, :, rank:] = right[k * rows : (k + 1) * rows]
    for t in range(SIDE):
        y = lax.rem(t + SIDE - core, SIDE)
        value = total[2 * y]

        @pl.when(pl.program_id(0) < 2)
        def _():
            away_a[0, t] = value

        @pl.when(pl.program_id(0) >= 2)
        def _():
            kept_a[0, t] = value

    for t in range(2):
        y = lax.rem(2 * half_y + t + SIDE - core, SIDE)
        kept_b[0, t] = total[2 * y + 1]
        y = lax.rem(2 * (1 - half_y) + t + SIDE - core, SIDE)
        away_b[0, t] = total[2 * y + 1]


def outer_products(hidden, hidden_s, cot, cot_s, right, right_sibling, down, joint):
    count, width = hidden.shape
    rank, cols = joint.shape
    part = width // SIDE
    rows = part // (2 * SIDE)

    def label(i, w):
        return step_label(i, 1 - w[1])

    def block(i, w):
        return (label(i, w) + SIDE - w[0]) % SIDE

    first = pl.BlockSpec((count, part), lambda i, w: (0, block(i, w)))
    third = pl.BlockSpec((count, part), lambda i, w: (0, (1 - w[0]) * block(i, w)))
    same = lambda shape: pl.BlockSpec(shape, lambda i, w: (0, 0))
    return pl.pallas_call(
        lambda *refs: outer_kernel(rank, *refs),
        grid_spec=pltpu.PrefetchScalarGridSpec(
            num_scalar_prefetch=1,
            grid=(SIDE,),
            in_specs=[
                first,
                first,
                third,
                third,
                same(right.shape),
                same(right.shape),
                pl.BlockSpec((part, rank), lambda i, w: (block(i, w), 0)),
                same(joint.shape),
            ],
            out_specs=[
                pl.BlockSpec((1, SIDE, rows, cols), lambda i, w: (jnp.maximum(i - 2, 0), 0, 0, 0)),
                pl.BlockSpec((1, SIDE, rows, cols), lambda i, w: (jnp.minimum(i, 1), 0, 0, 0)),
                pl.BlockSpec((1, 2, rows, cols), lambda i, w: (label(i, w), 0, 0, 0)),
                pl.BlockSpec((1, 2, rows, cols), lambda i, w: (label(i, w), 0, 0, 0)),
            ],
            scratch_shapes=[pltpu.VMEM((2 * SIDE, rows, cols), BF)],
        ),
        out_shape=[jax.ShapeDtypeStruct((2, SIDE, rows, cols), BF)] * 2
        + [jax.ShapeDtypeStruct((SIDE, 2, rows, cols), BF)] * 2,
        compiler_params=pltpu.CompilerParams(vmem_limit_bytes=VMEM_BYTES),
        cost_estimate=pl.CostEstimate(
            flops=2 * width * cols * (2 * count + rank),
            bytes_accessed=2 * width * (4 * count + cols + rank),
            transcendentals=0,
        ),
        name="outer_products",
    )(position(), hidden, hidden_s, cot, cot_s, right, right_sibling, down, joint)


def step_values(width, back, pre, slope, inverse):
    back_pre = (back * slope).astype(BF)
    wide = back_pre.astype(F32)
    pull = jnp.sum(wide * pre, axis=1, keepdims=True) / width * inverse * inverse
    return back_pre, wide, pull


def start_kernel(
    width, flag_ref, pre_ref, slope_ref, inverse_ref, near_ref, last_ref, mixed_ref, came_ref,
    back_ref, cross_ref, mixes_ref, step_ref, pull_ref, push_ref,
):
    count, rank = pre_ref.shape
    zero = flag_ref[0] == 0
    came = came_ref[:count, :].astype(F32)
    back = jnp.where(zero, last_ref[...], came[:, rank:])
    cross = jnp.where(zero, near_ref[...], came[:, :rank])
    cross_ref[:, :rank] = cross
    cross_ref[:, rank : 2 * rank] = jnp.where(zero, came[:, :rank], near_ref[...])
    cross_ref[:, 2 * rank :] = jnp.where(zero, came[:, rank:], last_ref[...])
    ours, theirs = mixed_ref[...], came_ref[count:, :]
    mix = jnp.where(zero, ours[:, :rank], theirs[:, :rank])
    mixes_ref[:, :rank] = mix
    mixes_ref[:, rank:] = jnp.where(zero, theirs, ours)
    inverse = inverse_ref[...]
    back_pre, wide, pull = step_values(width, back, pre_ref[...], slope_ref[...], inverse)
    back_ref[...] = back
    step_ref[...] = back_pre
    pull_ref[...] = pull
    push_ref[...] = (inverse * dot(back_pre, mix, ((1,), (0,))) - pull * cross).astype(BF)


def link_kernel(
    width, pushes, flag_ref, back_ref, *refs
):
    came, (pre_ref, slope_ref, inverse_ref, cross_ref, mixes_ref, *outs) = refs[:3], refs[3:]
    rank = pre_ref.shape[1]
    back = back_ref[...]
    for ref in came:
        back = back + ref[...].astype(F32)
    inverse = inverse_ref[...]
    back_pre, wide, pull = step_values(width, back, pre_ref[...], slope_ref[...], inverse)
    if not pushes:
        wire_ref, pull_ref = outs
        wire_ref[:, :rank] = (wide * inverse).astype(BF)
        wire_ref[:, rank:] = jnp.broadcast_to(pull, (back.shape[0], rank // 2)).astype(BF)
        pull_ref[...] = pull
        return
    outs[0][...] = back
    for k in range(pushes):
        span = pl.ds(k * rank, rank)
        pushed = inverse * dot(back_pre, mixes_ref[:, span], ((1,), (0,)))
        outs[1 + k][...] = (pushed - pull * cross_ref[:, span]).astype(BF)


def small_call(kernel, name, flags, operands, shapes):
    whole = lambda shape: pl.BlockSpec(shape, lambda i, flags: (0, 0))
    return pl.pallas_call(
        kernel,
        grid_spec=pltpu.PrefetchScalarGridSpec(
            num_scalar_prefetch=1,
            grid=(1,),
            in_specs=[whole(operand.shape) for operand in operands],
            out_specs=[whole(shape) for shape, _ in shapes],
        ),
        out_shape=[jax.ShapeDtypeStruct(shape, dtype) for shape, dtype in shapes],
        compiler_params=pltpu.CompilerParams(vmem_limit_bytes=VMEM_BYTES),
        name=name,
    )(flags, *operands)


def moved_kernel(rank, place_ref, picked_ref, down_ref, rows_ref, *outs):
    pull = picked_ref[:, rank : rank + 1].astype(F32)
    value = dot(picked_ref[:, :rank], down_ref[...], ((1,), (1,)))
    value = (value - pull * rows_ref[...].astype(F32)).astype(BF)
    half = value.shape[0] // 2
    for t in range(SECTIONS):

        @pl.when(pl.program_id(0) == t)
        def _():
            outs[2 * t][...] = value[:half]
            outs[2 * t + 1][...] = value[half:]


def moved_blocks(picked, down, rows, section):
    count, width = rows.shape
    rank = down.shape[1]
    part = width // SECTIONS
    half = jax.ShapeDtypeStruct((count // 2, part), BF)
    return pl.pallas_call(
        lambda *refs: moved_kernel(rank, *refs),
        grid_spec=pltpu.PrefetchScalarGridSpec(
            num_scalar_prefetch=1,
            grid=(SECTIONS,),
            in_specs=[
                pl.BlockSpec(picked.shape, lambda t, w: (0, 0)),
                pl.BlockSpec((part, rank), lambda t, w: ((w[0] + t) % SECTIONS, 0)),
                pl.BlockSpec((count, part), lambda t, w: (0, (w[0] + t) % SECTIONS)),
            ],
            out_specs=[pl.BlockSpec(half.shape, lambda t, w: (0, 0))] * (2 * SECTIONS),
        ),
        out_shape=[half] * (2 * SECTIONS),
        compiler_params=pltpu.CompilerParams(vmem_limit_bytes=VMEM_BYTES),
        cost_estimate=pl.CostEstimate(
            flops=2 * count * width * rank, bytes_accessed=4 * count * width, transcendentals=0
        ),
        name="moved_blocks",
    )(section.astype(jnp.int32).reshape(1), picked, down, rows)


def on_device(saved_inputs, cotangent, adapter_down, adapter_up, image_rows):
    section = lax.axis_index("pipe")
    x, y, z, core = place()
    micro, tokens, width = cotangent.shape
    rank = adapter_down.shape[2]
    count = micro * tokens
    factor = (count * lax.axis_size("dp")) ** (-0.5)
    hidden = saved_inputs.reshape(count, width)
    cot = cotangent.reshape(count, width)

    up_shard = adapter_up[0].T
    extra = [send(up_shard, ahead(d)) for d in (1, 2, 3)]
    sets = [
        jnp.concatenate([adapter_down[0], extra[0], up_shard], axis=1),
        jnp.concatenate([adapter_down[0], extra[1], extra[2]], axis=1),
    ]
    mine = jnp.where(core == 0, sets[0], sets[1])
    away = jnp.where(core == 0, sets[1], sets[0])
    by_z = send(mine, mate_z)
    by_core = send(away, mate_core)
    by_both = send(away, mate_cross)
    here = both(mine, by_core, core, 0)
    there = both(by_z, by_both, core, 0)
    blocks = [jnp.where(z == 0, here, there), jnp.where(z == 0, there, here)]
    hidden, cot, blocks = barrier((hidden, cot, blocks))
    hidden_s = send(hidden, mate_core)
    cot_s = send(cot, mate_core)
    ring = gather_ring(blocks)

    picks = (image_rows[:, :, None] == jnp.arange(tokens, dtype=jnp.int32)).astype(BF)

    def rows_of(array):
        array = array.reshape(micro, tokens, -1)
        out = lax.dot_general(picks, array, (((2,), (1,)), ((0,), (0,))), preferred_element_type=F32)
        return out.reshape(-1, out.shape[-1]).astype(BF)

    part = width // SECTIONS
    hidden_rows = rows_of(hidden)
    cot_rows = rows_of(lax.dynamic_slice_in_dim(cot, section * part, part, 1))
    wide = hidden.astype(F32)
    inverse = lax.rsqrt(jnp.mean(wide * wide, axis=1, keepdims=True) + 1e-06)
    ring, hidden_rows, cot_rows, inverse = barrier((ring, hidden_rows, cot_rows, inverse))

    down, pre, slope, act, near_m, last_m, mixed, swap = inner_products(
        hidden, hidden_s, cot, cot_s, ring, inverse, rank
    )
    swap = send(swap, mate_core)
    one_back = send(act, between((0, 1), (1, 2), (2, 3)))
    flags = core.astype(jnp.int32).reshape(1)
    square = (count, rank)
    step_shapes = [(square, BF), ((count, 1), F32), (square, BF)]
    back, cross, mixes, back_pre, pull, near = small_call(
        lambda *refs: start_kernel(width, *refs),
        "start",
        flags,
        [pre, slope, inverse, near_m, last_m, mixed, swap],
        [(square, F32), ((count, 3 * rank), F32), ((rank, 3 * rank), BF)] + step_shapes,
    )

    none = jnp.zeros(square, BF)

    def link(back, came, pushes):
        shapes = [(square, F32)] + [(square, BF)] * pushes
        if not pushes:
            shapes = [((count, rank + rank // 2), BF), ((count, 1), F32)]
        came = came + [none] * (3 - len(came))
        return small_call(
            lambda *refs: link_kernel(width, pushes, *refs),
            "link%d" % pushes,
            flags,
            [back] + came + [pre, slope, inverse, cross, mixes],
            shapes,
        )

    def bases(every):
        split = rank + rank // 2
        low = jnp.concatenate(
            [jnp.zeros((count, 2 * rank), BF), every[:, rank : rank + rank // 2]], axis=1
        )
        high = jnp.concatenate([every[:, 2 * rank :], every[:, split : 2 * rank]], axis=1)
        return jnp.where(core == 0, low, high)

    def right_side(every, base, scaled, pull):
        direct = jnp.concatenate(
            [every[:, :rank], scaled, jnp.zeros((count, rank // 2), BF)], axis=1
        )
        pulled = (-pull * base.astype(F32)).astype(BF)
        return jnp.where(core == 0, direct, 0) + pulled

    def push(back_pre, pull, low, high):
        pushed = dot(back_pre, mixes[:, low * rank : high * rank], ((1,), (0,)))
        return (inverse * pushed - pull * cross[:, low * rank : high * rank]).astype(BF)

    came = send(near, between((3, 2)))
    far = push(back_pre, pull, 1, 3)
    far_1 = send(far[:, :rank], between((3, 1)))
    two_back = send(one_back, between((1, 2), (2, 3)))
    came, far, two_back = barrier((came, far, two_back))
    back, near, far_2 = link(back, [came], 2)
    came = send(near, between((2, 1)))
    far_0 = [send(far_2, between((2, 0))), send(far[:, rank:], between((3, 0)))]
    came, far_1 = barrier((came, far_1))
    back, near = link(back, [came, far_1], 1)
    came = send(near, between((1, 0)))
    three_back = send(two_back, between((2, 3)))
    came, far_0, three_back = barrier((came, far_0, three_back))
    wire, pull = link(back, [came] + far_0, 0)
    every = jnp.concatenate([act, one_back, two_back, three_back], axis=1)
    wire, every = barrier((wire, every))
    wire_s = send(wire, mate_core)
    every_s = send(every, mate_core)
    base_m = bases(every)
    blocks = moved_blocks(rows_of(wire), down, hidden_rows, section)
    wire_s, every_s, base_m, blocks = barrier((wire_s, every_s, base_m, blocks))
    base_s = bases(every_s)
    scaled = wire[:, :rank]

    def features_of(which):
        came = [blocks[which]]
        for turn in range(1, SECTIONS):
            came.append(send(blocks[2 * turn + which], turned(turn)))
        return came

    scaled_s, pull_s = wire_s[:, :rank], wire_s[:, rank : rank + 1].astype(F32)
    joint = dot(scaled, base_m, ((0,), (0,))) + dot(scaled_s, base_s, ((0,), (0,)))
    sums = outer_products(
        hidden,
        hidden_s,
        cot,
        cot_s,
        right_side(every, base_m, scaled, pull),
        right_side(every_s, base_s, scaled_s, pull_s),
        down,
        joint.astype(BF),
    )
    sums, front = barrier((sums, features_of(0)))
    (own, other), rear = scatter_ring(*sums, features_of(1))

    feature = [[], [], []]
    for level in range(LEVELS):
        for rows, blocks in ((cot_rows[: cot_rows.shape[0] // 2], front), (cot_rows[cot_rows.shape[0] // 2 :], rear)):
            total = rows.astype(F32)
            for turn in range(SECTIONS):
                origin = (section - turn) % SECTIONS
                total = total + jnp.where(origin > level, blocks[turn].astype(F32), 0.0)
            feature[level].append(total.astype(BF).reshape(micro // 2, -1, part))
    feature_grads = jnp.stack([jnp.concatenate(pieces, axis=0) for pieces in feature])

    zero = jnp.where(core == 0, own, other)
    one = jnp.where(core == 0, other, own)
    down_grad = (zero[:, rank : 2 * rank] * factor)[None]
    near = jnp.concatenate([zero[:, 2 * rank :], one[:, 2 * rank :]], axis=1)
    up_sum = zero[:, :rank]
    for d, piece in ((1, near), (2, one[:, :rank]), (3, one[:, rank : 2 * rank])):
        up_sum = up_sum + send(piece.astype(BF), shifted(-d)).astype(F32)
    up_grad = (up_sum.T * factor)[None]
    return (down_grad, up_grad, feature_grads)


def solution(mesh):
    placed = (
        P("pipe", None, "dp", None),
        P(None, "dp", None),
        P("pipe", "dp", None),
        P("pipe", None, "dp"),
        P(None, "dp"),
    )
    return jax.shard_map(
        on_device,
        mesh=mesh,
        in_specs=placed,
        out_specs=(P("pipe", "dp", None), P("pipe", None, "dp"), P(None, None, "dp", "pipe")),
        check_vma=False,
    )
```

```python
import jax
import jax.numpy as jnp
from jax import lax
from jax.experimental import pallas as pl
from jax.experimental.pallas import tpu as pltpu
from jax.sharding import PartitionSpec as P

LEVELS = 3
SIDE = 4
SECTIONS = 4
AXES = ("dp", "pipe")
BF = jnp.bfloat16
F32 = jnp.float32
VMEM_BYTES = 48 * 1024 * 1024
barrier = lax.optimization_barrier


def route(target):
    pairs = []
    for x in range(SIDE):
        for y in range(SIDE):
            for z in range(2):
                for c in range(2):
                    for s in range(SECTIONS):
                        to = target(x, y, z, c, s)
                        if to is None:
                            continue
                        tx, ty, tz, tc, ts = to
                        source = (((x * SIDE + y) * 2 + z) * 2 + c) * SECTIONS + s
                        dest = (((tx * SIDE + ty) * 2 + tz) * 2 + tc) * SECTIONS + ts
                        pairs.append((source, dest))
    return pairs


def send(block, target):
    return lax.ppermute(block, AXES, route(target))


def mate_z(x, y, z, c, s):
    return (x, y, 1 - z, c, s)


def mate_core(x, y, z, c, s):
    return (x, y, z, 1 - c, s)


def mate_cross(x, y, z, c, s):
    return (x, y, 1 - z, 1 - c, s)


def mate_x(mask):
    def target(x, y, z, c, s):
        return (((((x + c) % SIDE) ^ mask) - c) % SIDE, y, z, c, s)

    return target


def mate_y(mask):
    def target(x, y, z, c, s):
        return (x, ((((y + c) % SIDE) ^ mask) - c) % SIDE, z, c, s)

    return target


def shifted(distance, only=None):
    def target(x, y, z, c, s):
        if only is not None and s != only:
            return None
        if not 0 <= s + distance < SECTIONS:
            return None
        return (x, y, z, c, s + distance)

    return target


def between(*pairs):
    def target(x, y, z, c, s):
        goal = dict(pairs).get(s)
        return None if goal is None else (x, y, z, c, goal)

    return target


def ahead(distance):
    def target(x, y, z, c, s):
        return (x, y, z, c, (s + distance) % SECTIONS)

    return target


def turned(distance):
    def target(x, y, z, c, s):
        if s == 0:
            return None
        return (x, y, z, c, (s + distance) % SECTIONS)

    return target


def both(mine, theirs, bit, axis):
    low = jnp.where(bit == 0, mine, theirs)
    high = jnp.where(bit == 0, theirs, mine)
    return jnp.concatenate([low, high], axis=axis)


def place():
    index = lax.axis_index("dp")
    core = index % 2
    z = (index // 2) % 2
    y = (index // 4) % SIDE
    x = index // (4 * SIDE)
    return x, y, z, core


def gather_ring(blocks):
    x, y, z, core = place()
    xs = (x + core) % SIDE
    ys = (y + core) % SIDE
    halves = []
    for color, block in enumerate(blocks):
        first, second = ((xs, mate_x), (ys, mate_y)) if color == 0 else ((ys, mate_y), (xs, mate_x))
        now = block[None, None]
        for axis, (label, mate) in ((1, first), (0, second)):
            now = both(now, send(now, mate(1)), label % 2, axis)
            far = send(now, mate(3))
            if axis == 1:
                now = both(now, far, label // 2, axis)
        halves += [now, far]
    return halves


def halve(now, label, mate, axis):
    for mask, bit, size in ((3, label // 2, 2), (1, label % 2, 1)):
        kept = lax.dynamic_slice_in_dim(now, bit * size, size, axis)
        away = lax.dynamic_slice_in_dim(now, (1 - bit) * size, size, axis)
        now = kept + send(away.astype(BF), mate(mask)).astype(F32)
    return now


def halve_rest(kept, away, label, mate, axis):
    now = kept.astype(F32) + send(away, mate(3)).astype(F32)
    low = lax.dynamic_slice_in_dim(now, label % 2, 1, axis)
    high = lax.dynamic_slice_in_dim(now, 1 - label % 2, 1, axis)
    return low + send(high.astype(BF), mate(1)).astype(F32)


def scatter_ring(kept_a, away_a, kept_b, away_b, beside):
    x, y, z, core = place()
    xs = (x + core) % SIDE
    ys = (y + core) % SIDE
    first = halve_rest(kept_a, away_a, xs, mate_x, 0)
    second = halve_rest(kept_b, away_b, ys, mate_y, 1)
    first, second, beside = barrier((first, second, beside))
    first = halve(first, ys, mate_y, 1)[0, 0]
    second = halve(second, xs, mate_x, 0)[0, 0]
    cols = first.shape[1]
    mine = jnp.where(z == 0, first, second).reshape(2, -1, cols)
    away = jnp.where(z == 0, second, first).astype(BF).reshape(2, -1, cols)
    own = lax.dynamic_index_in_dim(mine, core, 0, False)
    own = own + send(lax.dynamic_index_in_dim(away, core, 0, False), mate_z).astype(F32)
    other = send(lax.dynamic_index_in_dim(mine, 1 - core, 0, False).astype(BF), mate_core)
    cross = send(lax.dynamic_index_in_dim(away, 1 - core, 0, False), mate_cross)
    return (own, other.astype(F32) + cross.astype(F32)), beside


def dot(a, b, contract):
    return lax.dot_general(a, b, ((contract[0], contract[1]), ((), ())), preferred_element_type=F32)


def step_label(i, half):
    return 2 * jnp.where(i < 2, half, 1 - half) + i % 2


def inner_kernel(
    rank, where_ref, hm_ref, hs_ref, tm_ref, ts_ref, am_ref, at_ref, bm_ref, bt_ref, inverse_ref,
    down_ref, pre_ref, slope_ref, act_ref, nm_ref, um_ref, mixed_ref, swap_ref,
    weights, raw_ref, ns_ref, us_ref, blend_ref,
):
    core, half_y = where_ref[0], where_ref[2]
    step = pl.program_id(0)
    rows = am_ref.shape[2]
    for y in range(SIDE):
        label = lax.rem(core + y, SIDE)
        odd = lax.rem(label, 2)
        weights[pl.ds(2 * y * rows, rows), :] = jnp.where(
            label // 2 == half_y, am_ref[odd, 0], at_ref[odd, 0]
        )
        weights[pl.ds((2 * y + 1) * rows, rows), :] = jnp.where(
            step < 2, bm_ref[0, label], bt_ref[0, label]
        )
    down = weights[:, :rank]
    second = weights[:, rank : 2 * rank]
    third = weights[:, 2 * rank :]
    down_ref[...] = down
    hm, hs = hm_ref[...], hs_ref[...]

    tm = jnp.where(core == 0, tm_ref[...], hm)
    ts = jnp.where(core == 0, ts_ref[...], hs)
    results = (
        (raw_ref, dot(hm, down, ((1,), (0,)))),
        (nm_ref, dot(hm, second, ((1,), (0,)))),
        (ns_ref, dot(hs, second, ((1,), (0,)))),
        (um_ref, dot(tm, third, ((1,), (0,)))),
        (us_ref, dot(ts, third, ((1,), (0,)))),
        (blend_ref, dot(down, weights[:, rank:], ((0,), (0,)))),
    )

    @pl.when(step == 0)
    def _():
        for ref, value in results:
            ref[...] = value

    @pl.when(step > 0)
    def _():
        for ref, value in results:
            ref[...] += value

    @pl.when(step == SIDE - 1)
    def _():
        count = hm_ref.shape[0]
        pre = inverse_ref[...] * raw_ref[...]
        sigma = 1.0 / (1.0 + jnp.exp(-pre))
        pre_ref[...] = pre
        slope_ref[...] = sigma * (1.0 + pre * (1.0 - sigma))
        act_ref[...] = (pre * sigma).astype(BF)
        mixed = blend_ref[...].astype(BF)
        mixed_ref[...] = mixed
        swap_ref[:count, :rank] = ns_ref[...].astype(BF)
        swap_ref[:count, rank:] = us_ref[...].astype(BF)
        swap_ref[count:, :] = mixed


def position():
    x, y, z, core = place()
    return jnp.stack([core, (x + core) % SIDE // 2, (y + core) % SIDE // 2]).astype(jnp.int32)


def inner_products(hidden, hidden_s, cot, cot_s, ring, inverse, rank):
    count, width = hidden.shape
    part = width // SIDE
    rows, cols = ring[0].shape[2:]

    def label(i, w):
        return step_label(i, w[1])

    def block(i, w):
        return (label(i, w) + SIDE - w[0]) % SIDE

    first = pl.BlockSpec((count, part), lambda i, w: (0, block(i, w)))
    third = pl.BlockSpec((count, part), lambda i, w: (0, (1 - w[0]) * block(i, w)))
    one = pl.BlockSpec((2, 1, rows, cols), lambda i, w: (0, label(i, w), 0, 0))
    whole = lambda shape: pl.BlockSpec(shape, lambda i, w: (0, 0))
    small = (count, rank)
    shapes = [
        (small, F32),
        (small, F32),
        (small, BF),
        (small, F32),
        (small, F32),
        ((rank, 2 * rank), BF),
        ((count + rank, 2 * rank), BF),
    ]
    return pl.pallas_call(
        lambda *refs: inner_kernel(rank, *refs),
        grid_spec=pltpu.PrefetchScalarGridSpec(
            num_scalar_prefetch=1,
            grid=(SIDE,),
            in_specs=[
                first,
                first,
                third,
                third,
                one,
                one,
                pl.BlockSpec((1, SIDE, rows, cols), lambda i, w: (jnp.minimum(i, 1), 0, 0, 0)),
                pl.BlockSpec((1, SIDE, rows, cols), lambda i, w: (jnp.maximum(i - 2, 0), 0, 0, 0)),
                whole((count, 1)),
            ],
            out_specs=[pl.BlockSpec((part, rank), lambda i, w: (block(i, w), 0))]
            + [whole(shape) for shape, _ in shapes],
            scratch_shapes=[pltpu.VMEM((part, cols), BF)]
            + [pltpu.VMEM(small, F32)] * 3
            + [pltpu.VMEM((rank, 2 * rank), F32)],
        ),
        out_shape=[jax.ShapeDtypeStruct((width, rank), BF)]
        + [jax.ShapeDtypeStruct(shape, dtype) for shape, dtype in shapes],
        compiler_params=pltpu.CompilerParams(vmem_limit_bytes=VMEM_BYTES),
        cost_estimate=pl.CostEstimate(
            flops=2 * width * rank * (5 * count + 2 * rank),
            bytes_accessed=2 * width * (4 * count + cols + rank),
            transcendentals=0,
        ),
        name="inner_products",
    )(position(), hidden, hidden_s, cot, cot_s, *ring, inverse)


def outer_kernel(
    rank, where_ref, hm_ref, hs_ref, tm_ref, ts_ref, rm_ref, rs_ref, down_ref, joint_ref,
    kept_a, away_a, kept_b, away_b, total,
):
    core, half_y = where_ref[0], where_ref[2]
    rows = total.shape[1]
    chunk = 4 * rows
    cols = joint_ref.shape[1]
    for half in range(2):
        span = pl.ds(half * chunk, chunk)
        inner = dot(down_ref[span, :], joint_ref[...], ((1,), (0,)))
        hm, hs = hm_ref[:, span], hs_ref[:, span]
        tm = jnp.where(core == 0, tm_ref[:, span], hm)
        ts = jnp.where(core == 0, ts_ref[:, span], hs)
        left = dot(tm, rm_ref[:, :rank], ((0,), (0,)))
        left = left + dot(ts, rs_ref[:, :rank], ((0,), (0,)))
        right = dot(hm, rm_ref[:, rank:], ((0,), (0,)))
        right = right + dot(hs, rs_ref[:, rank:], ((0,), (0,)))
        left = (left + inner[:, :rank]).astype(BF)
        right = (right + inner[:, rank:]).astype(BF)
        for k in range(4):
            total[half * 4 + k, :, :rank] = left[k * rows : (k + 1) * rows]
            total[half * 4 + k, :, rank:] = right[k * rows : (k + 1) * rows]
    for t in range(SIDE):
        y = lax.rem(t + SIDE - core, SIDE)
        value = total[2 * y]

        @pl.when(pl.program_id(0) < 2)
        def _():
            away_a[0, t] = value

        @pl.when(pl.program_id(0) >= 2)
        def _():
            kept_a[0, t] = value

    for t in range(2):
        y = lax.rem(2 * half_y + t + SIDE - core, SIDE)
        kept_b[0, t] = total[2 * y + 1]
        y = lax.rem(2 * (1 - half_y) + t + SIDE - core, SIDE)
        away_b[0, t] = total[2 * y + 1]


def outer_products(hidden, hidden_s, cot, cot_s, right, right_sibling, down, joint):
    count, width = hidden.shape
    rank, cols = joint.shape
    part = width // SIDE
    rows = part // (2 * SIDE)

    def label(i, w):
        return step_label(i, 1 - w[1])

    def block(i, w):
        return (label(i, w) + SIDE - w[0]) % SIDE

    first = pl.BlockSpec((count, part), lambda i, w: (0, block(i, w)))
    third = pl.BlockSpec((count, part), lambda i, w: (0, (1 - w[0]) * block(i, w)))
    same = lambda shape: pl.BlockSpec(shape, lambda i, w: (0, 0))
    return pl.pallas_call(
        lambda *refs: outer_kernel(rank, *refs),
        grid_spec=pltpu.PrefetchScalarGridSpec(
            num_scalar_prefetch=1,
            grid=(SIDE,),
            in_specs=[
                first,
                first,
                third,
                third,
                same(right.shape),
                same(right.shape),
                pl.BlockSpec((part, rank), lambda i, w: (block(i, w), 0)),
                same(joint.shape),
            ],
            out_specs=[
                pl.BlockSpec((1, SIDE, rows, cols), lambda i, w: (jnp.maximum(i - 2, 0), 0, 0, 0)),
                pl.BlockSpec((1, SIDE, rows, cols), lambda i, w: (jnp.minimum(i, 1), 0, 0, 0)),
                pl.BlockSpec((1, 2, rows, cols), lambda i, w: (label(i, w), 0, 0, 0)),
                pl.BlockSpec((1, 2, rows, cols), lambda i, w: (label(i, w), 0, 0, 0)),
            ],
            scratch_shapes=[pltpu.VMEM((2 * SIDE, rows, cols), BF)],
        ),
        out_shape=[jax.ShapeDtypeStruct((2, SIDE, rows, cols), BF)] * 2
        + [jax.ShapeDtypeStruct((SIDE, 2, rows, cols), BF)] * 2,
        compiler_params=pltpu.CompilerParams(vmem_limit_bytes=VMEM_BYTES),
        cost_estimate=pl.CostEstimate(
            flops=2 * width * cols * (2 * count + rank),
            bytes_accessed=2 * width * (4 * count + cols + rank),
            transcendentals=0,
        ),
        name="outer_products",
    )(position(), hidden, hidden_s, cot, cot_s, right, right_sibling, down, joint)


def step_values(width, back, pre, slope, inverse):
    back_pre = (back * slope).astype(BF)
    wide = back_pre.astype(F32)
    pull = jnp.sum(wide * pre, axis=1, keepdims=True) / width * inverse * inverse
    return back_pre, wide, pull


def start_kernel(
    width, flag_ref, pre_ref, slope_ref, inverse_ref, near_ref, last_ref, mixed_ref, came_ref,
    back_ref, cross_ref, mixes_ref, step_ref, pull_ref, push_ref,
):
    count, rank = pre_ref.shape
    zero = flag_ref[0] == 0
    came = came_ref[:count, :].astype(F32)
    back = jnp.where(zero, last_ref[...], came[:, rank:])
    cross = jnp.where(zero, near_ref[...], came[:, :rank])
    cross_ref[:, :rank] = cross
    cross_ref[:, rank : 2 * rank] = jnp.where(zero, came[:, :rank], near_ref[...])
    cross_ref[:, 2 * rank :] = jnp.where(zero, came[:, rank:], last_ref[...])
    ours, theirs = mixed_ref[...], came_ref[count:, :]
    mix = jnp.where(zero, ours[:, :rank], theirs[:, :rank])
    mixes_ref[:, :rank] = mix
    mixes_ref[:, rank:] = jnp.where(zero, theirs, ours)
    inverse = inverse_ref[...]
    back_pre, wide, pull = step_values(width, back, pre_ref[...], slope_ref[...], inverse)
    back_ref[...] = back
    step_ref[...] = back_pre
    pull_ref[...] = pull
    push_ref[...] = (inverse * dot(back_pre, mix, ((1,), (0,))) - pull * cross).astype(BF)


def link_kernel(
    width, pushes, relay, flag_ref, back_ref, one_ref, two_ref, pre_ref, slope_ref, inverse_ref,
    cross_ref, mixes_ref, *outs,
):
    rank = pre_ref.shape[1]
    back = back_ref[...] + one_ref[:, :rank].astype(F32) + two_ref[...].astype(F32)
    inverse = inverse_ref[...]
    back_pre, wide, pull = step_values(width, back, pre_ref[...], slope_ref[...], inverse)
    if not pushes:
        wire_ref, pull_ref = outs
        wire_ref[:, :rank] = (wide * inverse).astype(BF)
        wire_ref[:, rank:] = jnp.broadcast_to(pull, (back.shape[0], rank // 2)).astype(BF)
        pull_ref[...] = pull
        return
    outs[0][...] = back
    for k in range(pushes):
        span = pl.ds(k * rank, rank)
        pushed = inverse * dot(back_pre, mixes_ref[:, span], ((1,), (0,)))
        pushed = pushed - pull * cross_ref[:, span]
        if relay:
            pushed = pushed + one_ref[:, rank:].astype(F32)
        outs[1][:, span] = pushed.astype(BF)


def small_call(kernel, name, flags, operands, shapes):
    whole = lambda shape: pl.BlockSpec(shape, lambda i, flags: (0, 0))
    return pl.pallas_call(
        kernel,
        grid_spec=pltpu.PrefetchScalarGridSpec(
            num_scalar_prefetch=1,
            grid=(1,),
            in_specs=[whole(operand.shape) for operand in operands],
            out_specs=[whole(shape) for shape, _ in shapes],
        ),
        out_shape=[jax.ShapeDtypeStruct(shape, dtype) for shape, dtype in shapes],
        compiler_params=pltpu.CompilerParams(vmem_limit_bytes=VMEM_BYTES),
        name=name,
    )(flags, *operands)


def moved_kernel(rank, place_ref, picked_ref, down_ref, rows_ref, *outs):
    pull = picked_ref[:, rank : rank + 1].astype(F32)
    value = dot(picked_ref[:, :rank], down_ref[...], ((1,), (1,)))
    value = (value - pull * rows_ref[...].astype(F32)).astype(BF)
    half = value.shape[0] // 4
    for t in range(SECTIONS):

        @pl.when(pl.program_id(0) == t)
        def _():
            outs[2 * t][...] = value[:half]
            outs[2 * t + 1][...] = value[half:]


def moved_blocks(picked, down, rows, section):
    count, width = rows.shape
    rank = down.shape[1]
    part = width // SECTIONS
    front = jax.ShapeDtypeStruct((count // 4, part), BF)
    rear = jax.ShapeDtypeStruct((count - count // 4, part), BF)
    return pl.pallas_call(
        lambda *refs: moved_kernel(rank, *refs),
        grid_spec=pltpu.PrefetchScalarGridSpec(
            num_scalar_prefetch=1,
            grid=(SECTIONS,),
            in_specs=[
                pl.BlockSpec(picked.shape, lambda t, w: (0, 0)),
                pl.BlockSpec((part, rank), lambda t, w: ((w[0] + t) % SECTIONS, 0)),
                pl.BlockSpec((count, part), lambda t, w: (0, (w[0] + t) % SECTIONS)),
            ],
            out_specs=[
                pl.BlockSpec(front.shape, lambda t, w: (0, 0)),
                pl.BlockSpec(rear.shape, lambda t, w: (0, 0)),
            ]
            * SECTIONS,
        ),
        out_shape=[front, rear] * SECTIONS,
        compiler_params=pltpu.CompilerParams(vmem_limit_bytes=VMEM_BYTES),
        cost_estimate=pl.CostEstimate(
            flops=2 * count * width * rank, bytes_accessed=4 * count * width, transcendentals=0
        ),
        name="moved_blocks",
    )(section.astype(jnp.int32).reshape(1), picked, down, rows)


def on_device(saved_inputs, cotangent, adapter_down, adapter_up, image_rows):
    section = lax.axis_index("pipe")
    x, y, z, core = place()
    micro, tokens, width = cotangent.shape
    rank = adapter_down.shape[2]
    count = micro * tokens
    factor = (count * lax.axis_size("dp")) ** (-0.5)
    hidden = saved_inputs.reshape(count, width)
    cot = cotangent.reshape(count, width)

    up_shard = adapter_up[0].T
    extra = [send(up_shard, ahead(d)) for d in (1, 2, 3)]
    sets = [
        jnp.concatenate([adapter_down[0], extra[0], up_shard], axis=1),
        jnp.concatenate([adapter_down[0], extra[1], extra[2]], axis=1),
    ]
    mine = jnp.where(core == 0, sets[0], sets[1])
    away = jnp.where(core == 0, sets[1], sets[0])
    by_z = send(mine, mate_z)
    by_core = send(away, mate_core)
    by_both = send(away, mate_cross)
    here = both(mine, by_core, core, 0)
    there = both(by_z, by_both, core, 0)
    blocks = [jnp.where(z == 0, here, there), jnp.where(z == 0, there, here)]
    hidden, cot, blocks = barrier((hidden, cot, blocks))
    hidden_s = send(hidden, mate_core)
    cot_s = send(cot, mate_core)
    ring = gather_ring(blocks)

    picks = (image_rows[:, :, None] == jnp.arange(tokens, dtype=jnp.int32)).astype(BF)

    def rows_of(array):
        array = array.reshape(micro, tokens, -1)
        out = lax.dot_general(picks, array, (((2,), (1,)), ((0,), (0,))), preferred_element_type=F32)
        return out.reshape(-1, out.shape[-1]).astype(BF)

    part = width // SECTIONS
    hidden_rows = rows_of(hidden)
    cot_rows = rows_of(lax.dynamic_slice_in_dim(cot, section * part, part, 1))
    wide = hidden.astype(F32)
    inverse = lax.rsqrt(jnp.mean(wide * wide, axis=1, keepdims=True) + 1e-06)
    ring, hidden_rows, cot_rows, inverse = barrier((ring, hidden_rows, cot_rows, inverse))

    down, pre, slope, act, near_m, last_m, mixed, swap = inner_products(
        hidden, hidden_s, cot, cot_s, ring, inverse, rank
    )
    swap = send(swap, mate_core)
    one_back = send(act, between((0, 1), (1, 2), (2, 3)))
    flags = core.astype(jnp.int32).reshape(1)
    square = (count, rank)
    step_shapes = [(square, BF), ((count, 1), F32), (square, BF)]
    back, cross, mixes, back_pre, pull, near = small_call(
        lambda *refs: start_kernel(width, *refs),
        "start",
        flags,
        [pre, slope, inverse, near_m, last_m, mixed, swap],
        [(square, F32), ((count, 3 * rank), F32), ((rank, 3 * rank), BF)] + step_shapes,
    )

    none = jnp.zeros(square, BF)

    def link(back, one, two, pushes):
        shapes = [(square, F32), ((count, pushes * rank), BF)]
        if not pushes:
            shapes = [((count, rank + rank // 2), BF), ((count, 1), F32)]
        relay = one.shape[1] > rank
        return small_call(
            lambda *refs: link_kernel(width, pushes, relay, *refs),
            "link%d" % pushes,
            flags,
            [back, one, two, pre, slope, inverse, cross, mixes],
            shapes,
        )

    def bases(every):
        split = rank + rank // 2
        low = jnp.concatenate(
            [jnp.zeros((count, 2 * rank), BF), every[:, rank : rank + rank // 2]], axis=1
        )
        high = jnp.concatenate([every[:, 2 * rank :], every[:, split : 2 * rank]], axis=1)
        return jnp.where(core == 0, low, high)

    def right_side(every, base, scaled, pull):
        direct = jnp.concatenate(
            [every[:, :rank], scaled, jnp.zeros((count, rank // 2), BF)], axis=1
        )
        pulled = (-pull * base.astype(F32)).astype(BF)
        return jnp.where(core == 0, direct, 0) + pulled

    def push(back_pre, pull, low, high):
        pushed = dot(back_pre, mixes[:, low * rank : high * rank], ((1,), (0,)))
        return (inverse * pushed - pull * cross[:, low * rank : high * rank]).astype(BF)

    came = send(near, between((3, 2)))
    far = push(back_pre, pull, 1, 3)
    far_1 = send(far[:, :rank], between((3, 1)))
    came, far, one_back = barrier((came, far, one_back))
    back, near = link(back, came, none, 2)
    came = send(near, between((2, 1)))
    far_0 = send(far[:, rank:], between((3, 0)))
    two_back = send(one_back, between((1, 2), (2, 3)))
    came, far_1, two_back = barrier((came, far_1, two_back))
    back, near = link(back, came, far_1, 1)
    came = send(near, between((1, 0)))
    three_back = send(two_back, between((2, 3)))
    came, far_0, three_back = barrier((came, far_0, three_back))
    wire, pull = link(back, came, far_0, 0)
    every = jnp.concatenate([act, one_back, two_back, three_back], axis=1)
    wire, every = barrier((wire, every))
    wire_s = send(wire, mate_core)
    every_s = send(every, mate_core)
    base_m = bases(every)
    blocks = moved_blocks(rows_of(wire), down, hidden_rows, section)
    wire_s, every_s, base_m, blocks = barrier((wire_s, every_s, base_m, blocks))
    base_s = bases(every_s)
    scaled = wire[:, :rank]

    def features_of(which):
        came = [blocks[which]]
        for turn in range(1, SECTIONS):
            came.append(send(blocks[2 * turn + which], turned(turn)))
        return came

    scaled_s, pull_s = wire_s[:, :rank], wire_s[:, rank : rank + 1].astype(F32)
    joint = dot(scaled, base_m, ((0,), (0,))) + dot(scaled_s, base_s, ((0,), (0,)))
    sums = outer_products(
        hidden,
        hidden_s,
        cot,
        cot_s,
        right_side(every, base_m, scaled, pull),
        right_side(every_s, base_s, scaled_s, pull_s),
        down,
        joint.astype(BF),
    )
    sums, front = barrier((sums, features_of(0)))
    (own, other), rear = scatter_ring(*sums, features_of(1))

    feature = [[], [], []]
    for level in range(LEVELS):
        cut = cot_rows.shape[0] // 4
        for rows, blocks in ((cot_rows[:cut], front), (cot_rows[cut:], rear)):
            total = rows.astype(F32)
            for turn in range(SECTIONS):
                origin = (section - turn) % SECTIONS
                total = total + jnp.where(origin > level, blocks[turn].astype(F32), 0.0)
            feature[level].append(total.astype(BF).reshape(-1, image_rows.shape[1], part))
    feature_grads = jnp.stack([jnp.concatenate(pieces, axis=0) for pieces in feature])

    zero = jnp.where(core == 0, own, other)
    one = jnp.where(core == 0, other, own)
    down_grad = (zero[:, rank : 2 * rank] * factor)[None]
    near = jnp.concatenate([zero[:, 2 * rank :], one[:, 2 * rank :]], axis=1)
    up_sum = zero[:, :rank]
    for d, piece in ((1, near), (2, one[:, :rank]), (3, one[:, rank : 2 * rank])):
        up_sum = up_sum + send(piece.astype(BF), shifted(-d)).astype(F32)
    up_grad = (up_sum.T * factor)[None]
    return (down_grad, up_grad, feature_grads)


def solution(mesh):
    placed = (
        P("pipe", None, "dp", None),
        P(None, "dp", None),
        P("pipe", "dp", None),
        P("pipe", None, "dp"),
        P(None, "dp"),
    )
    return jax.shard_map(
        on_device,
        mesh=mesh,
        in_specs=placed,
        out_specs=(P("pipe", "dp", None), P("pipe", None, "dp"), P(None, None, "dp", "pipe")),
        check_vma=False,
    )
```

```python
import jax
import jax.numpy as jnp
from jax import lax
from jax.experimental import pallas as pl
from jax.experimental.pallas import tpu as pltpu
from jax.sharding import PartitionSpec as P

LEVELS = 3
SIDE = 4
SECTIONS = 4
AXES = ("dp", "pipe")
BF = jnp.bfloat16
F32 = jnp.float32
VMEM_BYTES = 48 * 1024 * 1024
barrier = lax.optimization_barrier


def route(target):
    pairs = []
    for x in range(SIDE):
        for y in range(SIDE):
            for z in range(2):
                for c in range(2):
                    for s in range(SECTIONS):
                        to = target(x, y, z, c, s)
                        if to is None:
                            continue
                        tx, ty, tz, tc, ts = to
                        source = (((x * SIDE + y) * 2 + z) * 2 + c) * SECTIONS + s
                        dest = (((tx * SIDE + ty) * 2 + tz) * 2 + tc) * SECTIONS + ts
                        pairs.append((source, dest))
    return pairs


def send(block, target):
    return lax.ppermute(block, AXES, route(target))


def mate_z(x, y, z, c, s):
    return (x, y, 1 - z, c, s)


def mate_core(x, y, z, c, s):
    return (x, y, z, 1 - c, s)


def mate_cross(x, y, z, c, s):
    return (x, y, 1 - z, 1 - c, s)


def mate_x(mask):
    def target(x, y, z, c, s):
        return (((((x + c) % SIDE) ^ mask) - c) % SIDE, y, z, c, s)

    return target


def mate_y(mask):
    def target(x, y, z, c, s):
        return (x, ((((y + c) % SIDE) ^ mask) - c) % SIDE, z, c, s)

    return target


def shifted(distance, only=None):
    def target(x, y, z, c, s):
        if only is not None and s != only:
            return None
        if not 0 <= s + distance < SECTIONS:
            return None
        return (x, y, z, c, s + distance)

    return target


def between(*pairs):
    def target(x, y, z, c, s):
        goal = dict(pairs).get(s)
        return None if goal is None else (x, y, z, c, goal)

    return target


def ahead(distance):
    def target(x, y, z, c, s):
        return (x, y, z, c, (s + distance) % SECTIONS)

    return target


def turned(distance):
    def target(x, y, z, c, s):
        if s == 0:
            return None
        return (x, y, z, c, (s + distance) % SECTIONS)

    return target


def both(mine, theirs, bit, axis):
    low = jnp.where(bit == 0, mine, theirs)
    high = jnp.where(bit == 0, theirs, mine)
    return jnp.concatenate([low, high], axis=axis)


def place():
    index = lax.axis_index("dp")
    core = index % 2
    z = (index // 2) % 2
    y = (index // 4) % SIDE
    x = index // (4 * SIDE)
    return x, y, z, core


def gather_ring(blocks):
    x, y, z, core = place()
    xs = (x + core) % SIDE
    ys = (y + core) % SIDE
    halves = []
    for color, block in enumerate(blocks):
        first, second = ((xs, mate_x), (ys, mate_y)) if color == 0 else ((ys, mate_y), (xs, mate_x))
        now = block[None, None]
        for axis, (label, mate) in ((1, first), (0, second)):
            now = both(now, send(now, mate(1)), label % 2, axis)
            far = send(now, mate(3))
            if axis == 1:
                now = both(now, far, label // 2, axis)
        halves += [now, far]
    return halves


def halve(now, label, mate, axis):
    for mask, bit, size in ((3, label // 2, 2), (1, label % 2, 1)):
        kept = lax.dynamic_slice_in_dim(now, bit * size, size, axis)
        away = lax.dynamic_slice_in_dim(now, (1 - bit) * size, size, axis)
        now = kept + send(away.astype(BF), mate(mask)).astype(F32)
    return now


def halve_rest(kept, away, label, mate, axis):
    now = kept.astype(F32) + send(away, mate(3)).astype(F32)
    low = lax.dynamic_slice_in_dim(now, label % 2, 1, axis)
    high = lax.dynamic_slice_in_dim(now, 1 - label % 2, 1, axis)
    return low + send(high.astype(BF), mate(1)).astype(F32)


def scatter_ring(kept_a, away_a, kept_b, away_b, beside):
    x, y, z, core = place()
    xs = (x + core) % SIDE
    ys = (y + core) % SIDE
    first = halve_rest(kept_a, away_a, xs, mate_x, 0)
    second = halve_rest(kept_b, away_b, ys, mate_y, 1)
    first, second, beside = barrier((first, second, beside))
    first = halve(first, ys, mate_y, 1)[0, 0]
    second = halve(second, xs, mate_x, 0)[0, 0]
    cols = first.shape[1]
    mine = jnp.where(z == 0, first, second).reshape(2, -1, cols)
    away = jnp.where(z == 0, second, first).astype(BF).reshape(2, -1, cols)
    own = lax.dynamic_index_in_dim(mine, core, 0, False)
    own = own + send(lax.dynamic_index_in_dim(away, core, 0, False), mate_z).astype(F32)
    other = send(lax.dynamic_index_in_dim(mine, 1 - core, 0, False).astype(BF), mate_core)
    cross = send(lax.dynamic_index_in_dim(away, 1 - core, 0, False), mate_cross)
    return (own, other.astype(F32) + cross.astype(F32)), beside


def dot(a, b, contract):
    return lax.dot_general(a, b, ((contract[0], contract[1]), ((), ())), preferred_element_type=F32)


def step_label(i, half):
    return 2 * jnp.where(i < 2, half, 1 - half) + i % 2


def inner_kernel(
    rank, where_ref, hm_ref, hs_ref, tm_ref, ts_ref, am_ref, at_ref, bm_ref, bt_ref, inverse_ref,
    down_ref, pre_ref, slope_ref, act_ref, nm_ref, um_ref, mixed_ref, swap_ref,
    weights, raw_ref, ns_ref, us_ref, blend_ref,
):
    core, half_y = where_ref[0], where_ref[2]
    step = pl.program_id(0)
    rows = am_ref.shape[2]
    for y in range(SIDE):
        label = lax.rem(core + y, SIDE)
        odd = lax.rem(label, 2)
        weights[pl.ds(2 * y * rows, rows), :] = jnp.where(
            label // 2 == half_y, am_ref[odd, 0], at_ref[odd, 0]
        )
        weights[pl.ds((2 * y + 1) * rows, rows), :] = jnp.where(
            step < 2, bm_ref[0, label], bt_ref[0, label]
        )
    down = weights[:, :rank]
    second = weights[:, rank : 2 * rank]
    third = weights[:, 2 * rank :]
    down_ref[...] = down
    hm, hs = hm_ref[...], hs_ref[...]

    tm = jnp.where(core == 0, tm_ref[...], hm)
    ts = jnp.where(core == 0, ts_ref[...], hs)
    results = (
        (raw_ref, dot(hm, down, ((1,), (0,)))),
        (nm_ref, dot(hm, second, ((1,), (0,)))),
        (ns_ref, dot(hs, second, ((1,), (0,)))),
        (um_ref, dot(tm, third, ((1,), (0,)))),
        (us_ref, dot(ts, third, ((1,), (0,)))),
        (blend_ref, dot(down, weights[:, rank:], ((0,), (0,)))),
    )

    @pl.when(step == 0)
    def _():
        for ref, value in results:
            ref[...] = value

    @pl.when(step > 0)
    def _():
        for ref, value in results:
            ref[...] += value

    @pl.when(step == SIDE - 1)
    def _():
        count = hm_ref.shape[0]
        pre = inverse_ref[...] * raw_ref[...]
        sigma = 1.0 / (1.0 + jnp.exp(-pre))
        pre_ref[...] = pre
        slope_ref[...] = sigma * (1.0 + pre * (1.0 - sigma))
        act_ref[...] = (pre * sigma).astype(BF)
        mixed = blend_ref[...].astype(BF)
        mixed_ref[...] = mixed
        swap_ref[:count, :rank] = ns_ref[...].astype(BF)
        swap_ref[:count, rank:] = us_ref[...].astype(BF)
        swap_ref[count:, :] = mixed


def position():
    x, y, z, core = place()
    return jnp.stack([core, (x + core) % SIDE // 2, (y + core) % SIDE // 2]).astype(jnp.int32)


def inner_products(hidden, hidden_s, cot, cot_s, ring, inverse, rank):
    count, width = hidden.shape
    part = width // SIDE
    rows, cols = ring[0].shape[2:]

    def label(i, w):
        return step_label(i, w[1])

    def block(i, w):
        return (label(i, w) + SIDE - w[0]) % SIDE

    first = pl.BlockSpec((count, part), lambda i, w: (0, block(i, w)))
    third = pl.BlockSpec((count, part), lambda i, w: (0, (1 - w[0]) * block(i, w)))
    one = pl.BlockSpec((2, 1, rows, cols), lambda i, w: (0, label(i, w), 0, 0))
    whole = lambda shape: pl.BlockSpec(shape, lambda i, w: (0, 0))
    small = (count, rank)
    shapes = [
        (small, F32),
        (small, F32),
        (small, BF),
        (small, F32),
        (small, F32),
        ((rank, 2 * rank), BF),
        ((count + rank, 2 * rank), BF),
    ]
    return pl.pallas_call(
        lambda *refs: inner_kernel(rank, *refs),
        grid_spec=pltpu.PrefetchScalarGridSpec(
            num_scalar_prefetch=1,
            grid=(SIDE,),
            in_specs=[
                first,
                first,
                third,
                third,
                one,
                one,
                pl.BlockSpec((1, SIDE, rows, cols), lambda i, w: (jnp.minimum(i, 1), 0, 0, 0)),
                pl.BlockSpec((1, SIDE, rows, cols), lambda i, w: (jnp.maximum(i - 2, 0), 0, 0, 0)),
                whole((count, 1)),
            ],
            out_specs=[pl.BlockSpec((part, rank), lambda i, w: (block(i, w), 0))]
            + [whole(shape) for shape, _ in shapes],
            scratch_shapes=[pltpu.VMEM((part, cols), BF)]
            + [pltpu.VMEM(small, F32)] * 3
            + [pltpu.VMEM((rank, 2 * rank), F32)],
        ),
        out_shape=[jax.ShapeDtypeStruct((width, rank), BF)]
        + [jax.ShapeDtypeStruct(shape, dtype) for shape, dtype in shapes],
        compiler_params=pltpu.CompilerParams(vmem_limit_bytes=VMEM_BYTES),
        cost_estimate=pl.CostEstimate(
            flops=2 * width * rank * (5 * count + 2 * rank),
            bytes_accessed=2 * width * (4 * count + cols + rank),
            transcendentals=0,
        ),
        name="inner_products",
    )(position(), hidden, hidden_s, cot, cot_s, *ring, inverse)


def outer_kernel(
    rank, where_ref, hm_ref, hs_ref, tm_ref, ts_ref, rm_ref, rs_ref, down_ref, joint_ref,
    kept_a, away_a, kept_b, away_b, total,
):
    core, half_y = where_ref[0], where_ref[2]
    rows = total.shape[1]
    chunk = 4 * rows
    cols = joint_ref.shape[1]
    for half in range(2):
        span = pl.ds(half * chunk, chunk)
        inner = dot(down_ref[span, :], joint_ref[...], ((1,), (0,)))
        hm, hs = hm_ref[:, span], hs_ref[:, span]
        tm = jnp.where(core == 0, tm_ref[:, span], hm)
        ts = jnp.where(core == 0, ts_ref[:, span], hs)
        left = dot(tm, rm_ref[:, :rank], ((0,), (0,)))
        left = left + dot(ts, rs_ref[:, :rank], ((0,), (0,)))
        right = dot(hm, rm_ref[:, rank:], ((0,), (0,)))
        right = right + dot(hs, rs_ref[:, rank:], ((0,), (0,)))
        left = (left + inner[:, :rank]).astype(BF)
        right = (right + inner[:, rank:]).astype(BF)
        for k in range(4):
            total[half * 4 + k, :, :rank] = left[k * rows : (k + 1) * rows]
            total[half * 4 + k, :, rank:] = right[k * rows : (k + 1) * rows]
    for t in range(SIDE):
        y = lax.rem(t + SIDE - core, SIDE)
        value = total[2 * y]

        @pl.when(pl.program_id(0) < 2)
        def _():
            away_a[0, t] = value

        @pl.when(pl.program_id(0) >= 2)
        def _():
            kept_a[0, t] = value

    for t in range(2):
        y = lax.rem(2 * half_y + t + SIDE - core, SIDE)
        kept_b[0, t] = total[2 * y + 1]
        y = lax.rem(2 * (1 - half_y) + t + SIDE - core, SIDE)
        away_b[0, t] = total[2 * y + 1]


def outer_products(hidden, hidden_s, cot, cot_s, right, right_sibling, down, joint):
    count, width = hidden.shape
    rank, cols = joint.shape
    part = width // SIDE
    rows = part // (2 * SIDE)

    def label(i, w):
        return step_label(i, 1 - w[1])

    def block(i, w):
        return (label(i, w) + SIDE - w[0]) % SIDE

    first = pl.BlockSpec((count, part), lambda i, w: (0, block(i, w)))
    third = pl.BlockSpec((count, part), lambda i, w: (0, (1 - w[0]) * block(i, w)))
    same = lambda shape: pl.BlockSpec(shape, lambda i, w: (0, 0))
    return pl.pallas_call(
        lambda *refs: outer_kernel(rank, *refs),
        grid_spec=pltpu.PrefetchScalarGridSpec(
            num_scalar_prefetch=1,
            grid=(SIDE,),
            in_specs=[
                first,
                first,
                third,
                third,
                same(right.shape),
                same(right.shape),
                pl.BlockSpec((part, rank), lambda i, w: (block(i, w), 0)),
                same(joint.shape),
            ],
            out_specs=[
                pl.BlockSpec((1, SIDE, rows, cols), lambda i, w: (jnp.maximum(i - 2, 0), 0, 0, 0)),
                pl.BlockSpec((1, SIDE, rows, cols), lambda i, w: (jnp.minimum(i, 1), 0, 0, 0)),
                pl.BlockSpec((1, 2, rows, cols), lambda i, w: (label(i, w), 0, 0, 0)),
                pl.BlockSpec((1, 2, rows, cols), lambda i, w: (label(i, w), 0, 0, 0)),
            ],
            scratch_shapes=[pltpu.VMEM((2 * SIDE, rows, cols), BF)],
        ),
        out_shape=[jax.ShapeDtypeStruct((2, SIDE, rows, cols), BF)] * 2
        + [jax.ShapeDtypeStruct((SIDE, 2, rows, cols), BF)] * 2,
        compiler_params=pltpu.CompilerParams(vmem_limit_bytes=VMEM_BYTES),
        cost_estimate=pl.CostEstimate(
            flops=2 * width * cols * (2 * count + rank),
            bytes_accessed=2 * width * (4 * count + cols + rank),
            transcendentals=0,
        ),
        name="outer_products",
    )(position(), hidden, hidden_s, cot, cot_s, right, right_sibling, down, joint)


def step_values(width, back, pre, slope, inverse):
    back_pre = (back * slope).astype(BF)
    wide = back_pre.astype(F32)
    pull = jnp.sum(wide * pre, axis=1, keepdims=True) / width * inverse * inverse
    return back_pre, wide, pull


def start_kernel(
    width, flag_ref, pre_ref, slope_ref, inverse_ref, near_ref, last_ref, mixed_ref, came_ref,
    back_ref, cross_ref, mixes_ref, step_ref, pull_ref, push_ref,
):
    count, rank = pre_ref.shape
    zero = flag_ref[0] == 0
    came = came_ref[:count, :].astype(F32)
    back = jnp.where(zero, last_ref[...], came[:, rank:])
    cross = jnp.where(zero, near_ref[...], came[:, :rank])
    cross_ref[:, :rank] = cross
    cross_ref[:, rank : 2 * rank] = jnp.where(zero, came[:, :rank], near_ref[...])
    cross_ref[:, 2 * rank :] = jnp.where(zero, came[:, rank:], last_ref[...])
    ours, theirs = mixed_ref[...], came_ref[count:, :]
    mix = jnp.where(zero, ours[:, :rank], theirs[:, :rank])
    mixes_ref[:, :rank] = mix
    mixes_ref[:, rank:] = jnp.where(zero, theirs, ours)
    inverse = inverse_ref[...]
    back_pre, wide, pull = step_values(width, back, pre_ref[...], slope_ref[...], inverse)
    back_ref[...] = back
    step_ref[...] = back_pre
    pull_ref[...] = pull
    push_ref[...] = (inverse * dot(back_pre, mix, ((1,), (0,))) - pull * cross).astype(BF)


def link_kernel(
    width, pushes, relay, flag_ref, back_ref, one_ref, two_ref, pre_ref, slope_ref, inverse_ref,
    cross_ref, mixes_ref, *outs,
):
    rank = pre_ref.shape[1]
    back = back_ref[...] + one_ref[:, :rank].astype(F32) + two_ref[...].astype(F32)
    inverse = inverse_ref[...]
    back_pre, wide, pull = step_values(width, back, pre_ref[...], slope_ref[...], inverse)
    if not pushes:
        wire_ref, pull_ref = outs
        wire_ref[:, :rank] = (wide * inverse).astype(BF)
        wire_ref[:, rank:] = jnp.broadcast_to(pull, (back.shape[0], rank // 2)).astype(BF)
        pull_ref[...] = pull
        return
    outs[0][...] = back
    for k in range(pushes):
        span = pl.ds(k * rank, rank)
        pushed = inverse * dot(back_pre, mixes_ref[:, span], ((1,), (0,)))
        pushed = pushed - pull * cross_ref[:, span]
        if relay:
            pushed = pushed + one_ref[:, rank:].astype(F32)
        outs[1][:, span] = pushed.astype(BF)


def small_call(kernel, name, flags, operands, shapes):
    whole = lambda shape: pl.BlockSpec(shape, lambda i, flags: (0, 0))
    return pl.pallas_call(
        kernel,
        grid_spec=pltpu.PrefetchScalarGridSpec(
            num_scalar_prefetch=1,
            grid=(1,),
            in_specs=[whole(operand.shape) for operand in operands],
            out_specs=[whole(shape) for shape, _ in shapes],
        ),
        out_shape=[jax.ShapeDtypeStruct(shape, dtype) for shape, dtype in shapes],
        compiler_params=pltpu.CompilerParams(vmem_limit_bytes=VMEM_BYTES),
        name=name,
    )(flags, *operands)


def moved_kernel(rank, place_ref, picked_ref, down_ref, rows_ref, *outs):
    pull = picked_ref[:, rank : rank + 1].astype(F32)
    value = dot(picked_ref[:, :rank], down_ref[...], ((1,), (1,)))
    value = (value - pull * rows_ref[...].astype(F32)).astype(BF)
    half = outs[0].shape[0]
    for t in range(SECTIONS):

        @pl.when(pl.program_id(0) == t)
        def _():
            outs[2 * t][...] = value[:half]
            outs[2 * t + 1][...] = value[half:]


def front_rows(count):
    return count * 7 // 16


def moved_blocks(picked, down, rows, section):
    count, width = rows.shape
    rank = down.shape[1]
    part = width // SECTIONS
    cut = front_rows(count)
    front = jax.ShapeDtypeStruct((cut, part), BF)
    rear = jax.ShapeDtypeStruct((count - cut, part), BF)
    return pl.pallas_call(
        lambda *refs: moved_kernel(rank, *refs),
        grid_spec=pltpu.PrefetchScalarGridSpec(
            num_scalar_prefetch=1,
            grid=(SECTIONS,),
            in_specs=[
                pl.BlockSpec(picked.shape, lambda t, w: (0, 0)),
                pl.BlockSpec((part, rank), lambda t, w: ((w[0] + t) % SECTIONS, 0)),
                pl.BlockSpec((count, part), lambda t, w: (0, (w[0] + t) % SECTIONS)),
            ],
            out_specs=[
                pl.BlockSpec(front.shape, lambda t, w: (0, 0)),
                pl.BlockSpec(rear.shape, lambda t, w: (0, 0)),
            ]
            * SECTIONS,
        ),
        out_shape=[front, rear] * SECTIONS,
        compiler_params=pltpu.CompilerParams(vmem_limit_bytes=VMEM_BYTES),
        cost_estimate=pl.CostEstimate(
            flops=2 * count * width * rank, bytes_accessed=4 * count * width, transcendentals=0
        ),
        name="moved_blocks",
    )(section.astype(jnp.int32).reshape(1), picked, down, rows)


def on_device(saved_inputs, cotangent, adapter_down, adapter_up, image_rows):
    section = lax.axis_index("pipe")
    x, y, z, core = place()
    micro, tokens, width = cotangent.shape
    rank = adapter_down.shape[2]
    count = micro * tokens
    factor = (count * lax.axis_size("dp")) ** (-0.5)
    hidden = saved_inputs.reshape(count, width)
    cot = cotangent.reshape(count, width)

    up_shard = adapter_up[0].T
    extra = [send(up_shard, ahead(d)) for d in (1, 2, 3)]
    sets = [
        jnp.concatenate([adapter_down[0], extra[0], up_shard], axis=1),
        jnp.concatenate([adapter_down[0], extra[1], extra[2]], axis=1),
    ]
    mine = jnp.where(core == 0, sets[0], sets[1])
    away = jnp.where(core == 0, sets[1], sets[0])
    by_z = send(mine, mate_z)
    by_core = send(away, mate_core)
    by_both = send(away, mate_cross)
    here = both(mine, by_core, core, 0)
    there = both(by_z, by_both, core, 0)
    blocks = [jnp.where(z == 0, here, there), jnp.where(z == 0, there, here)]
    hidden, cot, blocks = barrier((hidden, cot, blocks))
    hidden_s = send(hidden, mate_core)
    cot_s = send(cot, mate_core)
    ring = gather_ring(blocks)

    picks = (image_rows[:, :, None] == jnp.arange(tokens, dtype=jnp.int32)).astype(BF)

    def rows_of(array):
        array = array.reshape(micro, tokens, -1)
        out = lax.dot_general(picks, array, (((2,), (1,)), ((0,), (0,))), preferred_element_type=F32)
        return out.reshape(-1, out.shape[-1]).astype(BF)

    part = width // SECTIONS
    hidden_rows = rows_of(hidden)
    cot_rows = rows_of(lax.dynamic_slice_in_dim(cot, section * part, part, 1))
    wide = hidden.astype(F32)
    inverse = lax.rsqrt(jnp.mean(wide * wide, axis=1, keepdims=True) + 1e-06)
    ring, hidden_rows, cot_rows, inverse = barrier((ring, hidden_rows, cot_rows, inverse))

    down, pre, slope, act, near_m, last_m, mixed, swap = inner_products(
        hidden, hidden_s, cot, cot_s, ring, inverse, rank
    )
    swap = send(swap, mate_core)
    one_back = send(act, between((0, 1), (1, 2), (2, 3)))
    flags = core.astype(jnp.int32).reshape(1)
    square = (count, rank)
    step_shapes = [(square, BF), ((count, 1), F32), (square, BF)]
    back, cross, mixes, back_pre, pull, near = small_call(
        lambda *refs: start_kernel(width, *refs),
        "start",
        flags,
        [pre, slope, inverse, near_m, last_m, mixed, swap],
        [(square, F32), ((count, 3 * rank), F32), ((rank, 3 * rank), BF)] + step_shapes,
    )

    none = jnp.zeros(square, BF)

    def link(back, one, two, pushes):
        shapes = [(square, F32), ((count, pushes * rank), BF)]
        if not pushes:
            shapes = [((count, rank + rank // 2), BF), ((count, 1), F32)]
        relay = one.shape[1] > rank
        return small_call(
            lambda *refs: link_kernel(width, pushes, relay, *refs),
            "link%d" % pushes,
            flags,
            [back, one, two, pre, slope, inverse, cross, mixes],
            shapes,
        )

    def bases(every):
        split = rank + rank // 2
        low = jnp.concatenate(
            [jnp.zeros((count, 2 * rank), BF), every[:, rank : rank + rank // 2]], axis=1
        )
        high = jnp.concatenate([every[:, 2 * rank :], every[:, split : 2 * rank]], axis=1)
        return jnp.where(core == 0, low, high)

    def right_side(every, base, scaled, pull):
        direct = jnp.concatenate(
            [every[:, :rank], scaled, jnp.zeros((count, rank // 2), BF)], axis=1
        )
        pulled = (-pull * base.astype(F32)).astype(BF)
        return jnp.where(core == 0, direct, 0) + pulled

    def push(back_pre, pull, low, high):
        pushed = dot(back_pre, mixes[:, low * rank : high * rank], ((1,), (0,)))
        return (inverse * pushed - pull * cross[:, low * rank : high * rank]).astype(BF)

    came = send(near, between((3, 2)))
    far = push(back_pre, pull, 1, 3)
    far_1 = send(far[:, :rank], between((3, 1)))
    came, far, one_back = barrier((came, far, one_back))
    back, near = link(back, came, none, 2)
    came = send(near, between((2, 1)))
    far_0 = send(far[:, rank:], between((3, 0)))
    two_back = send(one_back, between((1, 2), (2, 3)))
    came, far_1, two_back = barrier((came, far_1, two_back))
    back, near = link(back, came, far_1, 1)
    came = send(near, between((1, 0)))
    three_back = send(two_back, between((2, 3)))
    came, far_0, three_back = barrier((came, far_0, three_back))
    wire, pull = link(back, came, far_0, 0)
    every = jnp.concatenate([act, one_back, two_back, three_back], axis=1)
    wire, every = barrier((wire, every))
    wire_s = send(wire, mate_core)
    every_s = send(every, mate_core)
    base_m = bases(every)
    blocks = moved_blocks(rows_of(wire), down, hidden_rows, section)
    wire_s, every_s, base_m, blocks = barrier((wire_s, every_s, base_m, blocks))
    base_s = bases(every_s)
    scaled = wire[:, :rank]

    def features_of(which):
        came = [blocks[which]]
        for turn in range(1, SECTIONS):
            came.append(send(blocks[2 * turn + which], turned(turn)))
        return came

    scaled_s, pull_s = wire_s[:, :rank], wire_s[:, rank : rank + 1].astype(F32)
    joint = dot(scaled, base_m, ((0,), (0,))) + dot(scaled_s, base_s, ((0,), (0,)))
    sums = outer_products(
        hidden,
        hidden_s,
        cot,
        cot_s,
        right_side(every, base_m, scaled, pull),
        right_side(every_s, base_s, scaled_s, pull_s),
        down,
        joint.astype(BF),
    )
    sums, front = barrier((sums, features_of(0)))
    (own, other), rear = scatter_ring(*sums, features_of(1))

    feature = [[], [], []]
    for level in range(LEVELS):
        cut = front_rows(cot_rows.shape[0])
        for rows, blocks in ((cot_rows[:cut], front), (cot_rows[cut:], rear)):
            total = rows.astype(F32)
            for turn in range(SECTIONS):
                origin = (section - turn) % SECTIONS
                total = total + jnp.where(origin > level, blocks[turn].astype(F32), 0.0)
            feature[level].append(total.astype(BF))
    feature_grads = jnp.stack([jnp.concatenate(pieces, axis=0) for pieces in feature])
    feature_grads = feature_grads.reshape(LEVELS, micro, -1, part)

    zero = jnp.where(core == 0, own, other)
    one = jnp.where(core == 0, other, own)
    down_grad = (zero[:, rank : 2 * rank] * factor)[None]
    near = jnp.concatenate([zero[:, 2 * rank :], one[:, 2 * rank :]], axis=1)
    up_sum = zero[:, :rank]
    for d, piece in ((1, near), (2, one[:, :rank]), (3, one[:, rank : 2 * rank])):
        up_sum = up_sum + send(piece.astype(BF), shifted(-d)).astype(F32)
    up_grad = (up_sum.T * factor)[None]
    return (down_grad, up_grad, feature_grads)


def solution(mesh):
    placed = (
        P("pipe", None, "dp", None),
        P(None, "dp", None),
        P("pipe", "dp", None),
        P("pipe", None, "dp"),
        P(None, "dp"),
    )
    return jax.shard_map(
        on_device,
        mesh=mesh,
        in_specs=placed,
        out_specs=(P("pipe", "dp", None), P("pipe", None, "dp"), P(None, None, "dp", "pipe")),
        check_vma=False,
    )
```
